32 devices in a mesh: dp: 4 (over y, x), ctx: 4 (over z), mp: 2 (over core).
Axes of the slice: x: 2, y: 2, z: 4, core: 2. Of those that a mesh axis runs over, the one named last changes fastest.
Arguments:
- tokens: bfloat16 [2, 4, 2048, 1024], P(None, 'dp', 'ctx'), may hold values from -6 to 6
- cotangent: bfloat16 [2, 4, 2048, 1024], P(None, 'dp', 'ctx'), may hold values from -6 to 6
- routes: int32 [2, 4, 2048, 8], P(None, 'dp', 'ctx'), may hold values from 0 to 15, all different within a row; in each aligned block of 512 rows (0 to 511, 512 to 1023, ..., all dimensions but the last counted through in order) at most 320 rows name the same one
- norm_gain: bfloat16 [1024], P(('dp', 'ctx')), may hold values from 0.5 to 1.5
- w_query: bfloat16 [1024, 1024], P(('dp', 'ctx'), 'mp'), may hold values from -0.1875 to 0.1875
- w_key: bfloat16 [1024, 512], P(('dp', 'ctx'), 'mp'), may hold values from -0.1875 to 0.1875
- w_value: bfloat16 [1024, 512], P(('dp', 'ctx'), 'mp'), may hold values from -0.1875 to 0.1875
- w_output: bfloat16 [1024, 1024], P(('dp', 'ctx'), 'mp'), may hold values from -1.5 to 1.5
- ffn_gain: bfloat16 [1024], P(('dp', 'ctx')), may hold values from 0.5 to 1.5
- w_router: bfloat16 [1024, 16], P(('dp', 'ctx')), may hold values from -0.09375 to 0.09375
- w_gate: bfloat16 [16, 1024, 512], P(None, ('dp', 'ctx'), 'mp'), may hold values from -0.1875 to 0.1875
- w_up: bfloat16 [16, 1024, 512], P(None, ('dp', 'ctx'), 'mp'), may hold values from -0.1875 to 0.1875
- w_down: bfloat16 [16, 1024, 512], P(None, ('dp', 'ctx'), 'mp'), may hold values from -1 to 1
Outputs:
- output: bfloat16 [2, 4, 2048, 1024], P(None, 'dp', 'ctx')
- input_grad: bfloat16 [2, 4, 2048, 1024], P(None, 'dp', 'ctx')
- grad_norm_gain: float32 [1024], P(('dp', 'ctx'))
- grad_w_query: float32 [1024, 1024], P(('dp', 'ctx'), 'mp')
- grad_w_key: float32 [1024, 512], P(('dp', 'ctx'), 'mp')
- grad_w_value: float32 [1024, 512], P(('dp', 'ctx'), 'mp')
- grad_w_output: float32 [1024, 1024], P(('dp', 'ctx'), 'mp')
- grad_ffn_gain: float32 [1024], P(('dp', 'ctx'))
- grad_w_router: float32 [1024, 16], P(('dp', 'ctx'))
- grad_w_gate: float32 [16, 1024, 512], P(None, ('dp', 'ctx'), 'mp')
- grad_w_up: float32 [16, 1024, 512], P(None, ('dp', 'ctx'), 'mp')
- grad_w_down: float32 [16, 1024, 512], P(None, ('dp', 'ctx'), 'mp')
The draws below stay inside these ranges and needn't reach their ends.
Inputs may be any that keep to these rules, and one draw needn't show every extreme that they name: `routes`: each row names 8 different experts. Within each aligned block of 512 positions of one sequence, no expert is named by more than 320 rows, and in some block an expert is named by exactly 320 rows.
All inputs are finite; a program needn't handle non-finite values.
Results may differ from the reference program's by a relative error of at most 0.023.
Values may be sent and summed in bfloat16 or wider, within the bound.
No kernel may reach another device: no remote copies, remote signals or barrier semaphores. Data moves between devices by JAX's collectives and lax.ppermute only.
A program may use at most 320 MiB of HBM per device.

```python
import math
import jax
import jax.numpy as jnp
import numpy as np
from jax import lax

D = 1024
HEADS = 16
KVH = 8
HD = 64
FF = 512
EXPERTS = 16
TOP = 8
MICRO = 2
LMIN = 2048
LOCAL_LEN = 512
SEQS = 4
CAP = 320


def with_spikes(entries, rng, source, target, blocks, factor):
    owner, partner = [(jnp.arange(entries.shape[dim]) // (entries.shape[dim] // blocks)).reshape([-1 if axis == dim else 1 for axis in range(entries.ndim)]) for dim in (source, target)]
    chosen = jax.random.permutation(rng, blocks)[partner]
    strong = (owner == chosen) | (owner == (partner + blocks // 2) % blocks)
    return jnp.where(strong, factor * entries, entries)


def level_of(stream_key, shape, split, least, largest):
    factor_of = 1.0
    for axis_at, blocks in split:
        heights = jax.random.uniform(jax.random.fold_in(jax.random.fold_in(stream_key, 6), axis_at), (blocks,), jnp.float32, least / len(split), largest / len(split))
        factor_of = factor_of * jnp.repeat(jnp.exp(heights), shape[axis_at] // blocks).reshape((-1,) + (1,) * (len(shape) - 1 - axis_at))
    return factor_of


def shared_out(rng, own, number, rows, count, top, most, lean):
    ranking = jax.random.permutation(rng, count)
    crowded, ordinary = portions_of(count, rows * top, most, lean, True), portions_of(count, rows * top, most, lean, False)
    places = jnp.arange(count)

    def named(sizes, turn):
        used = int((sizes > 0).sum())
        fixed = max(1, used // 4)
        moved = fixed + (places - fixed + turn * (used - fixed)) % max(1, count - fixed)
        return jnp.zeros((count,), jnp.int32).at[ranking[jnp.where(places < fixed, places, moved)]].set(jnp.asarray(sizes, jnp.int32))

    sizes = jnp.where(number % 4 == 0, named(crowded, number // 4), named(ordinary, number - number // 4 - 1))
    mixed = jax.random.permutation(jax.random.fold_in(own, 3), count)
    giver, sink = mixed[0:count // 2 * 2:2], mixed[1:count // 2 * 2:2]
    slack = jnp.minimum(sizes[giver] - 1, most - sizes[sink]) // 2
    slack = jnp.where((giver == ranking[0]) | (sink == ranking[0]) | (sizes[sink] == 0), 0, jnp.maximum(slack, 0))
    moved = jax.random.randint(jax.random.fold_in(own, 4), (count // 2,), 0, 1 << 20) % (slack + 1)
    sizes = sizes.at[giver].add(-moved).at[sink].add(moved)
    members = jnp.searchsorted(jnp.cumsum(sizes), jnp.arange(rows * top), side="right").astype(jnp.int32)
    table = members.reshape(top, rows).T
    table = table[jax.random.permutation(jax.random.fold_in(own, 1), rows)]
    turn = jax.random.randint(jax.random.fold_in(own, 2), (rows, 1), 0, top)
    return jnp.take_along_axis(table, (jnp.arange(top)[None, :] + turn) % top, axis=1)


def portions_of(count, total, reach, lean, full):
    loads = [(1 << 20) // math.isqrt(grade ** lean) + 1 for grade in range(1, count + 1)]
    largest = reach if full else min(reach, max(-(-total // count), total * loads[0] // sum(loads)))
    least = 1 if total - largest >= count - 1 else 0
    given, surplus = [largest] + [least] * (count - 1), total - largest - least * (count - 1)
    while surplus > 0:
        movable = [i for i in range(1, count) if given[i] < largest] or [i for i in range(1, count) if given[i] < reach]
        whole, budget = sum([loads[i] for i in movable]), surplus
        for i in movable:
            addition = min(reach - given[i], max(1, budget * loads[i] // whole), surplus)
            given[i] = given[i] + addition
            surplus = surplus - addition
    return np.array(given)


def scatter_about(rng, extent, deviation, limit, cuts=(), kind=jnp.bfloat16):
    array = jax.random.normal(rng, extent, jnp.float32) * deviation
    if len(cuts) > 0:
        array = level_of(rng, extent, cuts, -0.22, 0.18) * array
    return jnp.clip(array, min=-limit, max=limit).astype(kind)


def noise_with(stream_key, extent, deviation, bound, split, heavy, held_as=jnp.bfloat16):
    drawn = deviation * jax.random.normal(stream_key, extent, jnp.float32)
    if split:
        drawn = drawn * level_of(stream_key, extent, split, -0.22, 0.18)
    return jnp.clip(with_spikes(drawn, jax.random.fold_in(stream_key, 3), *heavy), -bound, bound).astype(held_as)


def setup_inputs(seed: int = 0) -> dict:
    seeds = jax.random.split(jax.random.key(seed), 14)
    tokens = scatter_about(seeds[0], (MICRO, SEQS, LMIN, D), 1.0, 6.0, ((1, 4), (2, 4)))
    cotangent = noise_with(seeds[1], (MICRO, SEQS, LMIN, D), 1.0, 6.0, ((1, 4), (2, 4)), (2, 3, 4, 2.0))
    routes_keys = jax.random.split(jax.random.fold_in(seeds[2], 1), MICRO * SEQS * LMIN // LOCAL_LEN)
    routes_turns = jax.random.permutation(jax.random.fold_in(seeds[2], 3), MICRO * SEQS * LMIN // LOCAL_LEN)
    routes = jax.vmap(lambda own, number: shared_out(jax.random.fold_in(seeds[2], 2), own, number, LOCAL_LEN, EXPERTS, TOP, CAP, 1))(routes_keys, routes_turns).reshape((MICRO, SEQS, LMIN, TOP))
    norm_gain = jnp.clip(1.0 + 0.1 * jax.random.normal(seeds[3], (D,), jnp.float32), 0.5, 1.5).astype(jnp.bfloat16)
    w_query = scatter_about(seeds[4], (D, HEADS * HD), D ** -0.5, 0.1875, ((0, 16), (1, 2)))
    w_key = scatter_about(seeds[5], (D, KVH * HD), D ** -0.5, 0.1875, ((0, 16), (1, 2)))
    w_value = scatter_about(seeds[6], (D, KVH * HD), D ** -0.5, 0.1875, ((0, 16), (1, 2)))
    w_output = scatter_about(seeds[7], (D, HEADS * HD), (HEADS * HD // 64) ** -0.5, 1.5, ((0, 16), (1, 2)))
    ffn_gain = jnp.clip(1.0 + 0.1 * jax.random.normal(seeds[8], (D,), jnp.float32), 0.5, 1.5).astype(jnp.bfloat16)
    w_router = scatter_about(seeds[9], (D, EXPERTS), (4 * D) ** -0.5, 0.09375, ((0, 16),))
    w_gate = scatter_about(seeds[10], (EXPERTS, D, FF), D ** -0.5, 0.1875, ((1, 16), (2, 2)))
    w_up = scatter_about(seeds[11], (EXPERTS, D, FF), D ** -0.5, 0.1875, ((1, 16), (2, 2)))
    w_down = scatter_about(seeds[12], (EXPERTS, D, FF), (FF // 16) ** -0.5, 1.0, ((1, 16), (2, 2)))
    return dict(tokens=tokens, cotangent=cotangent, routes=routes, norm_gain=norm_gain, w_query=w_query, w_key=w_key, w_value=w_value, w_output=w_output, ffn_gain=ffn_gain, w_router=w_router, w_gate=w_gate, w_up=w_up, w_down=w_down)


EPS = 1e-06
THETA = 10000.0
NEG = -1e+30
HIGH = lax.Precision.HIGHEST

@jax.custom_vjp
def low(v):
    return lax.optimization_barrier(v.astype(jnp.bfloat16)).astype(jnp.float32)

@jax.custom_vjp
def low_back(v):
    return v

def low_keep(v):
    return (low(v), None)

def low_pass(kept, grad):
    return (grad,)

def back_keep(v):
    return (v, None)

def back_low(kept, grad):
    return (low(grad),)
low.defvjp(low_keep, low_pass)
low_back.defvjp(back_keep, back_low)

def normalize(values, gain):
    return values * lax.rsqrt(lax.optimization_barrier(jnp.mean(values * values, axis=-1, keepdims=True)) + EPS) * gain

def rotation(positions, head_dim):
    freqs = THETA ** (-(jnp.arange(head_dim // 2, dtype=jnp.float32) * 2.0) / head_dim)
    angles = positions.astype(jnp.float32)[:, None] * freqs[None, :]
    return (jnp.cos(angles), jnp.sin(angles))

def rotate(values, cosine, sine):
    half_dim = values.shape[-1] // 2
    first_half = values[..., :half_dim]
    second_half = values[..., half_dim:]
    return jnp.concatenate([first_half * cosine - second_half * sine, second_half * cosine + first_half * sine], axis=-1)

def pick_rows(table, picks):
    return jax.vmap(lambda source, choose: source[choose])(table, picks)

def slot_table(ids_flat):
    route_total = ids_flat.shape[0]
    onehot = (ids_flat[:, None] == jnp.arange(EXPERTS, dtype=jnp.int32)[None, :]).astype(jnp.int32)
    route_rank = lax.optimization_barrier(jnp.sum((jnp.cumsum(onehot, axis=0, dtype=jnp.int32) - 1) * onehot, axis=1, dtype=jnp.int32))
    slot_ids = (ids_flat * CAP + route_rank).astype(jnp.int32)
    owners = jnp.full((EXPERTS * CAP,), route_total, jnp.int32).at[slot_ids].set(jnp.arange(route_total, dtype=jnp.int32))
    return (slot_ids, owners)

def attend(q_rot, k_rot, v_low):
    group_size = HEADS // KVH
    keys_all = jnp.repeat(k_rot, group_size, axis=1)
    vals_all = jnp.repeat(v_low, group_size, axis=1)
    span = min(512, LMIN)
    key_where = jnp.arange(LMIN, dtype=jnp.int32)

    def one_block(begin):
        q_block = lax.dynamic_slice_in_dim(q_rot, begin, span, 0)
        scores = low_back(jnp.einsum('qhd,khd->hqk', q_block, keys_all, precision=HIGH) * HD ** (-0.5))
        allowed = (begin + jnp.arange(span, dtype=jnp.int32))[:, None] >= key_where[None, :]
        probs = jax.nn.softmax(jnp.where(allowed[None], scores, NEG), axis=-1)
        return jnp.einsum('hqk,khd->qhd', low(probs), vals_all, precision=HIGH)
    starts = jnp.arange(LMIN // span, dtype=jnp.int32) * span
    return lax.map(jax.checkpoint(one_block), starts).reshape(LMIN, HEADS * HD)

def experts(ffn_in, ids_seq, gate_weights, w_gate, w_up, w_down):
    blocks = LMIN // LOCAL_LEN
    slot_ids, owners = jax.vmap(slot_table)(ids_seq.reshape(blocks, LOCAL_LEN * TOP))
    padded_in = jnp.concatenate([ffn_in.reshape(blocks, LOCAL_LEN, D), jnp.zeros((blocks, 1, D), jnp.float32)], axis=1)
    dispatched = pick_rows(padded_in, owners // TOP).reshape(blocks, EXPERTS, CAP, D)
    gate_hidden = low_back(jnp.einsum('becd,edf->becf', dispatched, w_gate, precision=HIGH))
    up_hidden = low_back(jnp.einsum('becd,edf->becf', dispatched, w_up, precision=HIGH))
    act_low = low(jax.nn.silu(gate_hidden) * up_hidden)
    expert_out = low_back(jnp.einsum('becf,edf->becd', act_low, w_down, precision=HIGH))
    route_out = pick_rows(expert_out.reshape(blocks, EXPERTS * CAP, D), slot_ids).reshape(LMIN, TOP, D)
    return lax.optimization_barrier(jnp.sum(gate_weights[..., None] * route_out, axis=1))

def block_forward(x_seq, ids_seq, norm_gain, w_query, w_key, w_value, w_output, ffn_gain, w_router, w_gate, w_up, w_down):
    normed = low(normalize(x_seq, norm_gain))
    cosine, sine = rotation(jnp.arange(LMIN, dtype=jnp.int32), HD)
    cosine = cosine[:, None, :]
    sine = sine[:, None, :]
    q_raw = low_back(jnp.dot(normed, w_query, precision=HIGH)).reshape(LMIN, HEADS, HD)
    k_raw = low_back(jnp.dot(normed, w_key, precision=HIGH)).reshape(LMIN, KVH, HD)
    v_low = low(low_back(jnp.dot(normed, w_value, precision=HIGH))).reshape(LMIN, KVH, HD)
    q_rot = low(rotate(q_raw, cosine, sine))
    k_rot = low(rotate(k_raw, cosine, sine))
    attn_low = low_back(low(attend(q_rot, k_rot, v_low)))
    mixed = low_back(jnp.dot(attn_low, w_output.T, precision=HIGH))
    hidden = x_seq + mixed
    ffn_in = low(normalize(hidden, ffn_gain))
    logits = jnp.dot(ffn_in, w_router, precision=HIGH)
    gate_weights = jax.nn.softmax(jnp.take_along_axis(logits, ids_seq, axis=1), axis=-1)
    return hidden + experts(ffn_in, ids_seq, gate_weights, w_gate, w_up, w_down)

def reference(tokens, cotangent, routes, norm_gain, w_query, w_key, w_value, w_output, ffn_gain, w_router, w_gate, w_up, w_down):
    params = tuple((weight.astype(jnp.float32) for weight in (norm_gain, w_query, w_key, w_value, w_output, ffn_gain, w_router, w_gate, w_up, w_down)))
    seq_total = MICRO * SEQS
    x_all = tokens.reshape(seq_total, LMIN, D).astype(jnp.float32)
    dy_all = cotangent.reshape(seq_total, LMIN, D).astype(jnp.float32)
    ids_all = routes.reshape(seq_total, LMIN, TOP)

    def one_sequence(totals, inputs_now):
        x_seq, dy_seq, ids_seq = inputs_now

        def forward(x_in, *weights):
            return block_forward(x_in, ids_seq, *weights)
        out_seq, pullback = jax.vjp(forward, x_seq, *params)
        gradients = pullback(dy_seq)
        totals = tuple((running + grad_now for running, grad_now in zip(totals, gradients[1:])))
        return (totals, (out_seq.astype(jnp.bfloat16), gradients[0].astype(jnp.bfloat16)))
    initial = tuple((jnp.zeros_like(weight) for weight in params))
    totals, (outputs, input_grad) = lax.scan(one_sequence, initial, (x_all, dy_all, ids_all))
    return (outputs.reshape(tokens.shape), input_grad.reshape(tokens.shape), totals[0], totals[1], totals[2], totals[3], totals[4], totals[5], totals[6], totals[7], totals[8], totals[9])
```

```python
import functools
import math

import jax
import jax.numpy as jnp
from jax import lax
from jax.experimental import pallas as pl
from jax.experimental.pallas import tpu as pltpu
from jax.sharding import PartitionSpec as P

HD = 64
EPS = 1e-06
THETA = 10000.0
NEG = -1e30
VMEM_LIMIT = 60 * 1024 * 1024
BF = jnp.bfloat16
F32 = jnp.float32


def dot(a, b, ca, cb, precision=None):
    return lax.dot_general(
        a, b, (((ca,), (cb,)), ((), ())), preferred_element_type=F32, precision=precision
    )


def params(*semantics):
    return pltpu.CompilerParams(dimension_semantics=semantics, vmem_limit_bytes=VMEM_LIMIT)


def turn(values, cosine, sine):
    width = values.shape[1]
    lane = lax.broadcasted_iota(jnp.int32, values.shape, 1)
    ahead = pltpu.roll(values, width - HD // 2, 1)
    behind = pltpu.roll(values, HD // 2, 1)
    swapped = jnp.where(lane % HD < HD // 2, ahead, behind)
    reps = width // cosine.shape[1]
    return values * jnp.tile(cosine, (1, reps)) + swapped * jnp.tile(sine, (1, reps))


def qkv_kernel(x_ref, gain_ref, w_ref, cos_ref, sin_ref, normed_ref, q_ref, kv_ref):
    x = x_ref[...].astype(F32)
    inv = lax.rsqrt(jnp.mean(x * x, axis=1, keepdims=True) + EPS)
    normed = (x * inv * gain_ref[...]).astype(BF)
    normed_ref[...] = normed
    qw = q_ref.shape[1]
    kw = kv_ref.shape[1] // 2
    raw = dot(normed, w_ref[...], 1, 0)
    cosine = cos_ref[...]
    sine = sin_ref[...]
    q_ref[...] = turn(raw[:, :qw], cosine, sine).astype(BF)
    kv_ref[:, :kw] = turn(raw[:, qw : qw + kw], cosine, sine).astype(BF)
    kv_ref[:, kw:] = raw[:, qw + kw :].astype(BF)


def qkv_call(x, gain, w, cosine, sine, qw, kw):
    rows, d = x.shape
    local = cosine.shape[0]
    tile = min(256, local)
    per = local // tile
    return pl.pallas_call(
        qkv_kernel,
        grid=(rows // tile,),
        in_specs=[
            pl.BlockSpec((tile, d), lambda i: (i, 0)),
            pl.BlockSpec((1, d), lambda i: (0, 0)),
            pl.BlockSpec(w.shape, lambda i: (0, 0)),
            pl.BlockSpec((tile, 128), lambda i: (i % per, 0)),
            pl.BlockSpec((tile, 128), lambda i: (i % per, 0)),
        ],
        out_specs=[
            pl.BlockSpec((tile, d), lambda i: (i, 0)),
            pl.BlockSpec((tile, qw), lambda i: (i, 0)),
            pl.BlockSpec((tile, 2 * kw), lambda i: (i, 0)),
        ],
        out_shape=[
            jax.ShapeDtypeStruct((rows, d), BF),
            jax.ShapeDtypeStruct((rows, qw), BF),
            jax.ShapeDtypeStruct((rows, 2 * kw), BF),
        ],
        compiler_params=params("arbitrary"),
        cost_estimate=pl.CostEstimate(
            flops=2 * rows * d * w.shape[1], bytes_accessed=6 * rows * d, transcendentals=rows
        ),
        name="qkv",
    )(x, gain, w, cosine, sine)


def half_mask(block, which):
    lane = lax.broadcasted_iota(jnp.int32, block.shape, 1)
    keep = (lane < HD) if which == 0 else (lane >= HD)
    return jnp.where(keep, block, jnp.zeros_like(block))


def attn_fwd_kernel(ctx_ref, q_ref, k_ref, v_ref, o_ref, lse_ref):
    length = q_ref.shape[1]
    both = jnp.concatenate([q_ref[0, :, :128], q_ref[0, :, 128:]], axis=0)
    both = (both.astype(F32) * HD**-0.5).astype(BF)
    c = ctx_ref[0]
    cols = 2 * length

    def visit(j, state, diagonal):
        start = pl.multiple_of(j * length, length)
        k = k_ref[0, pl.ds(start, length), :]
        v = v_ref[0, pl.ds(start, length), :]
        new = []
        for i in range(2):
            peak, total, acc = state[i]
            s = dot(half_mask(k, i), both, 1, 1)
            if diagonal:
                key = lax.broadcasted_iota(jnp.int32, s.shape, 0)
                query = lax.broadcasted_iota(jnp.int32, s.shape, 1) % length
                s = jnp.where(key <= query, s, NEG)
            now = jnp.maximum(peak, jnp.max(s, axis=0, keepdims=True))
            p = jnp.exp(s - now)
            factor = jnp.exp(peak - now)
            total = total * factor + jnp.sum(p, axis=0, keepdims=True)
            acc = acc * factor + dot(v, p.astype(BF), 0, 0)
            new.append((now, total, acc))
        return tuple(new)

    one = (
        jnp.full((1, cols), NEG, F32),
        jnp.zeros((1, cols), F32),
        jnp.zeros((128, cols), F32),
    )
    state = lax.fori_loop(0, c, lambda j, st: visit(j, st, False), (one, one))
    state = visit(c, state, True)
    row = lax.broadcasted_iota(jnp.int32, (128, cols), 0)
    (m0, l0, a0), (m1, l1, a1) = state
    out = jnp.where(row < HD, a0 / l0, a1 / l1).T
    o_ref[0, :, :128] = out[:length].astype(BF)
    o_ref[0, :, 128:] = out[length:].astype(BF)
    lse_ref[0, 0] = jnp.concatenate([m0 + jnp.log(l0), m1 + jnp.log(l1)], axis=0)


def attn_fwd(ctx, q, kv):
    seqs, length, qw = q.shape
    total = kv.shape[1]
    pairs = qw // 256
    kb = kv.shape[2] // 256
    return pl.pallas_call(
        attn_fwd_kernel,
        grid=(seqs, pairs),
        in_specs=[
            pl.BlockSpec(memory_space=pltpu.SMEM),
            pl.BlockSpec((1, length, 256), lambda s, p: (s, 0, p)),
            pl.BlockSpec((1, total, 128), lambda s, p: (s, 0, p)),
            pl.BlockSpec((1, total, 128), lambda s, p: (s, 0, kb + p)),
        ],
        out_specs=[
            pl.BlockSpec((1, length, 256), lambda s, p: (s, 0, p)),
            pl.BlockSpec((1, 1, 2, 2 * length), lambda s, p: (s, p, 0, 0)),
        ],
        out_shape=[
            jax.ShapeDtypeStruct((seqs, length, qw), BF),
            jax.ShapeDtypeStruct((seqs, pairs, 2, 2 * length), F32),
        ],
        compiler_params=params("arbitrary", "arbitrary"),
        cost_estimate=pl.CostEstimate(
            flops=16 * seqs * length * total * qw,
            bytes_accessed=4 * seqs * total * qw,
            transcendentals=seqs * length * total * qw // 64,
        ),
        name="attn_fwd",
    )(ctx, q, kv, kv)


def attn_bwd_kernel(
    ctx_ref, q_ref, k_ref, v_ref, do_ref, o_ref, lse_ref, cos_ref, sin_ref, dq_ref, dk_ref, dv_ref
):
    length = q_ref.shape[1]
    total = k_ref.shape[1]

    def stacked(ref):
        return jnp.concatenate([ref[0, :, :128], ref[0, :, 128:]], axis=0)

    both = (stacked(q_ref).astype(F32) * HD**-0.5).astype(BF)
    dboth = stacked(do_ref)
    prod = dboth.astype(F32) * stacked(o_ref).astype(F32)
    pick_row = lax.broadcasted_iota(jnp.int32, (8, 128), 0)
    pick_lane = lax.broadcasted_iota(jnp.int32, (8, 128), 1) // HD
    picks = (pick_row == pick_lane).astype(F32)
    delta = dot(picks, prod, 1, 1, lax.Precision.HIGHEST)
    c = ctx_ref[0]
    cols = 2 * length

    def visit(j, dq, diagonal):
        start = pl.multiple_of(j * length, length)
        k = k_ref[0, pl.ds(start, length), :]
        v = v_ref[0, pl.ds(start, length), :]
        parts = []
        for i in range(2):
            ki = half_mask(k, i)
            s = dot(ki, both, 1, 1)
            p = jnp.exp(s - lse_ref[0, 0, i : i + 1, :])
            if diagonal:
                key = lax.broadcasted_iota(jnp.int32, s.shape, 0)
                query = lax.broadcasted_iota(jnp.int32, s.shape, 1) % length
                p = jnp.where(key <= query, p, 0.0)
            dp = dot(half_mask(v, i), dboth, 1, 1)
            ds = (p * (dp - delta[i : i + 1, :])).astype(BF)
            parts.append((dot(ds, both, 1, 0), dot(p.astype(BF), dboth, 1, 0)))
            dq = dq + dot(ki, ds, 0, 0)
        low = lax.broadcasted_iota(jnp.int32, (length, 128), 1) < HD
        dk_ref[0, pl.ds(start, length), :] = jnp.where(low, parts[0][0], parts[1][0]).astype(BF)
        dv_ref[0, pl.ds(start, length), :] = jnp.where(low, parts[0][1], parts[1][1]).astype(BF)
        return dq

    dq = lax.fori_loop(0, c, lambda j, st: visit(j, st, False), jnp.zeros((128, cols), F32))
    dq = visit(c, dq, True)

    def clear(j, carry):
        start = pl.multiple_of(j * length, length)
        dk_ref[0, pl.ds(start, length), :] = jnp.zeros((length, 128), BF)
        dv_ref[0, pl.ds(start, length), :] = jnp.zeros((length, 128), BF)
        return carry

    lax.fori_loop(c + 1, total // length, clear, 0)
    out = dq.T * HD**-0.5
    cosine = cos_ref[...]
    sine = -sin_ref[...]
    dq_ref[0, :, :128] = turn(out[:length], cosine, sine).astype(BF)
    dq_ref[0, :, 128:] = turn(out[length:], cosine, sine).astype(BF)


def attn_bwd(ctx, q, kv, do, o, lse, cosine, sine):
    seqs, length, qw = q.shape
    total = kv.shape[1]
    pairs = qw // 256
    kb = kv.shape[2] // 256
    blk = pl.BlockSpec((1, length, 256), lambda s, p: (s, 0, p))
    kblk = pl.BlockSpec((1, total, 128), lambda s, p: (s, 0, p))
    vblk = pl.BlockSpec((1, total, 128), lambda s, p: (s, 0, kb + p))
    tab = pl.BlockSpec((length, 128), lambda s, p: (0, 0))
    return pl.pallas_call(
        attn_bwd_kernel,
        grid=(seqs, pairs),
        in_specs=[
            pl.BlockSpec(memory_space=pltpu.SMEM),
            blk,
            kblk,
            vblk,
            blk,
            blk,
            pl.BlockSpec((1, 1, 2, 2 * length), lambda s, p: (s, p, 0, 0)),
            tab,
            tab,
        ],
        out_specs=[blk, kblk, kblk],
        out_shape=[
            jax.ShapeDtypeStruct((seqs, length, qw), BF),
            jax.ShapeDtypeStruct((seqs, total, kv.shape[2] // 2), BF),
            jax.ShapeDtypeStruct((seqs, total, kv.shape[2] // 2), BF),
        ],
        compiler_params=params("arbitrary", "arbitrary"),
        cost_estimate=pl.CostEstimate(
            flops=40 * seqs * length * total * qw,
            bytes_accessed=8 * seqs * total * qw,
            transcendentals=seqs * length * total * qw // 64,
        ),
        name="attn_bwd",
    )(ctx, q, kv, kv, do, o, lse, cosine, sine)


def masked_softmax(logits, named):
    peak = jnp.max(jnp.where(named, logits, NEG), axis=1, keepdims=True)
    grown = jnp.where(named, jnp.exp(jnp.where(named, logits - peak, 0.0)), 0.0)
    return grown / jnp.sum(grown, axis=1, keepdims=True)


def experts_kernel(
    x_ref, dy_ref, bits_ref, router_ref, w_ref, out_ref, dx_ref, dgate_ref, dw_ref, acc_ref
):
    step = pl.program_id(0)
    count = w_ref.shape[1]
    x = x_ref[...]
    dy = dy_ref[...]
    rows = x.shape[0]
    lane = lax.broadcasted_iota(jnp.int32, (rows, 128), 1)
    named = ((bits_ref[...] >> jnp.minimum(lane, 31)) & 1) == 1
    gates = masked_softmax(dot(x, router_ref[...], 1, 0), named)
    xt = x.T
    dyt = dy.T

    @pl.when(step == 0)
    def _():
        acc_ref[...] = jnp.zeros_like(acc_ref)

    dgates = jnp.zeros((rows, 128), F32)
    out = None
    dx = None
    for e in range(count):
        gate = gates[:, e : e + 1]
        wg = w_ref[0, e]
        wu = w_ref[1, e]
        wd = w_ref[2, e]
        g = dot(x, wg, 1, 0)
        u = dot(x, wu, 1, 0)
        z = dot(dy, wd, 1, 0)
        sig = 1.0 / (1.0 + jnp.exp(-g))
        silu = g * sig
        act = silu * u
        dgates = jnp.where(
            lane == e, jnp.sum(act.astype(BF).astype(F32) * z, axis=1, keepdims=True), dgates
        )
        gact = (gate * act).astype(BF)
        da = gate * z
        du = (da * silu).astype(BF)
        dg = (da * u * (sig * (1.0 + g * (1.0 - sig)))).astype(BF)
        o_part = dot(gact, wd, 1, 1)
        d_part = dot(dg, wg, 1, 1) + dot(du, wu, 1, 1)
        out = o_part if out is None else out + o_part
        dx = d_part if dx is None else dx + d_part
        acc_ref[0, e] += dot(xt, dg, 1, 0)
        acc_ref[1, e] += dot(xt, du, 1, 0)
        acc_ref[2, e] += dot(dyt, gact, 1, 0)
    out_ref[...] = out.astype(BF)
    dx_ref[...] = dx.astype(BF)
    dgate_ref[...] = dgates.T[:8]

    @pl.when(step == pl.num_programs(0) - 1)
    def _():
        dw_ref[...] = acc_ref[...].astype(BF)


def experts_call(x, dy, bits, router, w):
    rows, d = x.shape
    tile = min(512, rows)
    row = pl.BlockSpec((tile, d), lambda i: (i, 0))
    return pl.pallas_call(
        experts_kernel,
        grid=(rows // tile,),
        in_specs=[
            row,
            row,
            pl.BlockSpec((tile, 1), lambda i: (i, 0)),
            pl.BlockSpec((d, 128), lambda i: (0, 0)),
            pl.BlockSpec(memory_space=pltpu.VMEM),
        ],
        out_specs=[
            row,
            row,
            pl.BlockSpec((8, tile), lambda i: (0, i)),
            pl.BlockSpec(memory_space=pltpu.VMEM),
        ],
        out_shape=[
            jax.ShapeDtypeStruct((rows, d), BF),
            jax.ShapeDtypeStruct((rows, d), BF),
            jax.ShapeDtypeStruct((8, rows), F32),
            jax.ShapeDtypeStruct(w.shape, BF),
        ],
        scratch_shapes=[pltpu.VMEM(w.shape, F32)],
        compiler_params=params("arbitrary"),
        cost_estimate=pl.CostEstimate(
            flops=6 * rows * w.size, bytes_accessed=8 * rows * d + 4 * w.size, transcendentals=rows * d
        ),
        name="experts",
    )(x, dy, bits, router, w)


def apart(count, step):
    return [(i, i ^ step) for i in range(count)]


def swap(value):
    return lax.ppermute(value, "mp", [(0, 1), (1, 0)])


def head_order(weight):
    rows, width = weight.shape
    return (
        weight.reshape(rows, width // (4 * HD), 2, 2, HD).swapaxes(2, 3).reshape(rows, width)
    )


def per_device(
    tokens,
    cotangent,
    routes,
    norm_gain,
    w_query,
    w_key,
    w_value,
    w_output,
    ffn_gain,
    w_router,
    w_gate,
    w_up,
    w_down,
):
    micro, seq_count, local, width = tokens.shape
    top = routes.shape[3]
    experts = w_gate.shape[0]
    hidden_units = w_gate.shape[2]
    shard = w_gate.shape[1]
    dp = lax.axis_size("dp")
    ctx_size = lax.axis_size("ctx")
    me_dp = lax.axis_index("dp")
    me_ctx = lax.axis_index("ctx")
    me_mp = lax.axis_index("mp")
    mine_count = experts // dp
    seqs = micro * seq_count
    rows = seqs * local
    half = rows // 2
    qw = w_query.shape[1]
    kw = w_key.shape[1]
    ctx_now = me_ctx.astype(jnp.int32).reshape(1)

    def gather_tokens(halves):
        mine = lax.dynamic_index_in_dim(halves, me_mp, 0, keepdims=False)
        other = lax.dynamic_index_in_dim(halves, 1 - me_mp, 0, keepdims=False)
        far = jnp.stack([lax.ppermute(mine, "dp", apart(dp, s)) for s in range(1, dp)])
        near = swap(far)
        return jnp.concatenate([mine[None], far, other[None], near], axis=0)

    def return_tokens(part):
        cut = part.reshape((2, dp, half) + part.shape[1:])
        summed = (cut[0].astype(F32) + swap(cut[1]).astype(F32)).astype(BF)
        total = summed[0].astype(F32)
        for s in range(1, dp):
            total = total + lax.ppermute(summed[s], "dp", apart(dp, s)).astype(F32)
        total = total.astype(BF)
        return in_order(total, swap(total)).reshape((rows,) + part.shape[1:]).astype(F32)

    def in_order(mine, other):
        first = me_mp == 0
        return jnp.stack([jnp.where(first, mine, other), jnp.where(first, other, mine)])

    small = jnp.concatenate([w_router, norm_gain[:, None], ffn_gain[:, None]], axis=1)
    small = jnp.pad(small, ((0, 0), (0, 128 - small.shape[1])))
    packed = jnp.concatenate([head_order(w_query), w_key, w_value, head_order(w_output), small], axis=1)
    full = lax.all_gather(packed, ("dp", "ctx"), axis=0, tiled=True)
    w_qkv = full[:, : qw + 2 * kw]
    w_out = full[:, qw + 2 * kw : 2 * qw + 2 * kw]
    small = full[:, 2 * qw + 2 * kw :]
    router = small[:, :experts]
    gain_one = small[:, experts].astype(F32)[None, :]
    gain_two = small[:, experts + 1].astype(F32)[None, :]

    w3 = jnp.stack([w_gate, w_up, w_down])
    w3 = lax.all_to_all(w3, "dp", split_axis=1, concat_axis=2, tiled=True)
    w3 = lax.all_gather(w3, "ctx", axis=0, tiled=False)
    w3 = (
        w3.reshape(ctx_size, 3, mine_count, dp, shard, hidden_units)
        .transpose(1, 2, 3, 0, 4, 5)
        .reshape(3, mine_count, width, hidden_units)
    )

    ids = routes.reshape(rows, top)
    bits = jnp.sum(jnp.left_shift(1, ids), axis=1)
    bits_all = gather_tokens(bits.reshape(2, half // math.gcd(half, 128), -1))
    bits_all = bits_all.reshape(2 * dp * half, 1)
    turned = me_dp * mine_count
    bits_all = (bits_all >> turned) | ((bits_all << (experts - turned)) & ((1 << experts) - 1))
    router_turned = jnp.pad(
        jnp.roll(router, -turned, axis=1), ((0, 0), (0, 128 - experts))
    )
    dy = cotangent.reshape(rows, width)
    dy_all = gather_tokens(dy.reshape(2, half, width)).reshape(2 * dp * half, width)

    position = me_ctx * local + jnp.arange(local, dtype=jnp.int32)
    freqs = THETA ** (-(jnp.arange(HD // 2, dtype=F32) * 2.0) / HD)
    angles = position.astype(F32)[:, None] * freqs[None, :]
    cosine = jnp.tile(jnp.cos(angles), (1, 4))
    sine = jnp.sin(angles)
    sine = jnp.concatenate([-sine, sine, -sine, sine], axis=1)
    x = tokens.reshape(rows, width)
    normed, q, kv = qkv_call(x, gain_one, w_qkv, cosine, sine, qw, kw)
    q = q.reshape(seqs, local, qw)
    kv_all = lax.all_gather(kv.reshape(seqs, local, 2 * kw), "ctx", axis=1, tiled=True)
    attn, lse = attn_fwd(ctx_now, q, kv_all)
    attn_rows = attn.reshape(rows, qw)
    mixed_part = dot(attn_rows, w_out, 1, 1).astype(BF)
    x32 = x.astype(F32)
    hidden = x32 + (mixed_part.astype(F32) + swap(mixed_part).astype(F32))
    inv_two = lax.rsqrt(jnp.mean(hidden * hidden, axis=1, keepdims=True) + EPS)
    ffn_low = (hidden * inv_two * gain_two).astype(BF)

    x_all = gather_tokens(ffn_low.reshape(2, half, width)).reshape(2 * dp * half, width)
    out_part, dx_part, dgate, dw = experts_call(x_all, dy_all, bits_all, router_turned, w3)
    output = (hidden + return_tokens(out_part)).astype(BF)

    dw = (
        dw.reshape(3, mine_count, dp, ctx_size, shard, hidden_units)
        .transpose(3, 0, 1, 2, 4, 5)
        .reshape(ctx_size, 3, mine_count, dp * shard, hidden_units)
    )
    dw = lax.psum_scatter(dw, "ctx", scatter_dimension=0, tiled=False)
    dw = lax.all_to_all(dw, "dp", split_axis=2, concat_axis=1, tiled=True).astype(F32)

    moe_dx = return_tokens(dx_part)
    cut = dgate.reshape(8, 2, dp, half)[:mine_count]
    cut = cut[:, 0] + swap(cut[:, 1])
    back = [cut[:, 0]] + [lax.ppermute(cut[:, s], "dp", apart(dp, s)) for s in range(1, dp)]
    order = []
    for k in range(dp):
        order.append(
            functools.reduce(
                jnp.add, [jnp.where((me_dp ^ s) == k, back[s], 0.0) for s in range(dp)]
            )
        )
    dgate_mine = jnp.concatenate(order, axis=0)
    dgate_rows = in_order(dgate_mine, swap(dgate_mine)).transpose(0, 2, 1).reshape(rows, experts)
    named = ((bits[:, None] >> jnp.arange(experts, dtype=jnp.int32)[None, :]) & 1) == 1
    gates = masked_softmax(dot(ffn_low, router, 1, 0), named)
    dlogit = gates * (dgate_rows - jnp.sum(gates * dgate_rows, axis=1, keepdims=True))
    grad_router = dot(ffn_low, dlogit.astype(BF), 0, 0)
    d_ffn = moe_dx + dot(dlogit.astype(BF), router, 1, 1)
    n_two = hidden * inv_two
    grad_gain_two = jnp.sum(d_ffn * n_two, axis=0)
    g_two = d_ffn * gain_two
    dh = dy.astype(F32) + inv_two * (
        g_two - n_two * jnp.mean(g_two * n_two, axis=1, keepdims=True)
    )
    dz = dh.astype(BF)

    d_attn = dot(dz, w_out, 1, 0).astype(BF)
    grad_out = dot(dz, attn_rows, 0, 0).astype(BF)
    dq, dk, dv = attn_bwd(
        ctx_now, q, kv_all, d_attn.reshape(seqs, local, qw), attn, lse, cosine, sine
    )
    dkv = lax.psum_scatter(
        jnp.concatenate([dk, dv], axis=2), "ctx", scatter_dimension=1, tiled=True
    ).reshape(rows, 2 * kw)
    dk = dkv[:, :kw].astype(F32).reshape(seqs, local, kw // HD, 2, HD // 2)
    cos_h = jnp.cos(angles)[None, :, None, :]
    sin_h = jnp.sin(angles)[None, :, None, :]
    dk = jnp.concatenate(
        [
            dk[:, :, :, 0] * cos_h + dk[:, :, :, 1] * sin_h,
            dk[:, :, :, 1] * cos_h - dk[:, :, :, 0] * sin_h,
        ],
        axis=-1,
    )
    dk = dk.astype(BF).reshape(rows, kw)
    dqkv = jnp.concatenate([dq.reshape(rows, qw), dk, dkv[:, kw:]], axis=1)
    grad_qkv = dot(normed, dqkv, 0, 0).astype(BF)
    dn_part = dot(dqkv, w_qkv, 1, 1).astype(BF)
    d_normed = dn_part.astype(F32) + swap(dn_part).astype(F32)
    inv_one = lax.rsqrt(jnp.mean(x32 * x32, axis=1, keepdims=True) + EPS)
    n_one = x32 * inv_one
    grad_gain_one = jnp.sum(d_normed * n_one, axis=0)
    g_one = d_normed * gain_one
    input_grad = (
        dh + inv_one * (g_one - n_one * jnp.mean(g_one * n_one, axis=1, keepdims=True))
    ).astype(BF)

    small_grad = jnp.concatenate(
        [grad_router, grad_gain_one[:, None], grad_gain_two[:, None]], axis=1
    ).astype(BF)
    small_grad = jnp.pad(small_grad, ((0, 0), (0, 128 - small_grad.shape[1])))
    sent = jnp.concatenate([grad_qkv, grad_out, small_grad], axis=1)
    owned = lax.psum_scatter(sent, ("dp", "ctx"), scatter_dimension=0, tiled=True).astype(F32)
    small_grad = owned[:, 2 * qw + 2 * kw :]
    shape = tokens.shape
    return (
        output.reshape(shape),
        input_grad.reshape(shape),
        small_grad[:, experts],
        head_order(owned[:, :qw]),
        owned[:, qw : qw + kw],
        owned[:, qw + kw : qw + 2 * kw],
        head_order(owned[:, qw + 2 * kw : 2 * qw + 2 * kw]),
        small_grad[:, experts + 1],
        small_grad[:, :experts],
        dw[0],
        dw[1],
        dw[2],
    )


def solution(mesh):
    rows = P(None, "dp", "ctx", None)
    vector = P(("dp", "ctx"))
    matrix = P(("dp", "ctx"), "mp")
    router = P(("dp", "ctx"), None)
    expert = P(None, ("dp", "ctx"), "mp")
    return jax.shard_map(
        per_device,
        mesh=mesh,
        in_specs=(
            rows,
            rows,
            rows,
            vector,
            matrix,
            matrix,
            matrix,
            matrix,
            vector,
            router,
            expert,
            expert,
            expert,
        ),
        out_specs=(
            rows,
            rows,
            vector,
            matrix,
            matrix,
            matrix,
            matrix,
            vector,
            router,
            expert,
            expert,
            expert,
        ),
        check_vma=False,
    )
```

```python
import functools
import math

import jax
import jax.numpy as jnp
from jax import lax
from jax.experimental import pallas as pl
from jax.experimental.pallas import tpu as pltpu
from jax.sharding import PartitionSpec as P

HD = 64
EPS = 1e-06
THETA = 10000.0
NEG = -1e30
VMEM_LIMIT = 60 * 1024 * 1024
BF = jnp.bfloat16
F32 = jnp.float32


def dot(a, b, ca, cb, precision=None):
    return lax.dot_general(
        a, b, (((ca,), (cb,)), ((), ())), preferred_element_type=F32, precision=precision
    )


def params(*semantics):
    return pltpu.CompilerParams(dimension_semantics=semantics, vmem_limit_bytes=VMEM_LIMIT)


def turn(values, cosine, sine):
    width = values.shape[1]
    lane = lax.broadcasted_iota(jnp.int32, values.shape, 1)
    ahead = pltpu.roll(values, width - HD // 2, 1)
    behind = pltpu.roll(values, HD // 2, 1)
    swapped = jnp.where(lane % HD < HD // 2, ahead, behind)
    reps = width // cosine.shape[1]
    return values * jnp.tile(cosine, (1, reps)) + swapped * jnp.tile(sine, (1, reps))


def kv_kernel(x_ref, gain_ref, w_ref, cos_ref, sin_ref, normed_ref, kv_ref):
    x = x_ref[...].astype(F32)
    inv = lax.rsqrt(jnp.mean(x * x, axis=1, keepdims=True) + EPS)
    normed = (x * inv * gain_ref[...]).astype(BF)
    normed_ref[...] = normed
    kw = kv_ref.shape[1] // 2
    raw = dot(normed, w_ref[...], 1, 0)
    kv_ref[:, :kw] = turn(raw[:, :kw], cos_ref[...], sin_ref[...]).astype(BF)
    kv_ref[:, kw:] = raw[:, kw:].astype(BF)


def q_kernel(normed_ref, w_ref, cos_ref, sin_ref, q_ref):
    raw = dot(normed_ref[...], w_ref[...], 1, 0)
    q_ref[...] = turn(raw, cos_ref[...], sin_ref[...]).astype(BF)


def row_specs(rows, local, d, lanes):
    tile = min(256, local)
    per = local // tile
    return (
        rows // tile,
        pl.BlockSpec((tile, d), lambda i: (i, 0)),
        pl.BlockSpec((d, lanes), lambda i: (0, 0)),
        pl.BlockSpec((tile, 128), lambda i: (i % per, 0)),
        pl.BlockSpec((tile, lanes), lambda i: (i, 0)),
        pl.CostEstimate(
            flops=2 * rows * d * lanes, bytes_accessed=6 * rows * d, transcendentals=rows
        ),
    )


def kv_call(x, gain, w, lanes, cosine, sine):
    rows, d = x.shape
    steps, row, weight, table, out, cost = row_specs(rows, cosine.shape[0], d, lanes)
    return pl.pallas_call(
        kv_kernel,
        grid=(steps,),
        in_specs=[row, pl.BlockSpec((1, d), lambda i: (0, 0)), weight, table, table],
        out_specs=[row, out],
        out_shape=[
            jax.ShapeDtypeStruct((rows, d), BF),
            jax.ShapeDtypeStruct((rows, lanes), BF),
        ],
        compiler_params=params("arbitrary"),
        cost_estimate=cost,
        name="kv",
    )(x, gain, w, cosine, sine)


def q_call(normed, w, lanes, cosine, sine):
    rows, d = normed.shape
    steps, row, weight, table, out, cost = row_specs(rows, cosine.shape[0], d, lanes)
    return pl.pallas_call(
        q_kernel,
        grid=(steps,),
        in_specs=[row, weight, table, table],
        out_specs=out,
        out_shape=jax.ShapeDtypeStruct((rows, lanes), BF),
        compiler_params=params("arbitrary"),
        cost_estimate=cost,
        name="q",
    )(normed, w, cosine, sine)


def half_mask(block, which):
    lane = lax.broadcasted_iota(jnp.int32, block.shape, 1)
    keep = (lane < HD) if which == 0 else (lane >= HD)
    return jnp.where(keep, block, jnp.zeros_like(block))


def stacked(ref):
    return jnp.concatenate([ref[0, :, :128], ref[0, :, 128:]], axis=0)


def causal(shape, length):
    key = lax.broadcasted_iota(jnp.int32, shape, 0)
    query = lax.broadcasted_iota(jnp.int32, shape, 1) % length
    return key <= query


def each_earlier(c, counts, visit, otherwise=None, first=1):
    for piece, count in enumerate(counts):
        if count == 1:

            @pl.when(c >= first)
            def _():
                visit(piece, 0)

            if otherwise is not None:

                @pl.when(c < first)
                def _():
                    otherwise(piece, 0)

        else:
            reach = jnp.clip(c - first + 1, 0, count)

            @pl.loop(0, reach)
            def _(entry):
                visit(piece, entry)

            if otherwise is not None:

                @pl.loop(reach, count)
                def _(entry):
                    otherwise(piece, entry)

        first += count


def attn_part_kernel(counts, start, first, last, ctx_ref, q_ref, *refs):
    refs = list(refs)
    pieces = len(counts) + first
    keys = [refs.pop(0) for _ in range(pieces)]
    vals = [refs.pop(0) for _ in range(pieces)]
    old = None if first else [refs.pop(0) for _ in range(2)]
    if last:
        o_ref, lse_ref, stats_ref, acc_ref = refs
    else:
        stats_ref, acc_ref = (ref.at[0, 0] for ref in refs)
    length = q_ref.shape[1]
    both = (stacked(q_ref).astype(F32) * HD**-0.5).astype(BF)
    c = ctx_ref[0]

    if first:
        k = keys[0][0, 0]
        v = vals[0][0, 0]
        for i in range(2):
            s = dot(half_mask(k, i), both, 1, 1)
            s = jnp.where(causal(s.shape, length), s, NEG)
            peak = jnp.max(s, axis=0, keepdims=True)
            p = jnp.exp(s - peak)
            stats_ref[i : i + 1] = peak
            stats_ref[i + 2 : i + 3] = jnp.sum(p, axis=0, keepdims=True)
            acc_ref[i] = dot(v, p.astype(BF), 0, 0)
    else:
        stats_ref[...] = old[0][0, 0]
        acc_ref[...] = old[1][0, 0]

    def visit(piece, entry):
        k = keys[piece + first][entry, 0]
        v = vals[piece + first][entry, 0]
        for i in range(2):
            s = dot(half_mask(k, i), both, 1, 1)
            peak = stats_ref[i : i + 1]
            now = jnp.maximum(peak, jnp.max(s, axis=0, keepdims=True))
            p = jnp.exp(s - now)
            factor = jnp.exp(peak - now)
            stats_ref[i : i + 1] = now
            stats_ref[i + 2 : i + 3] = stats_ref[i + 2 : i + 3] * factor + jnp.sum(
                p, axis=0, keepdims=True
            )
            acc_ref[i] = acc_ref[i] * factor + dot(v, p.astype(BF), 0, 0)

    each_earlier(c, counts, visit, None, start)
    if last:
        row = lax.broadcasted_iota(jnp.int32, acc_ref.shape[1:], 0)
        stats = stats_ref[...]
        out = jnp.where(row < HD, acc_ref[0] / stats[2:3], acc_ref[1] / stats[3:4]).T
        o_ref[0, :, :128] = out[:length].astype(BF)
        o_ref[0, :, 128:] = out[length:].astype(BF)
        lse_ref[0, 0] = stats[:2] + jnp.log(stats[2:])


def kv_specs(pieces, length, lanes, at=0):
    kb = lanes // 256
    keys = [
        pl.BlockSpec((a.shape[0], 1, length, 128), lambda s, p: (0, s + at, 0, p)) for a in pieces
    ]
    vals = [
        pl.BlockSpec((a.shape[0], 1, length, 128), lambda s, p: (0, s + at, 0, kb + p))
        for a in pieces
    ]
    return keys + vals


def attn_part(ctx, q, own, prev, start, carry, last):
    seqs, length, qw = q.shape
    pairs = qw // 256
    cols = 2 * length
    first = own is not None
    pieces = ([own] if first else []) + prev
    counts = tuple(a.shape[0] for a in prev)
    spans = first + sum(counts)
    state = [
        pl.BlockSpec((1, 1, 4, cols), lambda s, p: (s, p, 0, 0)),
        pl.BlockSpec((1, 1, 2, 128, cols), lambda s, p: (s, p, 0, 0, 0)),
    ]
    if last:
        out_specs = [
            pl.BlockSpec((1, length, 256), lambda s, p: (s, 0, p)),
            pl.BlockSpec((1, 1, 2, cols), lambda s, p: (s, p, 0, 0)),
        ]
        out_shape = [
            jax.ShapeDtypeStruct((seqs, length, qw), BF),
            jax.ShapeDtypeStruct((seqs, pairs, 2, cols), F32),
        ]
        scratch = [pltpu.VMEM((4, cols), F32), pltpu.VMEM((2, 128, cols), F32)]
    else:
        out_specs = state
        out_shape = [
            jax.ShapeDtypeStruct((seqs, pairs, 4, cols), F32),
            jax.ShapeDtypeStruct((seqs, pairs, 2, 128, cols), F32),
        ]
        scratch = []
    return pl.pallas_call(
        functools.partial(attn_part_kernel, counts, start, first, last),
        grid=(seqs, pairs),
        in_specs=[
            pl.BlockSpec(memory_space=pltpu.SMEM),
            pl.BlockSpec((1, length, 256), lambda s, p: (s, 0, p)),
        ]
        + kv_specs(pieces, length, pieces[0].shape[3])
        + ([] if first else state),
        out_specs=out_specs,
        out_shape=out_shape,
        scratch_shapes=scratch,
        compiler_params=params("arbitrary", "arbitrary"),
        cost_estimate=pl.CostEstimate(
            flops=16 * seqs * length * length * spans * qw,
            bytes_accessed=4 * seqs * length * spans * qw,
            transcendentals=seqs * length * length * spans * qw // 64,
        ),
        name="attn_fwd",
    )(ctx, q, *pieces, *pieces, *(carry or []))


def attn_bwd_kernel(counts, ctx_ref, q_ref, do_ref, o_ref, lse_ref, cos_ref, sin_ref, *refs):
    pieces = len(counts)
    keys = refs[: pieces + 1]
    vals = refs[pieces + 1 : 2 * pieces + 2]
    dq_ref = refs[2 * pieces + 2]
    outs = refs[2 * pieces + 3 : 3 * pieces + 4]
    acc_ref = refs[3 * pieces + 4]
    length = q_ref.shape[1]
    lanes = outs[0].shape[3]
    pair = pl.program_id(1)
    both = (stacked(q_ref).astype(F32) * HD**-0.5).astype(BF)
    dboth = stacked(do_ref)
    prod = dboth.astype(F32) * stacked(o_ref).astype(F32)
    pick_row = lax.broadcasted_iota(jnp.int32, (8, 128), 0)
    pick_lane = lax.broadcasted_iota(jnp.int32, (8, 128), 1) // HD
    picks = (pick_row == pick_lane).astype(F32)
    delta = dot(picks, prod, 1, 1, lax.Precision.HIGHEST)
    c = ctx_ref[0]
    k_at = pl.ds(pl.multiple_of(pair * 128, 128), 128)
    v_at = pl.ds(pl.multiple_of(lanes // 2 + pair * 128, 128), 128)

    def block(piece, entry, diagonal):
        k = keys[piece][entry, 0]
        v = vals[piece][entry, 0]
        parts = []
        dq = None
        for i in range(2):
            ki = half_mask(k, i)
            s = dot(ki, both, 1, 1)
            p = jnp.exp(s - lse_ref[0, 0, i : i + 1, :])
            if diagonal:
                p = jnp.where(causal(s.shape, length), p, 0.0)
            dp = dot(half_mask(v, i), dboth, 1, 1)
            ds = (p * (dp - delta[i : i + 1, :])).astype(BF)
            parts.append((dot(ds, both, 1, 0), dot(p.astype(BF), dboth, 1, 0)))
            part = dot(ki, ds, 0, 0)
            dq = part if dq is None else dq + part
        low = lax.broadcasted_iota(jnp.int32, (length, 128), 1) < HD
        outs[piece][entry, 0, :, k_at] = jnp.where(low, parts[0][0], parts[1][0]).astype(BF)
        outs[piece][entry, 0, :, v_at] = jnp.where(low, parts[0][1], parts[1][1]).astype(BF)
        return dq

    acc_ref[...] = block(0, 0, True)

    def visit(piece, entry):
        acc_ref[...] += block(piece + 1, entry, False)

    def clear(piece, entry):
        outs[piece + 1][entry, 0, :, k_at] = jnp.zeros((length, 128), BF)
        outs[piece + 1][entry, 0, :, v_at] = jnp.zeros((length, 128), BF)

    each_earlier(c, counts, visit, clear)
    out = acc_ref[...].T * HD**-0.5
    cosine = cos_ref[...]
    sine = -sin_ref[...]
    dq_ref[0, :, :128] = turn(out[:length], cosine, sine).astype(BF)
    dq_ref[0, :, 128:] = turn(out[length:], cosine, sine).astype(BF)


def attn_bwd(ctx, q, do, o, lse, cosine, sine, own, prev, at):
    seqs, length, qw = do.shape
    pairs = qw // 256
    pieces = [own] + prev
    counts = tuple(a.shape[0] for a in prev)
    spans = 1 + sum(counts)
    blk = pl.BlockSpec((1, length, 256), lambda s, p: (s, 0, p))
    blk_at = pl.BlockSpec((1, length, 256), lambda s, p: (s + at, 0, p))
    tab = pl.BlockSpec((length, 128), lambda s, p: (0, 0))
    return pl.pallas_call(
        functools.partial(attn_bwd_kernel, counts),
        grid=(seqs, pairs),
        in_specs=[
            pl.BlockSpec(memory_space=pltpu.SMEM),
            blk_at,
            blk,
            blk_at,
            pl.BlockSpec((1, 1, 2, 2 * length), lambda s, p: (s + at, p, 0, 0)),
            tab,
            tab,
        ]
        + kv_specs(pieces, length, own.shape[3], at),
        out_specs=[blk]
        + [
            pl.BlockSpec((a.shape[0], 1) + a.shape[2:], lambda s, p: (0, s, 0, 0)) for a in pieces
        ],
        out_shape=[jax.ShapeDtypeStruct((seqs, length, qw), BF)]
        + [jax.ShapeDtypeStruct((a.shape[0], seqs) + a.shape[2:], BF) for a in pieces],
        scratch_shapes=[pltpu.VMEM((128, 2 * length), F32)],
        compiler_params=params("arbitrary", "arbitrary"),
        cost_estimate=pl.CostEstimate(
            flops=40 * seqs * length * length * spans * qw,
            bytes_accessed=8 * seqs * length * spans * qw,
            transcendentals=seqs * length * length * spans * qw // 64,
        ),
        name="attn_bwd",
    )(ctx, q, do, o, lse, cosine, sine, *pieces, *pieces)


def masked_softmax(logits, named):
    peak = jnp.max(jnp.where(named, logits, NEG), axis=1, keepdims=True)
    grown = jnp.where(named, jnp.exp(jnp.where(named, logits - peak, 0.0)), 0.0)
    return grown / jnp.sum(grown, axis=1, keepdims=True)


def experts_kernel(steps, first, count, more, joined, place_ref, router_ref, *refs):
    refs = list(refs)
    n = 1 if joined else refs[-5].shape[1]
    xs = [refs.pop(0) for _ in range(2 * steps)]
    dys = [refs.pop(0) for _ in range(2 * steps)]
    ws = [refs.pop(0) for _ in range(2 * n - 1)]
    before = [refs.pop(0) for _ in range(4)] if more else None
    outs = [refs.pop(0) for _ in range(4)]
    dws = [refs.pop(0) for _ in range(n)]
    acc_ref, w_ref, xbuf, dybuf, sems, wsems = refs
    step = pl.program_id(0)
    base = place_ref[0]
    c = place_ref[1]
    rows, width = xbuf.shape[1:]
    units = w_ref.shape[-1] // (3 * count)
    both = 2 * count * units
    half = rows // 2

    def copies(t, slot):
        return [
            pltpu.make_async_copy(
                src[2 * t + part],
                buf.at[slot, pl.ds(part * half, half)],
                sems.at[slot, 2 * which + part],
            )
            for which, (src, buf) in enumerate(((xs, xbuf), (dys, dybuf)))
            for part in range(2)
        ]

    def fetch(at, slot):
        for t in range(steps):

            @pl.when(at == t)
            def _():
                for copy in copies(t, slot):
                    copy.start()

    def weight_copy(src, d):
        if joined:
            return pltpu.make_async_copy(src, w_ref, wsems.at[0])
        return pltpu.make_async_copy(src, w_ref.at[:, (c + d) % n], wsems.at[d])

    slot = step % 2

    @pl.when(step == 0)
    def _():
        fetch(step, slot)
        weight_copy(ws[0], 0).start()
        for d in range(1, n):

            @pl.when(c + d < n)
            def _():
                weight_copy(ws[n - 1 + d], d).start()

            @pl.when(c + d >= n)
            def _():
                weight_copy(ws[n - d], d).start()

        for d in range(n):
            weight_copy(ws[0], d).wait()

    @pl.when(step + 1 < steps)
    def _():
        fetch(step + 1, 1 - slot)

    for copy in copies(0, slot):
        copy.wait()

    x = xbuf[slot]
    dy = dybuf[slot, :, :width]
    lane = lax.broadcasted_iota(jnp.int32, (rows, 128), 1)
    named = dybuf[slot, :, width:].astype(F32) > 0.5
    gates = masked_softmax(dot(x, router_ref[...], 1, 0), named)
    gates = pltpu.roll(gates, 128 - base, 1)
    w_in = w_ref[..., :both].reshape(width, both)
    w_back = w_ref[..., both:].reshape(width, both // 2)
    gu = dot(x, w_in, 1, 0)
    g = gu[:, : both // 2]
    u = gu[:, both // 2 :]
    z = dot(dy, w_back, 1, 0)
    gate = jnp.concatenate(
        [
            jnp.broadcast_to(gates[:, first + e : first + e + 1], (rows, units))
            for e in range(count)
        ],
        axis=1,
    )
    sig = 1.0 / (1.0 + jnp.exp(-g))
    silu = g * sig
    act = silu * u
    product = act.astype(BF).astype(F32) * z
    dgates = jnp.zeros((rows, 128), F32)
    for e in range(count):
        total = jnp.sum(product[:, e * units : (e + 1) * units], axis=1, keepdims=True)
        dgates = jnp.where(lane == base + first + e, total, dgates)
    gact = (gate * act).astype(BF)
    da = gate * z
    dgu = jnp.concatenate(
        [
            (da * u * (sig * (1.0 + g * (1.0 - sig)))).astype(BF),
            (da * silu).astype(BF),
        ],
        axis=1,
    )
    out = dot(gact, w_back, 1, 1)
    dx = dot(dgu, w_in, 1, 1)
    for part in range(2):
        at = slice(part * half, (part + 1) * half)
        o, d, t = out[at], dx[at], dgates[at]
        if more:
            o = o + before[part][0].astype(F32)
            d = d + before[2 + part][0, :, :width].astype(F32)
            t = t + before[2 + part][0, :, width:].astype(F32)
        outs[part][0] = o.astype(BF)
        outs[2 + part][0, :, :width] = d.astype(BF)
        outs[2 + part][0, :, width:] = t.astype(BF)
    grad_in = dot(x.T, dgu, 1, 0)
    grad_back = dot(dy.T, gact, 1, 0)

    @pl.when(step == 0)
    def _():
        acc_ref[:, :both] = grad_in
        acc_ref[:, both:] = grad_back

    @pl.when(step > 0)
    def _():
        acc_ref[:, :both] += grad_in
        acc_ref[:, both:] += grad_back

    @pl.when(step == pl.num_programs(0) - 1)
    def _():
        if joined:
            dws[0][...] = acc_ref[...].astype(BF)
        else:
            planes, _, shard, _ = w_ref.shape
            for d in range(n):
                for plane in range(planes):
                    row = pl.multiple_of((plane * n + (c + d) % n) * shard, shard)
                    dws[d][plane] = acc_ref[pl.ds(row, shard)].astype(BF)


def experts_call(xs, dys, place, router, weights, first, count, before):
    steps = len(xs) // 2
    half, width = xs[0].shape
    tile = 2 * half
    n = (len(weights) + 1) // 2
    joined = n == 1
    block = weights[0].shape
    whole_shape = block if joined else block[:1] + (n,) + block[1:]
    lanes = block[-1]
    out_block = pl.BlockSpec((1, half, width), lambda i: (i, 0, 0))
    dx_block = pl.BlockSpec((1, half, width + 128), lambda i: (i, 0, 0))
    whole = pl.BlockSpec(memory_space=pltpu.VMEM)
    anywhere = pl.BlockSpec(memory_space=pl.ANY)
    blocks = [out_block, out_block, dx_block, dx_block]
    rows = steps * tile
    return pl.pallas_call(
        functools.partial(experts_kernel, steps, first, count, bool(before), joined),
        grid=(steps,),
        in_specs=[
            pl.BlockSpec(memory_space=pltpu.SMEM),
            pl.BlockSpec((width, 128), lambda i: (0, 0)),
        ]
        + [anywhere] * (4 * steps + len(weights))
        + (blocks if before else []),
        out_specs=blocks + [whole] * n,
        out_shape=[jax.ShapeDtypeStruct((steps, half, width), BF)] * 2
        + [jax.ShapeDtypeStruct((steps, half, width + 128), BF)] * 2
        + [jax.ShapeDtypeStruct(block, BF)] * n,
        scratch_shapes=[
            pltpu.VMEM((width, lanes), F32),
            pltpu.VMEM(whole_shape, BF),
            pltpu.VMEM((2, tile, width), BF),
            pltpu.VMEM((2, tile, width + 128), BF),
            pltpu.SemaphoreType.DMA((2, 4)),
            pltpu.SemaphoreType.DMA((n,)),
        ],
        compiler_params=params("arbitrary"),
        cost_estimate=pl.CostEstimate(
            flops=6 * rows * width * lanes,
            bytes_accessed=8 * rows * width + 4 * width * lanes,
            transcendentals=rows * lanes // 3,
        ),
        name="experts",
    )(place, router, *xs, *dys, *weights, *(before or []))


def back_kernel(dq_ref, cos_ref, sin_ref, wq_ref, wkv_ref, *refs):
    *terms, dkv_ref, part_ref = refs
    total = functools.reduce(jnp.add, [t[...].astype(F32) for t in terms])
    kw = total.shape[1] // 2
    dk = turn(total[:, :kw], cos_ref[...], -sin_ref[...]).astype(BF)
    dkv = jnp.concatenate([dk, total[:, kw:].astype(BF)], axis=1)
    dkv_ref[...] = dkv
    part_ref[...] = (dot(dq_ref[...], wq_ref[...], 1, 1) + dot(dkv, wkv_ref[...], 1, 1)).astype(BF)


def back_call(dq, terms, cosine, sine, w_qo, w_kv):
    rows, qw = dq.shape
    lanes = terms[0].shape[1]
    d = w_qo.shape[0]
    tile = min(256, cosine.shape[0])
    per = cosine.shape[0] // tile
    row = lambda width: pl.BlockSpec((tile, width), lambda i: (i, 0))
    table = pl.BlockSpec((tile, 128), lambda i: (i % per, 0))
    return pl.pallas_call(
        back_kernel,
        grid=(rows // tile,),
        in_specs=[
            row(qw),
            table,
            table,
            pl.BlockSpec((d, qw), lambda i: (0, 0)),
            pl.BlockSpec((d, lanes), lambda i: (0, 0)),
        ]
        + [row(lanes)] * len(terms),
        out_specs=[row(lanes), row(d)],
        out_shape=[
            jax.ShapeDtypeStruct((rows, lanes), BF),
            jax.ShapeDtypeStruct((rows, d), BF),
        ],
        compiler_params=params("arbitrary"),
        cost_estimate=pl.CostEstimate(
            flops=2 * rows * d * (qw + lanes), bytes_accessed=8 * rows * d, transcendentals=0
        ),
        name="back",
    )(dq, cosine, sine, w_qo, w_kv, *terms)


def grads_kernel(pairs, extra, place_ref, *refs):
    refs = list(refs)
    sides = [[(refs.pop(0), refs.pop(0)) for _ in range(count)] for count in pairs]
    more = refs.pop(0) if extra else None
    count = len(refs)
    block = refs[0].shape[0]
    for s in range(count):
        at = pl.ds(pl.multiple_of((place_ref[0] ^ s) * block, block), block)
        column = 0
        for side in sides:
            total = functools.reduce(
                jnp.add, [dot(left[:, at], right[...], 0, 0) for left, right in side]
            )
            refs[s][:, column : column + total.shape[1]] = total.astype(BF)
            column += total.shape[1]
        if extra:
            refs[s][:, column:] = more[at, :]


def grads_call(me, sides, extra, count):
    d = sides[0][0][0].shape[1]
    lanes = sum(side[0][1].shape[1] for side in sides) + (0 if extra is None else extra.shape[1])
    whole = pl.BlockSpec(memory_space=pltpu.VMEM)
    operands = [a for side in sides for pair in side for a in pair]
    operands += [] if extra is None else [extra]
    return pl.pallas_call(
        functools.partial(grads_kernel, [len(side) for side in sides], extra is not None),
        in_specs=[pl.BlockSpec(memory_space=pltpu.SMEM)] + [whole] * len(operands),
        out_specs=[whole] * count,
        out_shape=[jax.ShapeDtypeStruct((d // count, lanes), BF)] * count,
        compiler_params=pltpu.CompilerParams(vmem_limit_bytes=VMEM_LIMIT),
        cost_estimate=pl.CostEstimate(
            flops=2 * d * lanes * 1024, bytes_accessed=4 * d * lanes, transcendentals=0
        ),
        name="grads",
    )(me, *operands)


def line_kernel(count, place_ref, *refs):
    terms, outs, scratch = refs[:-count - 1], refs[-count - 1 : -1], refs[-1]
    scratch[...] = functools.reduce(jnp.add, [t[...].astype(F32) for t in terms])
    shard = outs[0].shape[0]
    for s in range(count):
        row = pl.multiple_of((place_ref[0] ^ s) * shard, shard)
        outs[s][...] = scratch[pl.ds(row, shard)].astype(BF)


def line_call(me, terms, count):
    rows, lanes = terms[0].shape
    whole = pl.BlockSpec(memory_space=pltpu.VMEM)
    return pl.pallas_call(
        functools.partial(line_kernel, count),
        in_specs=[pl.BlockSpec(memory_space=pltpu.SMEM)] + [whole] * len(terms),
        out_specs=[whole] * count,
        out_shape=[jax.ShapeDtypeStruct((rows // count, lanes), BF)] * count,
        scratch_shapes=[pltpu.VMEM((rows, lanes), F32)],
        compiler_params=pltpu.CompilerParams(vmem_limit_bytes=VMEM_LIMIT),
        name="line",
    )(me, *terms)


def reorder_heads(values):
    parts = []
    for at in range(0, values.shape[1], 256):
        a = values[:, at : at + 128]
        b = values[:, at + 128 : at + 256]
        low = lax.broadcasted_iota(jnp.int32, a.shape, 1) < HD
        parts += [
            jnp.where(low, a, pltpu.roll(b, HD, 1)),
            jnp.where(low, pltpu.roll(a, HD, 1), b),
        ]
    return jnp.concatenate(parts, axis=1)


def finish_kernel(count, *refs):
    early = functools.reduce(jnp.add, [r[...].astype(F32) for r in refs[:count]])
    late = functools.reduce(jnp.add, [r[...].astype(F32) for r in refs[count : 2 * count]])
    q_ref, k_ref, v_ref, o_ref, small_ref = refs[2 * count :]
    qw = q_ref.shape[1]
    kw = k_ref.shape[1]
    q_ref[...] = reorder_heads(early[:, :qw])
    o_ref[...] = reorder_heads(early[:, qw:])
    k_ref[...] = late[:, :kw]
    v_ref[...] = late[:, kw : 2 * kw]
    small_ref[...] = late[:, 2 * kw :]


def finish_call(early, late, qw, kw):
    shard = early[0].shape[0]
    whole = pl.BlockSpec(memory_space=pltpu.VMEM)
    return pl.pallas_call(
        functools.partial(finish_kernel, len(early)),
        in_specs=[whole] * (2 * len(early)),
        out_specs=[whole] * 5,
        out_shape=[
            jax.ShapeDtypeStruct((shard, w), F32) for w in (qw, kw, kw, qw, 128)
        ],
        name="finish",
    )(*early, *late)


def expert_rows_kernel(count, place_ref, *refs):
    pieces, outs = refs[:-3], refs[-3:]
    groups = 2
    units = outs[0].shape[2]
    group = outs[0].shape[0] // (count * groups)
    for g in range(groups):
        for s in range(count):
            piece = pieces[g * count + s]
            at = ((place_ref[0] ^ s) * groups + g) * group
            for i in range(3):
                for e in range(group):
                    lanes = (i * group + e) * units
                    outs[i][at + e] = piece[:, lanes : lanes + units].astype(F32)


def expert_rows_call(me, pieces, experts, units):
    shard = pieces[0].shape[0]
    whole = pl.BlockSpec(memory_space=pltpu.VMEM)
    return pl.pallas_call(
        functools.partial(expert_rows_kernel, len(pieces) // 2),
        in_specs=[pl.BlockSpec(memory_space=pltpu.SMEM)] + [whole] * len(pieces),
        out_specs=[whole] * 3,
        out_shape=[jax.ShapeDtypeStruct((experts, shard, units), F32)] * 3,
        compiler_params=pltpu.CompilerParams(vmem_limit_bytes=VMEM_LIMIT),
        name="expert_rows",
    )(me, *pieces)


def apart(count, step):
    return [(i, i ^ step) for i in range(count)]


def swap(value):
    return lax.ppermute(value, "mp", [(0, 1), (1, 0)])


def pin(*values):
    return lax.optimization_barrier(values)


def up_hop(value, n, s):
    return lax.ppermute(value, "ctx", [(c, c + 1) for c in range(s, n - 1)])


def down_hop(value, n, s):
    return lax.ppermute(value, "ctx", [(c, c - 1) for c in range(1, n - s)])


def sum_up_hop(value, n, s):
    return lax.ppermute(value, "ctx", [(c, c + 1) for c in range(s + 1)])


def sum_down_hop(value, n, s):
    return lax.ppermute(value, "ctx", [(c, c - 1) for c in range(n - 1 - s, n)])


def add(*terms):
    return functools.reduce(jnp.add, [t.astype(F32) for t in terms]).astype(BF)


def by_xor(parts, me):
    bit = 1
    while bit < len(parts):
        flip = (me & bit) != 0
        parts = [jnp.where(flip, parts[i ^ bit], parts[i]) for i in range(len(parts))]
        bit *= 2
    return parts


def exchange(parts, axis):
    count = len(parts)
    return [parts[0]] + [
        lax.ppermute(parts[s], axis, apart(count, s)) for s in range(1, count)
    ]


def from_last(values, start, count):
    values = values[::-1]
    return lax.dynamic_slice_in_dim(jnp.concatenate([values, values]), start, count, 0)


def head_order(weight):
    rows, width = weight.shape
    return (
        weight.reshape(rows, width // (4 * HD), 2, 2, HD).swapaxes(2, 3).reshape(rows, width)
    )


def per_device(
    tokens,
    cotangent,
    routes,
    norm_gain,
    w_query,
    w_key,
    w_value,
    w_output,
    ffn_gain,
    w_router,
    w_gate,
    w_up,
    w_down,
):
    micro, seq_count, local, width = tokens.shape
    top = routes.shape[3]
    experts, shard, units = w_gate.shape
    dp = lax.axis_size("dp")
    n = lax.axis_size("ctx")
    hops = n == 4
    me_dp = lax.axis_index("dp")
    me_ctx = lax.axis_index("ctx")
    me_mp = lax.axis_index("mp")
    mine_count = experts // dp
    group = mine_count // 2
    micros = range(micro)
    per = seq_count * local
    half = per // 2
    rows = micro * per
    qw = w_query.shape[1]
    kw = w_key.shape[1]
    ctx_now = me_ctx.astype(jnp.int32).reshape(1)
    dp_now = me_dp.astype(jnp.int32).reshape(1)
    place = jnp.stack([me_dp * mine_count, me_ctx]).astype(jnp.int32)

    def in_order(mine, other):
        first = me_mp == 0
        return jnp.concatenate([jnp.where(first, mine, other), jnp.where(first, other, mine)])

    def halves(full):
        cut = full.reshape(2, half, full.shape[1])
        mine = lax.dynamic_index_in_dim(cut, me_mp, 0, keepdims=False)
        return mine, lax.dynamic_index_in_dim(cut, 1 - me_mp, 0, keepdims=False)

    def far_pieces(mine):
        return [lax.ppermute(mine, "dp", apart(dp, s)) for s in range(1, dp)]

    def paired(mine, far, other, near):
        return [piece for pair in zip([mine] + far, [other] + near) for piece in pair]

    def gather_line(value):
        return jnp.stack(
            [value] + [lax.ppermute(value, "ctx", apart(n, s)) for s in range(1, n)]
        )

    def gather_plane(value):
        return [value] + [lax.ppermute(value, "dp", apart(dp, s)) for s in range(1, dp)]

    def whole_rows(pieces):
        lines = by_xor(pieces, me_dp)
        full = jnp.stack(lines)
        cols = by_xor([full[:, i] for i in range(n)], me_ctx)
        return jnp.stack(cols, axis=1).reshape(dp * n * shard, full.shape[3])

    small = jnp.concatenate([w_router, norm_gain[:, None], ffn_gain[:, None]], axis=1)
    small = jnp.pad(small, ((0, 0), (0, 128 - small.shape[1])))
    kv_shard = jnp.concatenate([w_key, w_value, small], axis=1)
    qo_shard = jnp.concatenate([head_order(w_query), head_order(w_output)], axis=1)
    side = lambda w: w.reshape(dp, 2, group, shard, units)
    w3 = jnp.concatenate(
        [side(w)[:, :, e] for w in (w_gate, w_up, w_down) for e in range(group)], axis=3
    )
    if hops:
        kv_line = gather_line(kv_shard)
        qo_line = gather_line(qo_shard)
    w3_parts = exchange(by_xor([w3[i] for i in range(dp)], me_dp), "dp")
    own3 = by_xor(w3_parts, me_dp)
    own3 = [jnp.stack([o[g] for o in own3]) for g in range(2)]
    ups = [[], []]
    downs = [[], []]

    def weight_hop(g, s):
        if hops:
            ups[g].append(up_hop(ups[g][-1] if s else own3[g], n, s))
            downs[g].append(down_hop(downs[g][-1] if s else own3[g], n, s))

    if hops:
        kv_line, qo_line, own3 = pin(kv_line, qo_line, own3)
        kv_pieces = gather_plane(kv_line)
        weight_hop(0, 0)
        kv_pieces, qo_line, ups, downs, own3 = pin(kv_pieces, qo_line, ups, downs, own3)
        kv_full = whole_rows(kv_pieces)
        qo_pieces = gather_plane(qo_line)
    else:
        kv_full = lax.all_gather(kv_shard, ("dp", "ctx"), axis=0, tiled=True)
        qo_full = lax.all_gather(qo_shard, ("dp", "ctx"), axis=0, tiled=True)
        own3 = [lax.all_gather(o, "ctx", axis=1, tiled=False) for o in own3]
        own3 = [o.reshape(width, o.shape[-1]) for o in own3]
    small = kv_full[:, 2 * kw :]
    router = small[:, :experts]
    router_wide = jnp.pad(router, ((0, 0), (0, 128 - experts)))
    gain_one = small[:, experts].astype(F32)[None, :]
    gain_two = small[:, experts + 1].astype(F32)[None, :]

    position = me_ctx * local + jnp.arange(local, dtype=jnp.int32)
    freqs = THETA ** (-(jnp.arange(HD // 2, dtype=F32) * 2.0) / HD)
    angles = position.astype(F32)[:, None] * freqs[None, :]
    cosine = jnp.tile(jnp.cos(angles), (1, 4))
    sine = jnp.sin(angles)
    sine = jnp.concatenate([-sine, sine, -sine, sine], axis=1)
    x = tokens.reshape(rows, width)
    normed, kv = kv_call(x, gain_one, kv_full, 2 * kw, cosine, sine)
    kv = kv.reshape(1, micro * seq_count, local, 2 * kw)

    ids = routes.reshape(rows, top)
    marks = jnp.sum(
        (ids[:, :, None] == jnp.arange(128, dtype=jnp.int32)[None, None, :]).astype(F32), axis=1
    ).astype(BF)
    dy = cotangent.reshape(rows, width)
    dyx = jnp.concatenate([dy, marks], axis=1).reshape(micro, per, width + 128)
    dy_cut = [halves(dyx[m]) for m in micros]
    dy_far = [None] * micro
    dy_near = [None] * micro

    if hops:
        kv_got = up_hop(kv, n, 0)
        kv_got, qo_pieces, normed, dy_cut = pin(kv_got, qo_pieces, normed, dy_cut)
        kv_prev = [kv_got]
        qo_full = whole_rows(qo_pieces)
    else:
        every = lax.all_gather(kv[0], "ctx", axis=0, tiled=False)
        kv_prev = [from_last(every, n - me_ctx, n - 1)]
    w_out = qo_full[:, qw:]
    q = q_call(normed, qo_full, qw, cosine, sine).reshape(micro * seq_count, local, qw)
    if hops:
        carry = None
        own = kv
        for s in range(1, n):
            last = s == n - 1
            got = None if last else up_hop(kv_prev[-1], n, s)
            if s - 1 < micro:
                dy_far[s - 1] = far_pieces(dy_cut[s - 1][0])
            else:
                weight_hop(0, 1)
            if s >= 2:
                dy_near[s - 2] = [swap(f) for f in dy_far[s - 2]]
            carry = attn_part(ctx_now, q, own, [kv_prev[-1]], s, carry, last)
            if last:
                attn, lse = carry
                mixed = dot(attn.reshape(rows, qw), w_out, 1, 1).astype(BF)
                mixed, dy_near, ups, downs = pin(mixed, dy_near, ups, downs)
            else:
                got, carry, dy_far, dy_near = pin(got, carry, dy_far, dy_near)
                kv_prev.append(got)
            own = None
    else:
        attn, lse = attn_part(ctx_now, q, kv, kv_prev, 1, None, True)
        mixed = dot(attn.reshape(rows, qw), w_out, 1, 1).astype(BF)
    for m in micros:
        if dy_far[m] is None:
            dy_far[m] = far_pieces(dy_cut[m][0])
        if dy_near[m] is None:
            dy_near[m] = [swap(f) for f in dy_far[m]]
    dys = [paired(dy_cut[m][0], dy_far[m], dy_cut[m][1], dy_near[m]) for m in micros]

    mixed_got = swap(mixed)
    hidden = x.astype(F32) + (mixed.astype(F32) + mixed_got.astype(F32))
    inv_two = lax.rsqrt(jnp.mean(hidden * hidden, axis=1, keepdims=True) + EPS)
    ffn_low = (hidden * inv_two * gain_two).astype(BF)
    x_cut = [halves(ffn_low[m * per : (m + 1) * per]) for m in micros]
    x_far = [None] * micro
    x_near = [None] * micro

    x_cut, hidden, inv_two, ffn_low = pin(x_cut, hidden, inv_two, ffn_low)
    x_far[0] = far_pieces(x_cut[0][0])
    weight_hop(0, 2)
    x_far[0], ups, downs, x_cut = pin(x_far[0], ups, downs, x_cut)
    x_near[0] = [swap(f) for f in x_far[0]]
    x_near[0], x_cut = pin(x_near[0], x_cut)
    sums = []
    dws = [[], []]
    xs = []

    def run(g, m, before):
        whole = [own3[g]] + ups[g] + downs[g]
        part = experts_call(
            xs[m], dys[m], place, router_wide, whole, g * group, group, before
        )
        dws[g].append(part[4:])
        return part[:4]

    for m in micros:
        xs.append(paired(x_cut[m][0], x_far[m], x_cut[m][1], x_near[m]))
        sums.append(run(0, m, None))
        if m + 1 < micro:
            x_far[m + 1] = far_pieces(x_cut[m + 1][0])
        weight_hop(1, m)
        sums, dws, x_far, x_cut, ups, downs = pin(sums, dws, x_far, x_cut, ups, downs)
        if m + 1 < micro:
            x_near[m + 1] = [swap(f) for f in x_far[m + 1]]
            x_near, sums, x_cut, ups, downs = pin(x_near, sums, x_cut, ups, downs)
    if hops:
        for s in range(micro, n - 1):
            weight_hop(1, s)

    rising = [None, None]
    falling = [None, None]

    def grad_hop(g, s):
        if hops:
            d = n - 1 - s
            up_terms = [dw[d] for dw in dws[g]] + ([rising[g]] if s else [])
            down_terms = [dw[n - d] for dw in dws[g]] + ([falling[g]] if s else [])
            rising[g] = sum_up_hop(add(*up_terms), n, s)
            falling[g] = sum_down_hop(add(*down_terms), n, s)

    def grad_own(g):
        if hops:
            own = add(*[dw[0] for dw in dws[g]], rising[g], falling[g])
        else:
            whole = add(*[dw[0] for dw in dws[g]]).reshape(dp, n, shard, -1)
            own = lax.psum_scatter(whole, "ctx", scatter_dimension=1, tiled=False)
        return exchange(by_xor([own[i] for i in range(dp)], me_dp), "dp")

    parts = []
    dx_terms = []
    dx_back = []

    def terms_of(mine, got):
        return [add(mine[s], got[s]) for s in range(dp)]

    for m in micros:
        parts.append(run(1, m, sums[m]))
        if m > 0:
            dx_back.append(exchange(dx_terms[m - 1], "dp"))
        grad_hop(0, m)
        parts, dx_back, rising, falling, dws = pin(parts, dx_back, rising, falling, dws)
        if m + 1 < micro:
            dx_terms.append(terms_of(parts[m][2], swap(parts[m][3])))
            dx_terms, parts, dx_back = pin(dx_terms, parts, dx_back)

    cut = lambda whole, m: whole[m * per : (m + 1) * per]
    marked = dyx.reshape(rows, width + 128)[:, width : width + experts].astype(F32) > 0.5
    gates = masked_softmax(dot(ffn_low, router, 1, 0), marked)
    grad_sums = [0.0, 0.0]

    def before_attention(m):
        total = add(*dx_back[m])
        moe = in_order(total, swap(total)).astype(F32)
        dgate = moe[:, width : width + experts]
        gate = cut(gates, m)
        dlogit = gate * (dgate - jnp.sum(gate * dgate, axis=1, keepdims=True))
        dlogit = dlogit.astype(BF)
        grad_sums[0] = grad_sums[0] + dot(cut(ffn_low, m), dlogit, 0, 0)
        d_ffn = moe[:, :width] + dot(dlogit, router, 1, 1)
        unit = cut(hidden, m) * cut(inv_two, m)
        grad_sums[1] = grad_sums[1] + jnp.sum(d_ffn * unit, axis=0)
        g_two = d_ffn * gain_two
        dh = cut(dy, m).astype(F32) + cut(inv_two, m) * (
            g_two - unit * jnp.mean(g_two * unit, axis=1, keepdims=True)
        )
        dz = dh.astype(BF)
        return dh, dz, dot(dz, w_out, 1, 0).astype(BF)

    def attention_back(m, d_attn):
        dq, *dkv = attn_bwd(
            ctx_now,
            q,
            d_attn.reshape(seq_count, local, qw),
            attn,
            lse,
            cosine,
            sine,
            kv,
            kv_prev,
            m * seq_count,
        )
        return dq.reshape(per, qw), dkv

    dkv_sum = [None] * micro

    def dkv_hop(m, s):
        if hops:
            d = n - 1 - s
            term = dkv[m][d] if s == 0 else add(dkv[m][d], dkv_sum[m])
            dkv_sum[m] = sum_down_hop(term, n, s)

    def dkv_own(m):
        if hops:
            both = [dkv[m][0], dkv_sum[m]]
        else:
            every = from_last(jnp.concatenate(dkv[m]), n - 1 - me_ctx, n)
            both = [lax.psum_scatter(every, "ctx", scatter_dimension=0, tiled=True)]
        return [b.reshape(per, 2 * kw) for b in both]

    dh, dz, d_attn, dq, dkv = ([None] * micro for _ in range(5))
    out_terms = [None] * micro
    out_back = [None] * micro
    last = micro - 1
    dh[0], dz[0], d_attn[0] = before_attention(0)
    dx_terms.append(terms_of(parts[last][2], swap(parts[last][3])))
    d_attn, dx_terms, dh, dz = pin(d_attn, dx_terms, dh, dz)
    dx_back.append(exchange(dx_terms[last], "dp"))
    dq[0], dkv[0] = attention_back(0, d_attn[0])
    grad_hop(0, 2)
    dx_back, dq, dkv, rising, falling = pin(dx_back, dq, dkv, rising, falling)
    dkv_hop(0, 0)
    dh[last], dz[last], d_attn[last] = before_attention(last)
    d_attn, dkv_sum, dh, dz, dkv = pin(d_attn, dkv_sum, dh, dz, dkv)
    dkv_hop(0, 1)
    grad_hop(1, 0)
    dq[last], dkv[last] = attention_back(last, d_attn[last])
    dkv_sum, dq, dkv, rising, falling, parts = pin(dkv_sum, dq, dkv, rising, falling, parts)
    dkv_hop(0, 2)
    dkv_hop(last, 0)
    pieces_now = dp_now if hops else jnp.zeros((1,), jnp.int32)
    early = grads_call(
        pieces_now,
        [
            [(cut(normed, m), dq[m]) for m in micros],
            [(dz[m], attn[m * seq_count : (m + 1) * seq_count].reshape(per, qw)) for m in micros],
        ],
        None,
        dp,
    )
    out_got = [swap(parts[m][1]) for m in micros]
    early, out_got, dkv_sum, dkv, parts = pin(early, out_got, dkv_sum, dkv, parts)
    dkv_hop(last, 1)
    grad_hop(1, 1)
    if hops:
        early = exchange(early, "dp")
    owned = [grad_own(0)]
    out_terms = [terms_of(parts[m][0], out_got[m]) for m in micros]
    dkv_own_m, part = [None] * micro, [None] * micro

    def back(m):
        return back_call(dq[m], dkv_own(m), cosine, sine, qo_full, kv_full)

    dkv_own_m[0], part[0] = back(0)
    early, out_terms, dkv_sum, rising, falling, owned, part, dkv, dkv_own_m = pin(
        early, out_terms, dkv_sum, rising, falling, owned, part, dkv, dkv_own_m
    )
    dkv_hop(last, 2)
    if hops:
        early = exchange(line_call(ctx_now, early, n), "ctx")
    out_back[0] = exchange(out_terms[0], "dp")
    early, dkv_sum, out_back, out_terms, part, dkv = pin(
        early, dkv_sum, out_back, out_terms, part, dkv
    )
    grad_hop(1, 2)
    dkv_own_m[last], part[last] = back(last)
    got = [swap(p) for p in part]
    rows_late = [(cut(normed, m), dkv_own_m[m]) for m in micros]
    d_normed = jnp.concatenate([p.astype(F32) + g.astype(F32) for p, g in zip(part, got)])
    out_back[last] = exchange(out_terms[last], "dp")
    got, d_normed, out_back, rising, falling = pin(got, d_normed, out_back, rising, falling)
    x32 = x.astype(F32)
    inv_one = lax.rsqrt(jnp.mean(x32 * x32, axis=1, keepdims=True) + EPS)
    n_one = x32 * inv_one
    grad_gain_one = jnp.sum(d_normed * n_one, axis=0)
    small_grad = jnp.concatenate(
        [grad_sums[0], grad_gain_one[:, None], grad_sums[1][:, None]], axis=1
    )
    small_grad = jnp.pad(small_grad, ((0, 0), (0, 128 - small_grad.shape[1]))).astype(BF)
    late = grads_call(pieces_now, [rows_late], small_grad, dp)
    if hops:
        late = exchange(late, "dp")
        late = exchange(line_call(ctx_now, late, n), "ctx")
    else:
        early, late = (
            [
                lax.psum_scatter(
                    jnp.concatenate(p), ("dp", "ctx"), scatter_dimension=0, tiled=True
                )
            ]
            for p in (early, late)
        )
    owned.append(grad_own(1))
    g_one = d_normed * gain_one
    input_grad = (
        jnp.concatenate(dh)
        + inv_one * (g_one - n_one * jnp.mean(g_one * n_one, axis=1, keepdims=True))
    ).astype(BF)
    totals = [add(*b) for b in out_back]
    moe = jnp.concatenate([in_order(t, swap(t)) for t in totals])
    output = (hidden + moe.astype(F32)).astype(BF)
    grad_q, grad_k, grad_v, grad_o, small_grad = finish_call(early, late, qw, kw)
    dw_gate, dw_up, dw_down = expert_rows_call(dp_now, owned[0] + owned[1], experts, units)
    shape = tokens.shape
    return (
        output.reshape(shape),
        input_grad.reshape(shape),
        small_grad[:, experts],
        grad_q,
        grad_k,
        grad_v,
        grad_o,
        small_grad[:, experts + 1],
        small_grad[:, :experts],
        dw_gate,
        dw_up,
        dw_down,
    )


def solution(mesh):
    rows = P(None, "dp", "ctx", None)
    vector = P(("dp", "ctx"))
    matrix = P(("dp", "ctx"), "mp")
    router = P(("dp", "ctx"), None)
    expert = P(None, ("dp", "ctx"), "mp")
    return jax.shard_map(
        per_device,
        mesh=mesh,
        in_specs=(
            rows,
            rows,
            rows,
            vector,
            matrix,
            matrix,
            matrix,
            matrix,
            vector,
            router,
            expert,
            expert,
            expert,
        ),
        out_specs=(
            rows,
            rows,
            vector,
            matrix,
            matrix,
            matrix,
            matrix,
            vector,
            router,
            expert,
            expert,
            expert,
        ),
        check_vma=False,
    )
```

```python
import functools
import math

import jax
import jax.numpy as jnp
from jax import lax
from jax.experimental import pallas as pl
from jax.experimental.pallas import tpu as pltpu
from jax.sharding import PartitionSpec as P

HD = 64
EPS = 1e-06
THETA = 10000.0
NEG = -1e30
VMEM_LIMIT = 60 * 1024 * 1024
BF = jnp.bfloat16
F32 = jnp.float32


def dot(a, b, ca, cb, precision=None):
    return lax.dot_general(
        a, b, (((ca,), (cb,)), ((), ())), preferred_element_type=F32, precision=precision
    )


def params(*semantics):
    return pltpu.CompilerParams(dimension_semantics=semantics, vmem_limit_bytes=VMEM_LIMIT)


def turn(values, cosine, sine):
    width = values.shape[1]
    lane = lax.broadcasted_iota(jnp.int32, values.shape, 1)
    ahead = pltpu.roll(values, width - HD // 2, 1)
    behind = pltpu.roll(values, HD // 2, 1)
    swapped = jnp.where(lane % HD < HD // 2, ahead, behind)
    reps = width // cosine.shape[1]
    return values * jnp.tile(cosine, (1, reps)) + swapped * jnp.tile(sine, (1, reps))


def kv_kernel(x_ref, gain_ref, w_ref, cos_ref, sin_ref, normed_ref, kv_ref):
    x = x_ref[...].astype(F32)
    inv = lax.rsqrt(jnp.mean(x * x, axis=1, keepdims=True) + EPS)
    normed = (x * inv * gain_ref[...]).astype(BF)
    normed_ref[...] = normed
    kw = kv_ref.shape[1] // 2
    raw = dot(normed, w_ref[...], 1, 0)
    kv_ref[:, :kw] = turn(raw[:, :kw], cos_ref[...], sin_ref[...]).astype(BF)
    kv_ref[:, kw:] = raw[:, kw:].astype(BF)


def q_kernel(normed_ref, w_ref, cos_ref, sin_ref, q_ref):
    raw = dot(normed_ref[...], w_ref[...], 1, 0)
    q_ref[...] = turn(raw, cos_ref[...], sin_ref[...]).astype(BF)


def row_specs(rows, local, d, lanes):
    tile = min(256, local)
    per = local // tile
    return (
        rows // tile,
        pl.BlockSpec((tile, d), lambda i: (i, 0)),
        pl.BlockSpec((d, lanes), lambda i: (0, 0)),
        pl.BlockSpec((tile, 128), lambda i: (i % per, 0)),
        pl.BlockSpec((tile, lanes), lambda i: (i, 0)),
        pl.CostEstimate(
            flops=2 * rows * d * lanes, bytes_accessed=6 * rows * d, transcendentals=rows
        ),
    )


def kv_call(x, gain, w, lanes, cosine, sine):
    rows, d = x.shape
    steps, row, weight, table, out, cost = row_specs(rows, cosine.shape[0], d, lanes)
    return pl.pallas_call(
        kv_kernel,
        grid=(steps,),
        in_specs=[row, pl.BlockSpec((1, d), lambda i: (0, 0)), weight, table, table],
        out_specs=[row, out],
        out_shape=[
            jax.ShapeDtypeStruct((rows, d), BF),
            jax.ShapeDtypeStruct((rows, lanes), BF),
        ],
        compiler_params=params("arbitrary"),
        cost_estimate=cost,
        name="kv",
    )(x, gain, w, cosine, sine)


def q_call(normed, w, lanes, cosine, sine):
    rows, d = normed.shape
    steps, row, weight, table, out, cost = row_specs(rows, cosine.shape[0], d, lanes)
    return pl.pallas_call(
        q_kernel,
        grid=(steps,),
        in_specs=[row, weight, table, table],
        out_specs=out,
        out_shape=jax.ShapeDtypeStruct((rows, lanes), BF),
        compiler_params=params("arbitrary"),
        cost_estimate=cost,
        name="q",
    )(normed, w, cosine, sine)


def half_mask(block, which):
    lane = lax.broadcasted_iota(jnp.int32, block.shape, 1)
    keep = (lane < HD) if which == 0 else (lane >= HD)
    return jnp.where(keep, block, jnp.zeros_like(block))


def stacked(ref):
    return jnp.concatenate([ref[0, :, :128], ref[0, :, 128:]], axis=0)


def causal(shape, length):
    key = lax.broadcasted_iota(jnp.int32, shape, 0)
    query = lax.broadcasted_iota(jnp.int32, shape, 1) % length
    return key <= query


def each_earlier(c, counts, visit, otherwise=None, first=1):
    for piece, count in enumerate(counts):
        if count == 1:

            @pl.when(c >= first)
            def _():
                visit(piece, 0)

            if otherwise is not None:

                @pl.when(c < first)
                def _():
                    otherwise(piece, 0)

        else:
            reach = jnp.clip(c - first + 1, 0, count)

            @pl.loop(0, reach)
            def _(entry):
                visit(piece, entry)

            if otherwise is not None:

                @pl.loop(reach, count)
                def _(entry):
                    otherwise(piece, entry)

        first += count


def attn_part_kernel(counts, start, first, last, ctx_ref, q_ref, *refs):
    refs = list(refs)
    pieces = len(counts) + first
    keys = [refs.pop(0) for _ in range(pieces)]
    vals = [refs.pop(0) for _ in range(pieces)]
    old = None if first else [refs.pop(0) for _ in range(2)]
    if last:
        o_ref, lse_ref, stats_ref, acc_ref = refs
    else:
        stats_ref, acc_ref = (ref.at[0, 0] for ref in refs)
    length = q_ref.shape[1]
    both = (stacked(q_ref).astype(F32) * HD**-0.5).astype(BF)
    c = ctx_ref[0]

    if first:
        k = keys[0][0, 0]
        v = vals[0][0, 0]
        for i in range(2):
            s = dot(half_mask(k, i), both, 1, 1)
            s = jnp.where(causal(s.shape, length), s, NEG)
            peak = jnp.max(s, axis=0, keepdims=True)
            p = jnp.exp(s - peak)
            stats_ref[i : i + 1] = peak
            stats_ref[i + 2 : i + 3] = jnp.sum(p, axis=0, keepdims=True)
            acc_ref[i] = dot(v, p.astype(BF), 0, 0)
    else:
        stats_ref[...] = old[0][0, 0]
        acc_ref[...] = old[1][0, 0]

    def visit(piece, entry):
        k = keys[piece + first][entry, 0]
        v = vals[piece + first][entry, 0]
        for i in range(2):
            s = dot(half_mask(k, i), both, 1, 1)
            peak = stats_ref[i : i + 1]
            now = jnp.maximum(peak, jnp.max(s, axis=0, keepdims=True))
            p = jnp.exp(s - now)
            factor = jnp.exp(peak - now)
            stats_ref[i : i + 1] = now
            stats_ref[i + 2 : i + 3] = stats_ref[i + 2 : i + 3] * factor + jnp.sum(
                p, axis=0, keepdims=True
            )
            acc_ref[i] = acc_ref[i] * factor + dot(v, p.astype(BF), 0, 0)

    each_earlier(c, counts, visit, None, start)
    if last:
        row = lax.broadcasted_iota(jnp.int32, acc_ref.shape[1:], 0)
        stats = stats_ref[...]
        out = jnp.where(row < HD, acc_ref[0] / stats[2:3], acc_ref[1] / stats[3:4]).T
        o_ref[0, :, :128] = out[:length].astype(BF)
        o_ref[0, :, 128:] = out[length:].astype(BF)
        lse_ref[0, 0] = stats[:2] + jnp.log(stats[2:])


def kv_specs(pieces, length, lanes, at=0):
    kb = lanes // 256
    keys = [
        pl.BlockSpec((a.shape[0], 1, length, 128), lambda s, p: (0, s + at, 0, p)) for a in pieces
    ]
    vals = [
        pl.BlockSpec((a.shape[0], 1, length, 128), lambda s, p: (0, s + at, 0, kb + p))
        for a in pieces
    ]
    return keys + vals


def attn_part(ctx, q, own, prev, start, carry, last):
    seqs, length, qw = q.shape
    pairs = qw // 256
    cols = 2 * length
    first = own is not None
    pieces = ([own] if first else []) + prev
    counts = tuple(a.shape[0] for a in prev)
    spans = first + sum(counts)
    state = [
        pl.BlockSpec((1, 1, 4, cols), lambda s, p: (s, p, 0, 0)),
        pl.BlockSpec((1, 1, 2, 128, cols), lambda s, p: (s, p, 0, 0, 0)),
    ]
    if last:
        out_specs = [
            pl.BlockSpec((1, length, 256), lambda s, p: (s, 0, p)),
            pl.BlockSpec((1, 1, 2, cols), lambda s, p: (s, p, 0, 0)),
        ]
        out_shape = [
            jax.ShapeDtypeStruct((seqs, length, qw), BF),
            jax.ShapeDtypeStruct((seqs, pairs, 2, cols), F32),
        ]
        scratch = [pltpu.VMEM((4, cols), F32), pltpu.VMEM((2, 128, cols), F32)]
    else:
        out_specs = state
        out_shape = [
            jax.ShapeDtypeStruct((seqs, pairs, 4, cols), F32),
            jax.ShapeDtypeStruct((seqs, pairs, 2, 128, cols), F32),
        ]
        scratch = []
    return pl.pallas_call(
        functools.partial(attn_part_kernel, counts, start, first, last),
        grid=(seqs, pairs),
        in_specs=[
            pl.BlockSpec(memory_space=pltpu.SMEM),
            pl.BlockSpec((1, length, 256), lambda s, p: (s, 0, p)),
        ]
        + kv_specs(pieces, length, pieces[0].shape[3])
        + ([] if first else state),
        out_specs=out_specs,
        out_shape=out_shape,
        scratch_shapes=scratch,
        compiler_params=params("arbitrary", "arbitrary"),
        cost_estimate=pl.CostEstimate(
            flops=16 * seqs * length * length * spans * qw,
            bytes_accessed=4 * seqs * length * spans * qw,
            transcendentals=seqs * length * length * spans * qw // 64,
        ),
        name="attn_fwd",
    )(ctx, q, *pieces, *pieces, *(carry or []))


def attn_bwd_kernel(counts, ctx_ref, q_ref, do_ref, o_ref, lse_ref, cos_ref, sin_ref, *refs):
    pieces = len(counts)
    keys = refs[: pieces + 1]
    vals = refs[pieces + 1 : 2 * pieces + 2]
    dq_ref = refs[2 * pieces + 2]
    outs = refs[2 * pieces + 3 : 3 * pieces + 4]
    acc_ref = refs[3 * pieces + 4]
    length = q_ref.shape[1]
    lanes = outs[0].shape[3]
    pair = pl.program_id(1)
    both = (stacked(q_ref).astype(F32) * HD**-0.5).astype(BF)
    dboth = stacked(do_ref)
    prod = dboth.astype(F32) * stacked(o_ref).astype(F32)
    pick_row = lax.broadcasted_iota(jnp.int32, (8, 128), 0)
    pick_lane = lax.broadcasted_iota(jnp.int32, (8, 128), 1) // HD
    picks = (pick_row == pick_lane).astype(F32)
    delta = dot(picks, prod, 1, 1, lax.Precision.HIGHEST)
    c = ctx_ref[0]
    k_at = pl.ds(pl.multiple_of(pair * 128, 128), 128)
    v_at = pl.ds(pl.multiple_of(lanes // 2 + pair * 128, 128), 128)

    def block(piece, entry, diagonal):
        k = keys[piece][entry, 0]
        v = vals[piece][entry, 0]
        parts = []
        dq = None
        for i in range(2):
            ki = half_mask(k, i)
            s = dot(ki, both, 1, 1)
            p = jnp.exp(s - lse_ref[0, 0, i : i + 1, :])
            if diagonal:
                p = jnp.where(causal(s.shape, length), p, 0.0)
            dp = dot(half_mask(v, i), dboth, 1, 1)
            ds = (p * (dp - delta[i : i + 1, :])).astype(BF)
            parts.append((dot(ds, both, 1, 0), dot(p.astype(BF), dboth, 1, 0)))
            part = dot(ki, ds, 0, 0)
            dq = part if dq is None else dq + part
        low = lax.broadcasted_iota(jnp.int32, (length, 128), 1) < HD
        outs[piece][entry, 0, :, k_at] = jnp.where(low, parts[0][0], parts[1][0]).astype(BF)
        outs[piece][entry, 0, :, v_at] = jnp.where(low, parts[0][1], parts[1][1]).astype(BF)
        return dq

    acc_ref[...] = block(0, 0, True)

    def visit(piece, entry):
        acc_ref[...] += block(piece + 1, entry, False)

    def clear(piece, entry):
        outs[piece + 1][entry, 0, :, k_at] = jnp.zeros((length, 128), BF)
        outs[piece + 1][entry, 0, :, v_at] = jnp.zeros((length, 128), BF)

    each_earlier(c, counts, visit, clear)
    out = acc_ref[...].T * HD**-0.5
    cosine = cos_ref[...]
    sine = -sin_ref[...]
    dq_ref[0, :, :128] = turn(out[:length], cosine, sine).astype(BF)
    dq_ref[0, :, 128:] = turn(out[length:], cosine, sine).astype(BF)


def attn_bwd(ctx, q, do, o, lse, cosine, sine, own, prev, at):
    seqs, length, qw = do.shape
    pairs = qw // 256
    pieces = [own] + prev
    counts = tuple(a.shape[0] for a in prev)
    spans = 1 + sum(counts)
    blk = pl.BlockSpec((1, length, 256), lambda s, p: (s, 0, p))
    blk_at = pl.BlockSpec((1, length, 256), lambda s, p: (s + at, 0, p))
    tab = pl.BlockSpec((length, 128), lambda s, p: (0, 0))
    return pl.pallas_call(
        functools.partial(attn_bwd_kernel, counts),
        grid=(seqs, pairs),
        in_specs=[
            pl.BlockSpec(memory_space=pltpu.SMEM),
            blk_at,
            blk,
            blk_at,
            pl.BlockSpec((1, 1, 2, 2 * length), lambda s, p: (s + at, p, 0, 0)),
            tab,
            tab,
        ]
        + kv_specs(pieces, length, own.shape[3], at),
        out_specs=[blk]
        + [
            pl.BlockSpec((a.shape[0], 1) + a.shape[2:], lambda s, p: (0, s, 0, 0)) for a in pieces
        ],
        out_shape=[jax.ShapeDtypeStruct((seqs, length, qw), BF)]
        + [jax.ShapeDtypeStruct((a.shape[0], seqs) + a.shape[2:], BF) for a in pieces],
        scratch_shapes=[pltpu.VMEM((128, 2 * length), F32)],
        compiler_params=params("arbitrary", "arbitrary"),
        cost_estimate=pl.CostEstimate(
            flops=40 * seqs * length * length * spans * qw,
            bytes_accessed=8 * seqs * length * spans * qw,
            transcendentals=seqs * length * length * spans * qw // 64,
        ),
        name="attn_bwd",
    )(ctx, q, do, o, lse, cosine, sine, *pieces, *pieces)


def masked_softmax(logits, named):
    peak = jnp.max(jnp.where(named, logits, NEG), axis=1, keepdims=True)
    grown = jnp.where(named, jnp.exp(jnp.where(named, logits - peak, 0.0)), 0.0)
    return grown / jnp.sum(grown, axis=1, keepdims=True)


def experts_kernel(steps, first, count, micro, more, added, joined, place_ref, router_ref, *refs):
    refs = list(refs)
    n = 1 if joined else refs[-7].shape[1]
    xs = [refs.pop(0) for _ in range(2 * steps)]
    dys = [refs.pop(0) for _ in range(2 * steps)]
    ws = [refs.pop(0) for _ in range(n)]
    before = [refs.pop(0) for _ in range(4)] if more else None
    dws_before = [refs.pop(0) for _ in range(n)] if added else []
    outs = [refs.pop(0) for _ in range(4)]
    dws = [refs.pop(0) for _ in range(n)]
    acc_ref, w_ref, xbuf, dybuf, dwbuf, sems, wsems, dwsems = refs
    step = pl.program_id(0)
    base = place_ref[0]
    c = place_ref[1]
    rows, width = xbuf.shape[1:]
    units = w_ref.shape[-1] // (3 * count)
    both = 2 * count * units
    half = rows // 2

    def copies(t, slot):
        return [
            pltpu.make_async_copy(
                src[2 * t + part].at[micro] if which else src[2 * t + part],
                buf.at[slot, pl.ds(part * half, half)],
                sems.at[slot, 2 * which + part],
            )
            for which, (src, buf) in enumerate(((xs, xbuf), (dys, dybuf)))
            for part in range(2)
        ]

    def fetch(at, slot):
        for t in range(steps):

            @pl.when(at == t)
            def _():
                for copy in copies(t, slot):
                    copy.start()

    def weight_copy(d):
        to = w_ref if joined else w_ref.at[:, c ^ d]
        return pltpu.make_async_copy(ws[d], to, wsems.at[d])

    def added_copy(d):
        return pltpu.make_async_copy(dws_before[d], dwbuf.at[d], dwsems.at[d])

    slot = step % 2

    @pl.when(step == 0)
    def _():
        fetch(step, slot)
        for d in range(n):
            weight_copy(d).start()
        for d in range(n):
            weight_copy(d).wait()
        if added:
            for d in range(n):
                added_copy(d).start()

    @pl.when(step + 1 < steps)
    def _():
        fetch(step + 1, 1 - slot)

    for copy in copies(0, slot):
        copy.wait()

    x = xbuf[slot]
    dy = dybuf[slot, :, :width]
    lane = lax.broadcasted_iota(jnp.int32, (rows, 128), 1)
    named = dybuf[slot, :, width:].astype(F32) > 0.5
    gates = masked_softmax(dot(x, router_ref[...], 1, 0), named)
    gates = pltpu.roll(gates, 128 - base, 1)
    w_in = w_ref[..., :both].reshape(width, both)
    w_back = w_ref[..., both:].reshape(width, both // 2)
    gu = dot(x, w_in, 1, 0)
    g = gu[:, : both // 2]
    u = gu[:, both // 2 :]
    z = dot(dy, w_back, 1, 0)
    gate = jnp.concatenate(
        [
            jnp.broadcast_to(gates[:, first + e : first + e + 1], (rows, units))
            for e in range(count)
        ],
        axis=1,
    )
    sig = 1.0 / (1.0 + jnp.exp(-g))
    silu = g * sig
    act = silu * u
    product = act.astype(BF).astype(F32) * z
    dgates = jnp.zeros((rows, 128), F32)
    for e in range(count):
        total = jnp.sum(product[:, e * units : (e + 1) * units], axis=1, keepdims=True)
        dgates = jnp.where(lane == base + first + e, total, dgates)
    gact = (gate * act).astype(BF)
    da = gate * z
    dgu = jnp.concatenate(
        [
            (da * u * (sig * (1.0 + g * (1.0 - sig)))).astype(BF),
            (da * silu).astype(BF),
        ],
        axis=1,
    )
    out = dot(gact, w_back, 1, 1)
    dx = dot(dgu, w_in, 1, 1)
    for part in range(2):
        at = slice(part * half, (part + 1) * half)
        o, d, t = out[at], dx[at], dgates[at]
        if more:
            o = o + before[part][0].astype(F32)
            d = d + before[2 + part][0, :, :width].astype(F32)
            t = t + before[2 + part][0, :, width:].astype(F32)
        outs[part][0] = o.astype(BF)
        outs[2 + part][0, :, :width] = d.astype(BF)
        outs[2 + part][0, :, width:] = t.astype(BF)

    @pl.when(step == 0)
    def _():
        acc_ref[...] = jnp.zeros_like(acc_ref)

    acc_ref[:, :both] += dot(x.T, dgu, 1, 0)
    acc_ref[:, both:] += dot(dy.T, gact, 1, 0)

    @pl.when(step == pl.num_programs(0) - 1)
    def _():
        for d in range(n):
            if added:
                added_copy(d).wait()
            if joined:
                total = acc_ref[...]
                dws[0][...] = (total + dwbuf[0].astype(F32) if added else total).astype(BF)
                continue
            planes, _, shard, _ = w_ref.shape
            for plane in range(planes):
                row = pl.multiple_of((plane * n + (c ^ d)) * shard, shard)
                total = acc_ref[pl.ds(row, shard)]
                if added:
                    total = total + dwbuf[d, plane].astype(F32)
                dws[d][plane] = total.astype(BF)


def experts_call(
    xs, dys, micro, place, router, weights, first, count, before, dws_before
):
    steps = len(xs) // 2
    half, width = xs[0].shape
    tile = 2 * half
    n = len(weights)
    joined = n == 1
    block = weights[0].shape
    whole_shape = block if joined else block[:1] + (n,) + block[1:]
    lanes = block[-1]
    out_block = pl.BlockSpec((1, half, width), lambda i: (i, 0, 0))
    dx_block = pl.BlockSpec((1, half, width + 128), lambda i: (i, 0, 0))
    whole = pl.BlockSpec(memory_space=pltpu.VMEM)
    anywhere = pl.BlockSpec(memory_space=pl.ANY)
    blocks = [out_block, out_block, dx_block, dx_block]
    rows = steps * tile
    return pl.pallas_call(
        functools.partial(
            experts_kernel, steps, first, count, micro, bool(before), bool(dws_before), joined
        ),
        grid=(steps,),
        in_specs=[
            pl.BlockSpec(memory_space=pltpu.SMEM),
            pl.BlockSpec((width, 128), lambda i: (0, 0)),
        ]
        + [anywhere] * (4 * steps + n)
        + (blocks if before else [])
        + [anywhere] * len(dws_before),
        out_specs=blocks + [whole] * n,
        out_shape=[jax.ShapeDtypeStruct((steps, half, width), BF)] * 2
        + [jax.ShapeDtypeStruct((steps, half, width + 128), BF)] * 2
        + [jax.ShapeDtypeStruct(block, BF)] * n,
        scratch_shapes=[
            pltpu.VMEM((width, lanes), F32),
            pltpu.VMEM(whole_shape, BF),
            pltpu.VMEM((2, tile, width), BF),
            pltpu.VMEM((2, tile, width + 128), BF),
            pltpu.VMEM(((n if dws_before else 1),) + (block if dws_before else (16, 128)), BF),
            pltpu.SemaphoreType.DMA((2, 4)),
            pltpu.SemaphoreType.DMA((n,)),
            pltpu.SemaphoreType.DMA((n,)),
        ],
        compiler_params=params("arbitrary"),
        cost_estimate=pl.CostEstimate(
            flops=6 * rows * width * lanes,
            bytes_accessed=8 * rows * width + 4 * width * lanes,
            transcendentals=rows * lanes // 3,
        ),
        name="experts",
    )(place, router, *xs, *dys, *weights, *(before or []), *dws_before)


def back_kernel(dq_ref, x_ref, cos_ref, sin_ref, wq_ref, wkv_ref, *refs):
    *terms, dkv_ref, part_ref, gain_ref = refs
    total = functools.reduce(jnp.add, [t[...].astype(F32) for t in terms])
    kw = total.shape[1] // 2
    dk = turn(total[:, :kw], cos_ref[...], -sin_ref[...]).astype(BF)
    dkv = jnp.concatenate([dk, total[:, kw:].astype(BF)], axis=1)
    dkv_ref[...] = dkv
    part = dot(dq_ref[...], wq_ref[...], 1, 1) + dot(dkv, wkv_ref[...], 1, 1)
    part_ref[...] = part.astype(BF)
    x = x_ref[...].astype(F32)
    unit = x * lax.rsqrt(jnp.mean(x * x, axis=1, keepdims=True) + EPS)
    sums = jnp.broadcast_to(jnp.sum(part * unit, axis=0, keepdims=True), gain_ref.shape)

    @pl.when(pl.program_id(0) == 0)
    def _():
        gain_ref[...] = sums

    @pl.when(pl.program_id(0) > 0)
    def _():
        gain_ref[...] += sums


def back_call(dq, terms, x, micro, cosine, sine, w_qo, w_kv):
    rows, qw = dq.shape
    lanes = terms[0].shape[1]
    d = w_qo.shape[0]
    tile = min(256, cosine.shape[0])
    per = cosine.shape[0] // tile
    row = lambda width: pl.BlockSpec((tile, width), lambda i: (i, 0))
    table = pl.BlockSpec((tile, 128), lambda i: (i % per, 0))
    return pl.pallas_call(
        back_kernel,
        grid=(rows // tile,),
        in_specs=[
            row(qw),
            pl.BlockSpec((tile, d), lambda i: (i + micro * (rows // tile), 0)),
            table,
            table,
            pl.BlockSpec((d, qw), lambda i: (0, 0)),
            pl.BlockSpec((d, lanes), lambda i: (0, 0)),
        ]
        + [row(lanes)] * len(terms),
        out_specs=[row(lanes), row(d), pl.BlockSpec((8, d), lambda i: (0, 0))],
        out_shape=[
            jax.ShapeDtypeStruct((rows, lanes), BF),
            jax.ShapeDtypeStruct((rows, d), BF),
            jax.ShapeDtypeStruct((8, d), F32),
        ],
        compiler_params=params("arbitrary"),
        cost_estimate=pl.CostEstimate(
            flops=2 * rows * d * (qw + lanes), bytes_accessed=8 * rows * d, transcendentals=0
        ),
        name="back",
    )(dq, x, cosine, sine, w_qo, w_kv, *terms)


def grads_kernel(pairs, starts, extra, place_ref, *refs):
    refs = list(refs)
    sides = [[(refs.pop(0), refs.pop(0)) for _ in range(count)] for count in pairs]
    more = refs.pop(0) if extra else None
    count = len(refs)
    block = refs[0].shape[0]
    for s in range(count):
        at = pl.ds(pl.multiple_of((place_ref[0] ^ s) * block, block), block)
        column = 0
        for side, firsts in zip(sides, starts):
            total = functools.reduce(
                jnp.add,
                [
                    dot(left[first : first + right.shape[0], at], right[...], 0, 0)
                    for (left, right), first in zip(side, firsts)
                ],
            )
            refs[s][:, column : column + total.shape[1]] = total.astype(BF)
            column += total.shape[1]
        if extra:
            refs[s][:, column:] = more[at, :]


def grads_call(me, sides, extra, count):
    d = sides[0][0][0].shape[1]
    lanes = sum(side[0][1].shape[1] for side in sides) + (0 if extra is None else extra.shape[1])
    whole = pl.BlockSpec(memory_space=pltpu.VMEM)
    operands = [a for side in sides for term in side for a in term[:2]]
    starts = [[term[2] for term in side] for side in sides]
    operands += [] if extra is None else [extra]
    return pl.pallas_call(
        functools.partial(grads_kernel, [len(side) for side in sides], starts, extra is not None),
        in_specs=[pl.BlockSpec(memory_space=pltpu.SMEM)] + [whole] * len(operands),
        out_specs=[whole] * count,
        out_shape=[jax.ShapeDtypeStruct((d // count, lanes), BF)] * count,
        compiler_params=pltpu.CompilerParams(vmem_limit_bytes=VMEM_LIMIT),
        cost_estimate=pl.CostEstimate(
            flops=2 * d * lanes * 1024, bytes_accessed=4 * d * lanes, transcendentals=0
        ),
        name="grads",
    )(me, *operands)


def line_kernel(count, place_ref, *refs):
    terms, outs, scratch = refs[:-count - 1], refs[-count - 1 : -1], refs[-1]
    scratch[...] = functools.reduce(jnp.add, [t[...].astype(F32) for t in terms])
    shard = outs[0].shape[0]
    for s in range(count):
        row = pl.multiple_of((place_ref[0] ^ s) * shard, shard)
        outs[s][...] = scratch[pl.ds(row, shard)].astype(BF)


def line_call(me, terms, count):
    rows, lanes = terms[0].shape
    whole = pl.BlockSpec(memory_space=pltpu.VMEM)
    return pl.pallas_call(
        functools.partial(line_kernel, count),
        in_specs=[pl.BlockSpec(memory_space=pltpu.SMEM)] + [whole] * len(terms),
        out_specs=[whole] * count,
        out_shape=[jax.ShapeDtypeStruct((rows // count, lanes), BF)] * count,
        scratch_shapes=[pltpu.VMEM((rows, lanes), F32)],
        compiler_params=pltpu.CompilerParams(vmem_limit_bytes=VMEM_LIMIT),
        name="line",
    )(me, *terms)


def reorder_heads(values):
    parts = []
    for at in range(0, values.shape[1], 256):
        a = values[:, at : at + 128]
        b = values[:, at + 128 : at + 256]
        low = lax.broadcasted_iota(jnp.int32, a.shape, 1) < HD
        parts += [
            jnp.where(low, a, pltpu.roll(b, HD, 1)),
            jnp.where(low, pltpu.roll(a, HD, 1), b),
        ]
    return jnp.concatenate(parts, axis=1)


def finish_kernel(count, *refs):
    early = functools.reduce(jnp.add, [r[...].astype(F32) for r in refs[:count]])
    late = functools.reduce(jnp.add, [r[...].astype(F32) for r in refs[count : 2 * count]])
    q_ref, k_ref, v_ref, o_ref, small_ref = refs[2 * count :]
    qw = q_ref.shape[1]
    kw = k_ref.shape[1]
    q_ref[...] = reorder_heads(early[:, :qw])
    o_ref[...] = reorder_heads(early[:, qw:])
    k_ref[...] = late[:, :kw]
    v_ref[...] = late[:, kw : 2 * kw]
    small_ref[...] = late[:, 2 * kw :]


def finish_call(early, late, qw, kw):
    shard = early[0].shape[0]
    whole = pl.BlockSpec(memory_space=pltpu.VMEM)
    return pl.pallas_call(
        functools.partial(finish_kernel, len(early)),
        in_specs=[whole] * (2 * len(early)),
        out_specs=[whole] * 5,
        out_shape=[
            jax.ShapeDtypeStruct((shard, w), F32) for w in (qw, kw, kw, qw, 128)
        ],
        name="finish",
    )(*early, *late)


def expert_rows_kernel(count, place_ref, *refs):
    pieces, outs = refs[:-3], refs[-3:]
    groups = 2
    units = outs[0].shape[2]
    group = outs[0].shape[0] // (count * groups)
    for g in range(groups):
        for s in range(count):
            piece = pieces[g * count + s]
            at = ((place_ref[0] ^ s) * groups + g) * group
            for i in range(3):
                for e in range(group):
                    lanes = (i * group + e) * units
                    outs[i][at + e] = piece[:, lanes : lanes + units].astype(F32)


def expert_rows_call(me, pieces, experts, units):
    shard = pieces[0].shape[0]
    whole = pl.BlockSpec(memory_space=pltpu.VMEM)
    return pl.pallas_call(
        functools.partial(expert_rows_kernel, len(pieces) // 2),
        in_specs=[pl.BlockSpec(memory_space=pltpu.SMEM)] + [whole] * len(pieces),
        out_specs=[whole] * 3,
        out_shape=[jax.ShapeDtypeStruct((experts, shard, units), F32)] * 3,
        compiler_params=pltpu.CompilerParams(vmem_limit_bytes=VMEM_LIMIT),
        name="expert_rows",
    )(me, *pieces)


def apart(count, step):
    return [(i, i ^ step) for i in range(count)]


def swap(value):
    return lax.ppermute(value, "mp", [(0, 1), (1, 0)])


def up_hop(value, n, s):
    return lax.ppermute(value, "ctx", [(c, c + 1) for c in range(s, n - 1)])


def add(*terms):
    return functools.reduce(jnp.add, [t.astype(F32) for t in terms]).astype(BF)


def by_xor(parts, me):
    bit = 1
    while bit < len(parts):
        flip = (me & bit) != 0
        parts = [jnp.where(flip, parts[i ^ bit], parts[i]) for i in range(len(parts))]
        bit *= 2
    return parts


def exchange(parts, axis):
    count = len(parts)
    return [parts[0]] + [
        lax.ppermute(parts[s], axis, apart(count, s)) for s in range(1, count)
    ]


def from_last(values, start, count):
    values = values[::-1]
    return lax.dynamic_slice_in_dim(jnp.concatenate([values, values]), start, count, 0)


def head_order(weight):
    rows, width = weight.shape
    return (
        weight.reshape(rows, width // (4 * HD), 2, 2, HD).swapaxes(2, 3).reshape(rows, width)
    )


def per_device(
    tokens,
    cotangent,
    routes,
    norm_gain,
    w_query,
    w_key,
    w_value,
    w_output,
    ffn_gain,
    w_router,
    w_gate,
    w_up,
    w_down,
):
    micro, seq_count, local, width = tokens.shape
    top = routes.shape[3]
    experts, shard, units = w_gate.shape
    dp = lax.axis_size("dp")
    n = lax.axis_size("ctx")
    hops = n == 4
    me_dp = lax.axis_index("dp")
    me_ctx = lax.axis_index("ctx")
    me_mp = lax.axis_index("mp")
    mine_count = experts // dp
    group = mine_count // 2
    micros = range(micro)
    per = seq_count * local
    half = per // 2
    rows = micro * per
    qw = w_query.shape[1]
    kw = w_key.shape[1]
    ctx_now = me_ctx.astype(jnp.int32).reshape(1)
    dp_now = me_dp.astype(jnp.int32).reshape(1)
    place = jnp.stack([me_dp * mine_count, me_ctx]).astype(jnp.int32)

    def in_order(mine, other):
        first = me_mp == 0
        return jnp.concatenate([jnp.where(first, mine, other), jnp.where(first, other, mine)])

    def halves(full):
        cut = full.reshape(2, half, full.shape[1])
        mine = lax.dynamic_index_in_dim(cut, me_mp, 0, keepdims=False)
        return mine, lax.dynamic_index_in_dim(cut, 1 - me_mp, 0, keepdims=False)

    def far_pieces(mine, steps=range(1, dp)):
        return [lax.ppermute(mine, "dp", apart(dp, s)) for s in steps]

    def paired(mine, far, other, near):
        return [piece for pair in zip([mine] + far, [other] + near) for piece in pair]

    def gather_line(value):
        return jnp.stack(
            [value] + [lax.ppermute(value, "ctx", apart(n, s)) for s in range(1, n)]
        )

    def gather_plane(value):
        return [value] + [lax.ppermute(value, "dp", apart(dp, s)) for s in range(1, dp)]

    def whole_rows(pieces):
        lines = by_xor(pieces, me_dp)
        full = jnp.stack(lines)
        cols = by_xor([full[:, i] for i in range(n)], me_ctx)
        return jnp.stack(cols, axis=1).reshape(dp * n * shard, full.shape[3])

    live = {}

    def seal(**values):
        live.update(values)
        live.update(lax.optimization_barrier(live))

    small = jnp.concatenate([w_router, norm_gain[:, None], ffn_gain[:, None]], axis=1)
    small = jnp.pad(small, ((0, 0), (0, 128 - small.shape[1])))
    kv_shard = jnp.concatenate([w_key, w_value, small], axis=1)
    qo_shard = jnp.concatenate([head_order(w_query), head_order(w_output)], axis=1)
    side = lambda w: w.reshape(dp, 2, group, shard, units)
    w3 = jnp.concatenate(
        [side(w)[:, :, e] for w in (w_gate, w_up, w_down) for e in range(group)], axis=3
    )
    if hops:
        kv_line = gather_line(kv_shard)
        qo_line = gather_line(qo_shard)
    w3_parts = exchange(by_xor([w3[i] for i in range(dp)], me_dp), "dp")
    own3 = by_xor(w3_parts, me_dp)
    own3 = [jnp.stack([o[g] for o in own3]) for g in range(2)]
    def weight_send(g, *steps):
        if hops:
            for s in steps:
                at, hop = (2, 1) if s == 3 else (0, s)
                live["weights"][g][s] = lax.ppermute(live["weights"][g][at], "ctx", apart(n, hop))

    def seal_but(under_way, **values):
        kept = [(d, {k: d.pop(k) for k in keys if k in d}) for d, keys in under_way()]
        seal(**values)
        for (d, keys), (_, taken) in zip(under_way(), kept):
            d.update(taken)

    if hops:
        own3 = [{0: o} for o in own3]
        seal(kv_line=kv_line, qo_line=qo_line, weights=own3, x=tokens, dy=cotangent, routes=routes)
        kv_pieces = gather_plane(live.pop("kv_line"))
        weight_send(0, 1)
        seal(kv_pieces=kv_pieces)
        kv_full = whole_rows(live.pop("kv_pieces"))
        qo_pieces = gather_plane(live.pop("qo_line"))
    else:
        kv_full = lax.all_gather(kv_shard, ("dp", "ctx"), axis=0, tiled=True)
        qo_full = lax.all_gather(qo_shard, ("dp", "ctx"), axis=0, tiled=True)
        own3 = [lax.all_gather(o, "ctx", axis=1, tiled=False) for o in own3]
        own3 = [{0: o.reshape(width, o.shape[-1])} for o in own3]
        seal(weights=own3, x=tokens, dy=cotangent, routes=routes)
    small = kv_full[:, 2 * kw :]
    router = small[:, :experts]
    router_wide = jnp.pad(router, ((0, 0), (0, 128 - experts)))
    gain_one = small[:, experts].astype(F32)[None, :]
    gain_two = small[:, experts + 1].astype(F32)[None, :]

    position = me_ctx * local + jnp.arange(local, dtype=jnp.int32)
    freqs = THETA ** (-(jnp.arange(HD // 2, dtype=F32) * 2.0) / HD)
    angles = position.astype(F32)[:, None] * freqs[None, :]
    cosine = jnp.tile(jnp.cos(angles), (1, 4))
    sine = jnp.sin(angles)
    sine = jnp.concatenate([-sine, sine, -sine, sine], axis=1)
    live["x"] = live["x"].reshape(rows, width)
    live["dy"] = live["dy"].reshape(rows, width)
    normed, kv = kv_call(live["x"], gain_one, kv_full, 2 * kw, cosine, sine)
    kv = kv.reshape(1, micro * seq_count, local, 2 * kw)

    ids = live.pop("routes").reshape(rows, top)
    marks = jnp.sum(
        (ids[:, :, None] == jnp.arange(128, dtype=jnp.int32)[None, None, :]).astype(F32), axis=1
    ).astype(BF)
    dyx = jnp.concatenate([live["dy"], marks], axis=1)
    dyx = dyx.reshape(micro, 2, half, width + 128)
    dy_cut = [
        lax.dynamic_index_in_dim(dyx, at, 1, keepdims=False) for at in (me_mp, 1 - me_mp)
    ]

    if hops:
        kv_got = up_hop(kv, n, 0)
        seal(
            kv=kv,
            kv_prev=[kv_got],
            qo_pieces=qo_pieces,
            normed=normed,
            dy_cut=dy_cut,
            marks=marks[:, :experts],
            kv_full=kv_full,
            cosine=cosine,
            sine=sine,
            router=router,
            router_wide=router_wide,
            gain_one=gain_one,
            gain_two=gain_two,
        )
        qo_full = whole_rows(live.pop("qo_pieces"))
    else:
        every = lax.all_gather(kv[0], "ctx", axis=0, tiled=False)
        seal(
            kv=kv,
            kv_prev=[from_last(every, n - me_ctx, n - 1)],
            normed=normed,
            dy_cut=dy_cut,
            marks=marks[:, :experts],
            kv_full=kv_full,
            cosine=cosine,
            sine=sine,
            router=router,
            router_wide=router_wide,
            gain_one=gain_one,
            gain_two=gain_two,
        )
    live.update(qo_full=qo_full, dy_far=[], dy_near=[])
    q = q_call(live["normed"], qo_full, qw, live["cosine"], live["sine"])
    live["q"] = q.reshape(micro * seq_count, local, qw)

    def dy_send(steps):
        for s in steps:
            live["dy_far"].append(lax.ppermute(live["dy_cut"][0], "dp", apart(dp, s)))

    def attend(first, s, done):
        return attn_part(
            ctx_now,
            live["q"],
            live["kv"] if first else None,
            [live["kv_prev"][s - 1]],
            s,
            None if first else live.pop("carry"),
            done,
        )

    def mix(attn):
        return dot(attn.reshape(rows, qw), live["qo_full"][:, qw:], 1, 1).astype(BF)

    if hops:
        dy_send((1, 2))
        got = up_hop(live["kv_prev"][-1], n, 1)
        carry = attend(True, 1, False)
        live["kv_prev"].append(got)
        seal(carry=carry)
        dy_send((3,))
        got = up_hop(live["kv_prev"][-1], n, 2)
        carry = attend(False, 2, False)
        live["kv_prev"].append(got)
        seal(carry=carry)
        weight_send(0, 2)
        attn, lse = attend(False, 3, True)
    else:
        attn, lse = attend(True, 1, True)
        dy_send(range(1, dp))
    live["dy_near"] = [swap(f) for f in live["dy_far"]]
    late = lambda: [(live["weights"][0], [2])]
    seal_but(late, attn=attn, lse=lse, mixed=mix(attn))

    mixed_got = swap(live["mixed"])
    hidden = live["x"].astype(F32) + (live.pop("mixed").astype(F32) + mixed_got.astype(F32))
    inv_two = lax.rsqrt(jnp.mean(hidden * hidden, axis=1, keepdims=True) + EPS)
    ffn_low = (hidden * inv_two * live["gain_two"]).astype(BF)
    x_cut = [halves(ffn_low[m * per : (m + 1) * per]) for m in micros]

    seal_but(late, hidden=hidden, inv_two=inv_two, ffn_low=ffn_low, x_cut=x_cut)
    first = far_pieces(live["x_cut"][0][0], (1, 2))
    live["x_far"] = [first] + [[]] * (micro - 1)
    seal()
    live["x_far"][0] = live["x_far"][0] + far_pieces(live["x_cut"][0][0], (3,))
    weight_send(0, 3)
    seal()
    live["x_near"] = [[swap(f) for f in live["x_far"][0]]] + [[]] * (micro - 1)
    seal()
    live.update(sums=[], dws=[[], []], parts=[])

    def run(g, m, before):
        weights = [live["weights"][g][s] for s in sorted(live["weights"][g])]
        x_cut, dy_cut = live["x_cut"][m], live["dy_cut"]
        xs = paired(x_cut[0], live["x_far"][m], x_cut[1], live["x_near"][m])
        dys = paired(dy_cut[0], live["dy_far"], dy_cut[1], live["dy_near"])
        part = experts_call(
            xs,
            dys,
            m,
            place,
            live["router_wide"],
            weights,
            g * group,
            group,
            before,
            live["dws"][g],
        )
        live["dws"][g] = part[4:]
        return list(part[:4])

    live["x_far"][1] = far_pieces(live["x_cut"][1][0])
    weight_send(1, 1, 2)
    live["sums"].append(run(0, 0, None))
    seal()
    live["x_near"][1] = [swap(f) for f in live["x_far"][1]]
    seal()
    weight_send(1, 3)
    live["sums"].append(run(0, 1, None))
    seal()

    live.update(rows=[{}, {}])

    def grad_send(g, *steps):
        if hops:
            for s in steps:
                live["rows"][g][s] = lax.ppermute(live["dws"][g][s], "ctx", apart(n, s))

    def grad_own(g):
        if hops:
            own = add(live["dws"][g][0], *live["rows"][g].values())
        else:
            whole = live["dws"][g][0].reshape(dp, n, shard, -1)
            own = lax.psum_scatter(whole, "ctx", scatter_dimension=1, tiled=False)
        return exchange(by_xor([own[i] for i in range(dp)], me_dp), "dp")

    def terms_of(mine, got):
        return [add(mine[s], got[s]) for s in range(dp)]

    live.update(dx_terms=[None] * micro, dx_back=[None] * micro)
    live.update(out_terms=[None] * micro, out_back={})

    def dx_terms(m):
        part = live["parts"][m]
        live["dx_terms"][m] = terms_of(part[2], swap(part[3]))

    def dx_send(m):
        live["dx_back"][m] = exchange(live["dx_terms"][m], "dp")

    def out_terms(m):
        part = live["parts"][m]
        live["out_terms"][m] = terms_of(part[0], swap(part[1]))

    def out_send(m):
        live["out_back"][m] = exchange(live["out_terms"][m], "dp")

    grad_send(0, 1, 2)
    live["parts"].append(run(1, 0, live["sums"][0]))
    seal()
    dx_terms(0)
    seal()
    dx_send(0)
    grad_send(0, 3)
    live["parts"].append(run(1, 1, live.pop("sums")[1]))
    seal()

    cut = lambda whole, m: whole[m * per : (m + 1) * per]
    live.update({name: [None] * micro for name in ("dh", "dz", "d_attn", "dq", "dkv")})
    live.update(dkv_sum=[{} for _ in micros])
    live.update(router_sums=[None] * micro, gain_sums=[None] * micro)

    def before_attention(m):
        total = add(*live["dx_back"][m])
        moe = in_order(total, swap(total)).astype(F32)
        low = cut(live["ffn_low"], m)
        inv = cut(live["inv_two"], m)
        dgate = moe[:, width : width + experts]
        gate = masked_softmax(
            dot(low, live["router"], 1, 0), cut(live["marks"], m).astype(F32) > 0.5
        )
        dlogit = gate * (dgate - jnp.sum(gate * dgate, axis=1, keepdims=True))
        dlogit = dlogit.astype(BF)
        live["router_sums"][m] = dot(low, dlogit, 0, 0)
        d_ffn = moe[:, :width] + dot(dlogit, live["router"], 1, 1)
        unit = cut(live["hidden"], m) * inv
        live["gain_sums"][m] = jnp.sum(d_ffn * unit, axis=0)
        g_two = d_ffn * live["gain_two"]
        dh = cut(live["dy"], m).astype(F32) + inv * (
            g_two - unit * jnp.mean(g_two * unit, axis=1, keepdims=True)
        )
        dz = dh.astype(BF)
        live["dh"][m] = dh
        live["dz"][m] = dz
        live["d_attn"][m] = dot(dz, live["qo_full"][:, qw:], 1, 0).astype(BF)

    def attention_back(m):
        dq, *dkv = attn_bwd(
            ctx_now,
            live["q"],
            live["d_attn"][m].reshape(seq_count, local, qw),
            live["attn"],
            live["lse"],
            live["cosine"],
            live["sine"],
            live["kv"],
            live["kv_prev"],
            m * seq_count,
        )
        live["dq"][m] = dq.reshape(per, qw)
        live["dkv"][m] = dkv

    def dkv_send(m, *steps):
        if hops:
            for d in steps:
                live["dkv_sum"][m][d] = lax.ppermute(
                    live["dkv"][m][d], "ctx", [(c, c - d) for c in range(d, n)]
                )

    def back(m):
        if hops:
            terms = [live["dkv"][m][0], *live["dkv_sum"][m].values()]
        else:
            every = from_last(jnp.concatenate(live["dkv"][m]), n - 1 - me_ctx, n)
            terms = [lax.psum_scatter(every, "ctx", scatter_dimension=0, tiled=True)]
        terms = [t.reshape(per, 2 * kw) for t in terms]
        return back_call(
            live["dq"][m],
            terms,
            live["x"],
            m,
            live["cosine"],
            live["sine"],
            live["qo_full"],
            live["kv_full"],
        )

    def out_total(m):
        total = add(*live["out_back"][m])
        moe = in_order(total, swap(total)).astype(F32)
        return (cut(live["hidden"], m) + moe).astype(BF)

    def early_send(*steps):
        if hops:
            for s in steps:
                live["early"][s] = lax.ppermute(live["early"][s], "dp", apart(dp, s))

    before_attention(0)
    dx_terms(1)
    grad_send(1, 1, 2)
    out_terms(0)
    seal_but(lambda: [(live["rows"][1], [1, 2])])
    dx_send(1)
    attention_back(0)
    seal()
    dkv_send(0, 1, 2, 3)
    out_send(0)
    before_attention(1)
    out_terms(1)
    seal_but(lambda: [(live["dkv_sum"][0], [1, 2, 3]), (live["out_back"], [0])])
    out_send(1)
    attention_back(1)
    seal()
    dkv_send(1, 1, 2, 3)
    pieces_now = dp_now if hops else jnp.zeros((1,), jnp.int32)
    early = grads_call(
        pieces_now,
        [
            [(live["normed"], live["dq"][m], m * per) for m in micros],
            [(jnp.concatenate(live["dz"]), live["attn"].reshape(rows, qw), 0)],
        ],
        None,
        dp,
    )
    seal_but(lambda: [(live["dkv_sum"][1], [1, 2, 3])], early=list(early))
    early_send(1, 2, 3)
    owned = [grad_own(0)]
    dkv_first, part_first, gain_first = back(0)
    got_first = swap(part_first)
    out_first = out_total(0)
    out_last = out_total(1)
    seal(
        got=[got_first],
        output=[out_first, out_last],
        owned=owned,
        dkv_final=[dkv_first],
        part=[part_first],
        gain_one_sums=[gain_first],
    )
    grad_send(1, 3)
    dkv_last, part_last, gain_last = back(1)
    live["dkv_final"].append(dkv_last)
    live["part"].append(part_last)
    small = jnp.concatenate(
        [
            live["router_sums"][0] + live["router_sums"][1],
            (live["gain_one_sums"][0] + gain_last)[0][:, None],
            (live["gain_sums"][0] + live["gain_sums"][1])[:, None],
        ],
        axis=1,
    )
    small = jnp.pad(small, ((0, 0), (0, 128 - small.shape[1]))).astype(BF)
    late = grads_call(
        pieces_now,
        [[(live["normed"], live["dkv_final"][m], m * per) for m in micros]],
        small,
        dp,
    )
    got_last = swap(part_last)
    early = live["early"]
    if hops:
        early = line_call(ctx_now, early, n)
    seal_but(
        lambda: [(live["rows"][1], [3])], late=late, early=early, got=live["got"] + [got_last]
    )
    late = live["late"]
    if hops:
        late = exchange(late, "dp")
    d_normed = jnp.concatenate(
        [p.astype(F32) + g.astype(F32) for p, g in zip(live["part"], live["got"])]
    )
    x32 = live["x"].astype(F32)
    inv_one = lax.rsqrt(jnp.mean(x32 * x32, axis=1, keepdims=True) + EPS)
    n_one = x32 * inv_one
    g_one = d_normed * live["gain_one"]
    input_grad = (
        jnp.concatenate(live["dh"])
        + inv_one * (g_one - n_one * jnp.mean(g_one * n_one, axis=1, keepdims=True))
    ).astype(BF)
    seal_but(lambda: [(live["rows"][1], [3])], late=late, input_grad=input_grad)
    early, late = live["early"], live["late"]
    if hops:
        late = exchange(line_call(ctx_now, late, n), "ctx")
        early = exchange(early, "ctx")
    else:
        early, late = (
            [
                lax.psum_scatter(
                    jnp.concatenate(p), ("dp", "ctx"), scatter_dimension=0, tiled=True
                )
            ]
            for p in (early, late)
        )
    owned = [live["owned"][0], grad_own(1)]
    output = jnp.concatenate(live["output"])
    grad_q, grad_k, grad_v, grad_o, small_grad = finish_call(early, late, qw, kw)
    gain_part = small_grad[:, experts]
    dw_gate, dw_up, dw_down = expert_rows_call(dp_now, owned[0] + owned[1], experts, units)
    shape = tokens.shape
    return (
        output.reshape(shape),
        live["input_grad"].reshape(shape),
        gain_part + swap(gain_part),
        grad_q,
        grad_k,
        grad_v,
        grad_o,
        small_grad[:, experts + 1],
        small_grad[:, :experts],
        dw_gate,
        dw_up,
        dw_down,
    )


def solution(mesh):
    rows = P(None, "dp", "ctx", None)
    vector = P(("dp", "ctx"))
    matrix = P(("dp", "ctx"), "mp")
    router = P(("dp", "ctx"), None)
    expert = P(None, ("dp", "ctx"), "mp")
    return jax.shard_map(
        per_device,
        mesh=mesh,
        in_specs=(
            rows,
            rows,
            rows,
            vector,
            matrix,
            matrix,
            matrix,
            matrix,
            vector,
            router,
            expert,
            expert,
            expert,
        ),
        out_specs=(
            rows,
            rows,
            vector,
            matrix,
            matrix,
            matrix,
            matrix,
            vector,
            router,
            expert,
            expert,
            expert,
        ),
        check_vma=False,
    )
```

```python
import functools
import math

import jax
import jax.numpy as jnp
from jax import lax
from jax.experimental import pallas as pl
from jax.experimental.pallas import tpu as pltpu
from jax.sharding import PartitionSpec as P

HD = 64
EPS = 1e-06
THETA = 10000.0
NEG = -1e30
VMEM_LIMIT = 60 * 1024 * 1024
BF = jnp.bfloat16
F32 = jnp.float32


def dot(a, b, ca, cb, precision=None):
    return lax.dot_general(
        a, b, (((ca,), (cb,)), ((), ())), preferred_element_type=F32, precision=precision
    )


def params(*semantics):
    return pltpu.CompilerParams(dimension_semantics=semantics, vmem_limit_bytes=VMEM_LIMIT)


def turn(values, cosine, sine):
    width = values.shape[1]
    lane = lax.broadcasted_iota(jnp.int32, values.shape, 1)
    ahead = pltpu.roll(values, width - HD // 2, 1)
    behind = pltpu.roll(values, HD // 2, 1)
    swapped = jnp.where(lane % HD < HD // 2, ahead, behind)
    reps = width // cosine.shape[1]
    return values * jnp.tile(cosine, (1, reps)) + swapped * jnp.tile(sine, (1, reps))


def kv_kernel(x_ref, gain_ref, w_ref, cos_ref, sin_ref, normed_ref, kv_ref):
    x = x_ref[...].astype(F32)
    inv = lax.rsqrt(jnp.mean(x * x, axis=1, keepdims=True) + EPS)
    normed = (x * inv * gain_ref[...]).astype(BF)
    normed_ref[...] = normed
    kw = kv_ref.shape[1] // 2
    raw = dot(normed, w_ref[...], 1, 0)
    kv_ref[:, :kw] = turn(raw[:, :kw], cos_ref[...], sin_ref[...]).astype(BF)
    kv_ref[:, kw:] = raw[:, kw:].astype(BF)


def q_kernel(normed_ref, w_ref, cos_ref, sin_ref, q_ref):
    raw = dot(normed_ref[...], w_ref[...], 1, 0)
    q_ref[...] = turn(raw, cos_ref[...], sin_ref[...]).astype(BF)


def row_specs(rows, local, d, lanes):
    tile = min(256, local)
    per = local // tile
    return (
        rows // tile,
        pl.BlockSpec((tile, d), lambda i: (i, 0)),
        pl.BlockSpec((d, lanes), lambda i: (0, 0)),
        pl.BlockSpec((tile, 128), lambda i: (i % per, 0)),
        pl.BlockSpec((tile, lanes), lambda i: (i, 0)),
        pl.CostEstimate(
            flops=2 * rows * d * lanes, bytes_accessed=6 * rows * d, transcendentals=rows
        ),
    )


def kv_call(x, gain, w, lanes, cosine, sine):
    rows, d = x.shape
    steps, row, weight, table, out, cost = row_specs(rows, cosine.shape[0], d, lanes)
    return pl.pallas_call(
        kv_kernel,
        grid=(steps,),
        in_specs=[row, pl.BlockSpec((1, d), lambda i: (0, 0)), weight, table, table],
        out_specs=[row, out],
        out_shape=[
            jax.ShapeDtypeStruct((rows, d), BF),
            jax.ShapeDtypeStruct((rows, lanes), BF),
        ],
        compiler_params=params("arbitrary"),
        cost_estimate=cost,
        name="kv",
    )(x, gain, w, cosine, sine)


def q_call(normed, w, lanes, cosine, sine):
    rows, d = normed.shape
    steps, row, weight, table, out, cost = row_specs(rows, cosine.shape[0], d, lanes)
    return pl.pallas_call(
        q_kernel,
        grid=(steps,),
        in_specs=[row, weight, table, table],
        out_specs=out,
        out_shape=jax.ShapeDtypeStruct((rows, lanes), BF),
        compiler_params=params("arbitrary"),
        cost_estimate=cost,
        name="q",
    )(normed, w, cosine, sine)


def half_mask(block, which):
    lane = lax.broadcasted_iota(jnp.int32, block.shape, 1)
    keep = (lane < HD) if which == 0 else (lane >= HD)
    return jnp.where(keep, block, jnp.zeros_like(block))


def stacked(ref):
    return jnp.concatenate([ref[0, :, :128], ref[0, :, 128:]], axis=0)


def causal(shape, length):
    key = lax.broadcasted_iota(jnp.int32, shape, 0)
    query = lax.broadcasted_iota(jnp.int32, shape, 1) % length
    return key <= query


def each_earlier(c, counts, visit, otherwise=None, first=1):
    for piece, count in enumerate(counts):
        if count == 1:

            @pl.when(c >= first)
            def _():
                visit(piece, 0)

            if otherwise is not None:

                @pl.when(c < first)
                def _():
                    otherwise(piece, 0)

        else:
            reach = jnp.clip(c - first + 1, 0, count)

            @pl.loop(0, reach)
            def _(entry):
                visit(piece, entry)

            if otherwise is not None:

                @pl.loop(reach, count)
                def _(entry):
                    otherwise(piece, entry)

        first += count


def attn_part_kernel(counts, start, first, last, ctx_ref, q_ref, *refs):
    refs = list(refs)
    pieces = len(counts) + first
    keys = [refs.pop(0) for _ in range(pieces)]
    vals = [refs.pop(0) for _ in range(pieces)]
    old = None if first else [refs.pop(0) for _ in range(2)]
    if last:
        o_ref, lse_ref, stats_ref, acc_ref = refs
    else:
        stats_ref, acc_ref = (ref.at[0, 0] for ref in refs)
    length = q_ref.shape[1]
    both = (stacked(q_ref).astype(F32) * HD**-0.5).astype(BF)
    c = ctx_ref[0]

    if first:
        k = keys[0][0, 0]
        v = vals[0][0, 0]
        for i in range(2):
            s = dot(half_mask(k, i), both, 1, 1)
            s = jnp.where(causal(s.shape, length), s, NEG)
            peak = jnp.max(s, axis=0, keepdims=True)
            p = jnp.exp(s - peak)
            stats_ref[i : i + 1] = peak
            stats_ref[i + 2 : i + 3] = jnp.sum(p, axis=0, keepdims=True)
            acc_ref[i] = dot(v, p.astype(BF), 0, 0)
    else:
        stats_ref[...] = old[0][0, 0]
        acc_ref[...] = old[1][0, 0]

    def visit(piece, entry):
        k = keys[piece + first][entry, 0]
        v = vals[piece + first][entry, 0]
        for i in range(2):
            s = dot(half_mask(k, i), both, 1, 1)
            peak = stats_ref[i : i + 1]
            now = jnp.maximum(peak, jnp.max(s, axis=0, keepdims=True))
            p = jnp.exp(s - now)
            factor = jnp.exp(peak - now)
            stats_ref[i : i + 1] = now
            stats_ref[i + 2 : i + 3] = stats_ref[i + 2 : i + 3] * factor + jnp.sum(
                p, axis=0, keepdims=True
            )
            acc_ref[i] = acc_ref[i] * factor + dot(v, p.astype(BF), 0, 0)

    each_earlier(c, counts, visit, None, start)
    if last:
        row = lax.broadcasted_iota(jnp.int32, acc_ref.shape[1:], 0)
        stats = stats_ref[...]
        out = jnp.where(row < HD, acc_ref[0] / stats[2:3], acc_ref[1] / stats[3:4]).T
        o_ref[0, :, :128] = out[:length].astype(BF)
        o_ref[0, :, 128:] = out[length:].astype(BF)
        lse_ref[0, 0] = stats[:2] + jnp.log(stats[2:])


def kv_specs(pieces, length, lanes, at=0):
    kb = lanes // 256
    keys = [
        pl.BlockSpec((a.shape[0], 1, length, 128), lambda s, p: (0, s + at, 0, p)) for a in pieces
    ]
    vals = [
        pl.BlockSpec((a.shape[0], 1, length, 128), lambda s, p: (0, s + at, 0, kb + p))
        for a in pieces
    ]
    return keys + vals


def attn_part(ctx, q, own, prev, start, carry, last):
    seqs, length, qw = q.shape
    pairs = qw // 256
    cols = 2 * length
    first = own is not None
    pieces = ([own] if first else []) + prev
    counts = tuple(a.shape[0] for a in prev)
    spans = first + sum(counts)
    state = [
        pl.BlockSpec((1, 1, 4, cols), lambda s, p: (s, p, 0, 0)),
        pl.BlockSpec((1, 1, 2, 128, cols), lambda s, p: (s, p, 0, 0, 0)),
    ]
    if last:
        out_specs = [
            pl.BlockSpec((1, length, 256), lambda s, p: (s, 0, p)),
            pl.BlockSpec((1, 1, 2, cols), lambda s, p: (s, p, 0, 0)),
        ]
        out_shape = [
            jax.ShapeDtypeStruct((seqs, length, qw), BF),
            jax.ShapeDtypeStruct((seqs, pairs, 2, cols), F32),
        ]
        scratch = [pltpu.VMEM((4, cols), F32), pltpu.VMEM((2, 128, cols), F32)]
    else:
        out_specs = state
        out_shape = [
            jax.ShapeDtypeStruct((seqs, pairs, 4, cols), F32),
            jax.ShapeDtypeStruct((seqs, pairs, 2, 128, cols), F32),
        ]
        scratch = []
    return pl.pallas_call(
        functools.partial(attn_part_kernel, counts, start, first, last),
        grid=(seqs, pairs),
        in_specs=[
            pl.BlockSpec(memory_space=pltpu.SMEM),
            pl.BlockSpec((1, length, 256), lambda s, p: (s, 0, p)),
        ]
        + kv_specs(pieces, length, pieces[0].shape[3])
        + ([] if first else state),
        out_specs=out_specs,
        out_shape=out_shape,
        scratch_shapes=scratch,
        compiler_params=params("arbitrary", "arbitrary"),
        cost_estimate=pl.CostEstimate(
            flops=16 * seqs * length * length * spans * qw,
            bytes_accessed=4 * seqs * length * spans * qw,
            transcendentals=seqs * length * length * spans * qw // 64,
        ),
        name="attn_fwd",
    )(ctx, q, *pieces, *pieces, *(carry or []))


def attn_bwd_kernel(counts, ctx_ref, q_ref, do_ref, o_ref, lse_ref, cos_ref, sin_ref, *refs):
    pieces = len(counts)
    keys = refs[: pieces + 1]
    vals = refs[pieces + 1 : 2 * pieces + 2]
    dq_ref = refs[2 * pieces + 2]
    outs = refs[2 * pieces + 3 : 3 * pieces + 4]
    acc_ref = refs[3 * pieces + 4]
    length = q_ref.shape[1]
    lanes = outs[0].shape[3]
    pair = pl.program_id(1)
    both = (stacked(q_ref).astype(F32) * HD**-0.5).astype(BF)
    dboth = stacked(do_ref)
    prod = dboth.astype(F32) * stacked(o_ref).astype(F32)
    pick_row = lax.broadcasted_iota(jnp.int32, (8, 128), 0)
    pick_lane = lax.broadcasted_iota(jnp.int32, (8, 128), 1) // HD
    picks = (pick_row == pick_lane).astype(F32)
    delta = dot(picks, prod, 1, 1, lax.Precision.HIGHEST)
    c = ctx_ref[0]
    k_at = pl.ds(pl.multiple_of(pair * 128, 128), 128)
    v_at = pl.ds(pl.multiple_of(lanes // 2 + pair * 128, 128), 128)

    def block(piece, entry, diagonal):
        k = keys[piece][entry, 0]
        v = vals[piece][entry, 0]
        parts = []
        dq = None
        for i in range(2):
            ki = half_mask(k, i)
            s = dot(ki, both, 1, 1)
            p = jnp.exp(s - lse_ref[0, 0, i : i + 1, :])
            if diagonal:
                p = jnp.where(causal(s.shape, length), p, 0.0)
            dp = dot(half_mask(v, i), dboth, 1, 1)
            ds = (p * (dp - delta[i : i + 1, :])).astype(BF)
            parts.append((dot(ds, both, 1, 0), dot(p.astype(BF), dboth, 1, 0)))
            part = dot(ki, ds, 0, 0)
            dq = part if dq is None else dq + part
        low = lax.broadcasted_iota(jnp.int32, (length, 128), 1) < HD
        outs[piece][entry, 0, :, k_at] = jnp.where(low, parts[0][0], parts[1][0]).astype(BF)
        outs[piece][entry, 0, :, v_at] = jnp.where(low, parts[0][1], parts[1][1]).astype(BF)
        return dq

    acc_ref[...] = block(0, 0, True)

    def visit(piece, entry):
        acc_ref[...] += block(piece + 1, entry, False)

    def clear(piece, entry):
        outs[piece + 1][entry, 0, :, k_at] = jnp.zeros((length, 128), BF)
        outs[piece + 1][entry, 0, :, v_at] = jnp.zeros((length, 128), BF)

    each_earlier(c, counts, visit, clear)
    out = acc_ref[...].T * HD**-0.5
    cosine = cos_ref[...]
    sine = -sin_ref[...]
    dq_ref[0, :, :128] = turn(out[:length], cosine, sine).astype(BF)
    dq_ref[0, :, 128:] = turn(out[length:], cosine, sine).astype(BF)


def attn_bwd(ctx, q, do, o, lse, cosine, sine, own, prev, at):
    seqs, length, qw = do.shape
    pairs = qw // 256
    pieces = [own] + prev
    counts = tuple(a.shape[0] for a in prev)
    spans = 1 + sum(counts)
    blk = pl.BlockSpec((1, length, 256), lambda s, p: (s, 0, p))
    blk_at = pl.BlockSpec((1, length, 256), lambda s, p: (s + at, 0, p))
    tab = pl.BlockSpec((length, 128), lambda s, p: (0, 0))
    return pl.pallas_call(
        functools.partial(attn_bwd_kernel, counts),
        grid=(seqs, pairs),
        in_specs=[
            pl.BlockSpec(memory_space=pltpu.SMEM),
            blk_at,
            blk,
            blk_at,
            pl.BlockSpec((1, 1, 2, 2 * length), lambda s, p: (s + at, p, 0, 0)),
            tab,
            tab,
        ]
        + kv_specs(pieces, length, own.shape[3], at),
        out_specs=[blk]
        + [
            pl.BlockSpec((a.shape[0], 1) + a.shape[2:], lambda s, p: (0, s, 0, 0)) for a in pieces
        ],
        out_shape=[jax.ShapeDtypeStruct((seqs, length, qw), BF)]
        + [jax.ShapeDtypeStruct((a.shape[0], seqs) + a.shape[2:], BF) for a in pieces],
        scratch_shapes=[pltpu.VMEM((128, 2 * length), F32)],
        compiler_params=params("arbitrary", "arbitrary"),
        cost_estimate=pl.CostEstimate(
            flops=40 * seqs * length * length * spans * qw,
            bytes_accessed=8 * seqs * length * spans * qw,
            transcendentals=seqs * length * length * spans * qw // 64,
        ),
        name="attn_bwd",
    )(ctx, q, do, o, lse, cosine, sine, *pieces, *pieces)


def masked_softmax(logits, named):
    peak = jnp.max(jnp.where(named, logits, NEG), axis=1, keepdims=True)
    grown = jnp.where(named, jnp.exp(jnp.where(named, logits - peak, 0.0)), 0.0)
    return grown / jnp.sum(grown, axis=1, keepdims=True)


def experts_kernel(steps, first, count, micro, more, added, joined, place_ref, router_ref, *refs):
    refs = list(refs)
    n = 1 if joined else refs[-7].shape[1]
    xs = [refs.pop(0) for _ in range(2 * steps)]
    dys = [refs.pop(0) for _ in range(2 * steps)]
    ws = [refs.pop(0) for _ in range(n)]
    before = [refs.pop(0) for _ in range(4)] if more else None
    dws_before = [refs.pop(0) for _ in range(n)] if added else []
    outs = [refs.pop(0) for _ in range(4)]
    dws = [refs.pop(0) for _ in range(n)]
    acc_ref, w_ref, xbuf, dybuf, dwbuf, sems, wsems, dwsems = refs
    step = pl.program_id(0)
    base = place_ref[0]
    c = place_ref[1]
    rows, width = xbuf.shape[1:]
    units = w_ref.shape[-1] // (3 * count)
    both = 2 * count * units
    half = rows // 2

    def copies(t, slot):
        return [
            pltpu.make_async_copy(
                src[2 * t + part].at[micro] if which else src[2 * t + part],
                buf.at[slot, pl.ds(part * half, half)],
                sems.at[slot, 2 * which + part],
            )
            for which, (src, buf) in enumerate(((xs, xbuf), (dys, dybuf)))
            for part in range(2)
        ]

    def fetch(at, slot):
        for t in range(steps):

            @pl.when(at == t)
            def _():
                for copy in copies(t, slot):
                    copy.start()

    def weight_copy(d):
        to = w_ref if joined else w_ref.at[:, c ^ d]
        return pltpu.make_async_copy(ws[d], to, wsems.at[d])

    def added_copy(d):
        return pltpu.make_async_copy(dws_before[d], dwbuf.at[d], dwsems.at[d])

    slot = step % 2

    @pl.when(step == 0)
    def _():
        fetch(step, slot)
        for d in range(n):
            weight_copy(d).start()
        for d in range(n):
            weight_copy(d).wait()
        if added:
            for d in range(n):
                added_copy(d).start()

    @pl.when(step + 1 < steps)
    def _():
        fetch(step + 1, 1 - slot)

    for copy in copies(0, slot):
        copy.wait()

    x = xbuf[slot]
    dy = dybuf[slot, :, :width]
    lane = lax.broadcasted_iota(jnp.int32, (rows, 128), 1)
    named = dybuf[slot, :, width:].astype(F32) > 0.5
    gates = masked_softmax(dot(x, router_ref[...], 1, 0), named)
    gates = pltpu.roll(gates, 128 - base, 1)
    w_in = w_ref[..., :both].reshape(width, both)
    w_back = w_ref[..., both:].reshape(width, both // 2)
    gu = dot(x, w_in, 1, 0)
    g = gu[:, : both // 2]
    u = gu[:, both // 2 :]
    z = dot(dy, w_back, 1, 0)
    gate = jnp.concatenate(
        [
            jnp.broadcast_to(gates[:, first + e : first + e + 1], (rows, units))
            for e in range(count)
        ],
        axis=1,
    )
    sig = 1.0 / (1.0 + jnp.exp(-g))
    silu = g * sig
    act = silu * u
    product = act.astype(BF).astype(F32) * z
    dgates = jnp.zeros((rows, 128), F32)
    for e in range(count):
        total = jnp.sum(product[:, e * units : (e + 1) * units], axis=1, keepdims=True)
        dgates = jnp.where(lane == base + first + e, total, dgates)
    gact = (gate * act).astype(BF)
    da = gate * z
    dgu = jnp.concatenate(
        [
            (da * u * (sig * (1.0 + g * (1.0 - sig)))).astype(BF),
            (da * silu).astype(BF),
        ],
        axis=1,
    )
    out = dot(gact, w_back, 1, 1)
    dx = dot(dgu, w_in, 1, 1)
    for part in range(2):
        at = slice(part * half, (part + 1) * half)
        o, d, t = out[at], dx[at], dgates[at]
        if more:
            o = o + before[part][0].astype(F32)
            d = d + before[2 + part][0, :, :width].astype(F32)
            t = t + before[2 + part][0, :, width:].astype(F32)
        outs[part][0] = o.astype(BF)
        outs[2 + part][0, :, :width] = d.astype(BF)
        outs[2 + part][0, :, width:] = t.astype(BF)

    @pl.when(step == 0)
    def _():
        acc_ref[...] = jnp.zeros_like(acc_ref)

    acc_ref[:, :both] += dot(x.T, dgu, 1, 0)
    acc_ref[:, both:] += dot(dy.T, gact, 1, 0)

    @pl.when(step == pl.num_programs(0) - 1)
    def _():
        for d in range(n):
            if added:
                added_copy(d).wait()
            if joined:
                total = acc_ref[...]
                dws[0][...] = (total + dwbuf[0].astype(F32) if added else total).astype(BF)
                continue
            planes, _, shard, _ = w_ref.shape
            for plane in range(planes):
                row = pl.multiple_of((plane * n + (c ^ d)) * shard, shard)
                total = acc_ref[pl.ds(row, shard)]
                if added:
                    total = total + dwbuf[d, plane].astype(F32)
                dws[d][plane] = total.astype(BF)


def experts_call(
    xs, dys, micro, place, router, weights, first, count, before, dws_before
):
    steps = len(xs) // 2
    half, width = xs[0].shape
    tile = 2 * half
    n = len(weights)
    joined = n == 1
    block = weights[0].shape
    whole_shape = block if joined else block[:1] + (n,) + block[1:]
    lanes = block[-1]
    out_block = pl.BlockSpec((1, half, width), lambda i: (i, 0, 0))
    dx_block = pl.BlockSpec((1, half, width + 128), lambda i: (i, 0, 0))
    whole = pl.BlockSpec(memory_space=pltpu.VMEM)
    anywhere = pl.BlockSpec(memory_space=pl.ANY)
    blocks = [out_block, out_block, dx_block, dx_block]
    rows = steps * tile
    return pl.pallas_call(
        functools.partial(
            experts_kernel, steps, first, count, micro, bool(before), bool(dws_before), joined
        ),
        grid=(steps,),
        in_specs=[
            pl.BlockSpec(memory_space=pltpu.SMEM),
            pl.BlockSpec((width, 128), lambda i: (0, 0)),
        ]
        + [anywhere] * (4 * steps + n)
        + (blocks if before else [])
        + [anywhere] * len(dws_before),
        out_specs=blocks + [whole] * n,
        out_shape=[jax.ShapeDtypeStruct((steps, half, width), BF)] * 2
        + [jax.ShapeDtypeStruct((steps, half, width + 128), BF)] * 2
        + [jax.ShapeDtypeStruct(block, BF)] * n,
        scratch_shapes=[
            pltpu.VMEM((width, lanes), F32),
            pltpu.VMEM(whole_shape, BF),
            pltpu.VMEM((2, tile, width), BF),
            pltpu.VMEM((2, tile, width + 128), BF),
            pltpu.VMEM(((n if dws_before else 1),) + (block if dws_before else (16, 128)), BF),
            pltpu.SemaphoreType.DMA((2, 4)),
            pltpu.SemaphoreType.DMA((n,)),
            pltpu.SemaphoreType.DMA((n,)),
        ],
        compiler_params=params("arbitrary"),
        cost_estimate=pl.CostEstimate(
            flops=6 * rows * width * lanes,
            bytes_accessed=8 * rows * width + 4 * width * lanes,
            transcendentals=rows * lanes // 3,
        ),
        name="experts",
    )(place, router, *xs, *dys, *weights, *(before or []), *dws_before)


def back_kernel(dq_ref, x_ref, cos_ref, sin_ref, wq_ref, wkv_ref, *refs):
    *terms, dkv_ref, part_ref, gain_ref = refs
    total = functools.reduce(jnp.add, [t[...].astype(F32) for t in terms])
    kw = total.shape[1] // 2
    dk = turn(total[:, :kw], cos_ref[...], -sin_ref[...]).astype(BF)
    dkv = jnp.concatenate([dk, total[:, kw:].astype(BF)], axis=1)
    dkv_ref[...] = dkv
    part = dot(dq_ref[...], wq_ref[...], 1, 1) + dot(dkv, wkv_ref[...], 1, 1)
    part_ref[...] = part.astype(BF)
    x = x_ref[...].astype(F32)
    unit = x * lax.rsqrt(jnp.mean(x * x, axis=1, keepdims=True) + EPS)
    sums = jnp.broadcast_to(jnp.sum(part * unit, axis=0, keepdims=True), gain_ref.shape)

    @pl.when(pl.program_id(0) == 0)
    def _():
        gain_ref[...] = sums

    @pl.when(pl.program_id(0) > 0)
    def _():
        gain_ref[...] += sums


def back_call(dq, terms, x, micro, cosine, sine, w_qo, w_kv):
    rows, qw = dq.shape
    lanes = terms[0].shape[1]
    d = w_qo.shape[0]
    tile = min(256, cosine.shape[0])
    per = cosine.shape[0] // tile
    row = lambda width: pl.BlockSpec((tile, width), lambda i: (i, 0))
    table = pl.BlockSpec((tile, 128), lambda i: (i % per, 0))
    return pl.pallas_call(
        back_kernel,
        grid=(rows // tile,),
        in_specs=[
            row(qw),
            pl.BlockSpec((tile, d), lambda i: (i + micro * (rows // tile), 0)),
            table,
            table,
            pl.BlockSpec((d, qw), lambda i: (0, 0)),
            pl.BlockSpec((d, lanes), lambda i: (0, 0)),
        ]
        + [row(lanes)] * len(terms),
        out_specs=[row(lanes), row(d), pl.BlockSpec((8, d), lambda i: (0, 0))],
        out_shape=[
            jax.ShapeDtypeStruct((rows, lanes), BF),
            jax.ShapeDtypeStruct((rows, d), BF),
            jax.ShapeDtypeStruct((8, d), F32),
        ],
        compiler_params=params("arbitrary"),
        cost_estimate=pl.CostEstimate(
            flops=2 * rows * d * (qw + lanes), bytes_accessed=8 * rows * d, transcendentals=0
        ),
        name="back",
    )(dq, x, cosine, sine, w_qo, w_kv, *terms)


def grads_kernel(pairs, starts, extra, place_ref, *refs):
    refs = list(refs)
    sides = [[(refs.pop(0), refs.pop(0)) for _ in range(count)] for count in pairs]
    more = refs.pop(0) if extra else None
    count = len(refs)
    block = refs[0].shape[0]
    for s in range(count):
        at = pl.ds(pl.multiple_of((place_ref[0] ^ s) * block, block), block)
        column = 0
        for side, firsts in zip(sides, starts):
            total = functools.reduce(
                jnp.add,
                [
                    dot(left[first : first + right.shape[0], at], right[...], 0, 0)
                    for (left, right), first in zip(side, firsts)
                ],
            )
            refs[s][:, column : column + total.shape[1]] = total.astype(BF)
            column += total.shape[1]
        if extra:
            refs[s][:, column:] = more[at, :]


def grads_call(me, sides, extra, count):
    d = sides[0][0][0].shape[1]
    lanes = sum(side[0][1].shape[1] for side in sides) + (0 if extra is None else extra.shape[1])
    whole = pl.BlockSpec(memory_space=pltpu.VMEM)
    operands = [a for side in sides for term in side for a in term[:2]]
    starts = [[term[2] for term in side] for side in sides]
    operands += [] if extra is None else [extra]
    return pl.pallas_call(
        functools.partial(grads_kernel, [len(side) for side in sides], starts, extra is not None),
        in_specs=[pl.BlockSpec(memory_space=pltpu.SMEM)] + [whole] * len(operands),
        out_specs=[whole] * count,
        out_shape=[jax.ShapeDtypeStruct((d // count, lanes), BF)] * count,
        compiler_params=pltpu.CompilerParams(vmem_limit_bytes=VMEM_LIMIT),
        cost_estimate=pl.CostEstimate(
            flops=2 * d * lanes * 1024, bytes_accessed=4 * d * lanes, transcendentals=0
        ),
        name="grads",
    )(me, *operands)


def line_kernel(count, place_ref, *refs):
    terms, outs, scratch = refs[:-count - 1], refs[-count - 1 : -1], refs[-1]
    scratch[...] = functools.reduce(jnp.add, [t[...].astype(F32) for t in terms])
    shard = outs[0].shape[0]
    for s in range(count):
        row = pl.multiple_of((place_ref[0] ^ s) * shard, shard)
        outs[s][...] = scratch[pl.ds(row, shard)].astype(BF)


def line_call(me, terms, count):
    rows, lanes = terms[0].shape
    whole = pl.BlockSpec(memory_space=pltpu.VMEM)
    return pl.pallas_call(
        functools.partial(line_kernel, count),
        in_specs=[pl.BlockSpec(memory_space=pltpu.SMEM)] + [whole] * len(terms),
        out_specs=[whole] * count,
        out_shape=[jax.ShapeDtypeStruct((rows // count, lanes), BF)] * count,
        scratch_shapes=[pltpu.VMEM((rows, lanes), F32)],
        compiler_params=pltpu.CompilerParams(vmem_limit_bytes=VMEM_LIMIT),
        name="line",
    )(me, *terms)


def reorder_heads(values):
    parts = []
    for at in range(0, values.shape[1], 256):
        a = values[:, at : at + 128]
        b = values[:, at + 128 : at + 256]
        low = lax.broadcasted_iota(jnp.int32, a.shape, 1) < HD
        parts += [
            jnp.where(low, a, pltpu.roll(b, HD, 1)),
            jnp.where(low, pltpu.roll(a, HD, 1), b),
        ]
    return jnp.concatenate(parts, axis=1)


def finish_kernel(count, *refs):
    early = functools.reduce(jnp.add, [r[...].astype(F32) for r in refs[:count]])
    late = functools.reduce(jnp.add, [r[...].astype(F32) for r in refs[count : 2 * count]])
    q_ref, k_ref, v_ref, o_ref, small_ref = refs[2 * count :]
    qw = q_ref.shape[1]
    kw = k_ref.shape[1]
    q_ref[...] = reorder_heads(early[:, :qw])
    o_ref[...] = reorder_heads(early[:, qw:])
    k_ref[...] = late[:, :kw]
    v_ref[...] = late[:, kw : 2 * kw]
    small_ref[...] = late[:, 2 * kw :]


def finish_call(early, late, qw, kw):
    shard = early[0].shape[0]
    whole = pl.BlockSpec(memory_space=pltpu.VMEM)
    return pl.pallas_call(
        functools.partial(finish_kernel, len(early)),
        in_specs=[whole] * (2 * len(early)),
        out_specs=[whole] * 5,
        out_shape=[
            jax.ShapeDtypeStruct((shard, w), F32) for w in (qw, kw, kw, qw, 128)
        ],
        name="finish",
    )(*early, *late)


def expert_rows_kernel(count, place_ref, *refs):
    pieces, outs = refs[:-3], refs[-3:]
    groups = 2
    units = outs[0].shape[2]
    group = outs[0].shape[0] // (count * groups)
    for g in range(groups):
        for s in range(count):
            piece = pieces[g * count + s]
            at = ((place_ref[0] ^ s) * groups + g) * group
            for i in range(3):
                for e in range(group):
                    lanes = (i * group + e) * units
                    outs[i][at + e] = piece[:, lanes : lanes + units].astype(F32)


def expert_rows_call(me, pieces, experts, units):
    shard = pieces[0].shape[0]
    whole = pl.BlockSpec(memory_space=pltpu.VMEM)
    return pl.pallas_call(
        functools.partial(expert_rows_kernel, len(pieces) // 2),
        in_specs=[pl.BlockSpec(memory_space=pltpu.SMEM)] + [whole] * len(pieces),
        out_specs=[whole] * 3,
        out_shape=[jax.ShapeDtypeStruct((experts, shard, units), F32)] * 3,
        compiler_params=pltpu.CompilerParams(vmem_limit_bytes=VMEM_LIMIT),
        name="expert_rows",
    )(me, *pieces)


def apart(count, step):
    return [(i, i ^ step) for i in range(count)]


def swap(value):
    return lax.ppermute(value, "mp", [(0, 1), (1, 0)])


def up_hop(value, n, s):
    return lax.ppermute(value, "ctx", [(c, c + 1) for c in range(s, n - 1)])


def add(*terms):
    return functools.reduce(jnp.add, [t.astype(F32) for t in terms]).astype(BF)


def by_xor(parts, me):
    bit = 1
    while bit < len(parts):
        flip = (me & bit) != 0
        parts = [jnp.where(flip, parts[i ^ bit], parts[i]) for i in range(len(parts))]
        bit *= 2
    return parts


def exchange(parts, axis):
    count = len(parts)
    return [parts[0]] + [
        lax.ppermute(parts[s], axis, apart(count, s)) for s in range(1, count)
    ]


def from_last(values, start, count):
    values = values[::-1]
    return lax.dynamic_slice_in_dim(jnp.concatenate([values, values]), start, count, 0)


def head_order(weight):
    rows, width = weight.shape
    return (
        weight.reshape(rows, width // (4 * HD), 2, 2, HD).swapaxes(2, 3).reshape(rows, width)
    )


def per_device(
    tokens,
    cotangent,
    routes,
    norm_gain,
    w_query,
    w_key,
    w_value,
    w_output,
    ffn_gain,
    w_router,
    w_gate,
    w_up,
    w_down,
):
    micro, seq_count, local, width = tokens.shape
    top = routes.shape[3]
    experts, shard, units = w_gate.shape
    dp = lax.axis_size("dp")
    n = lax.axis_size("ctx")
    hops = n == 4
    me_dp = lax.axis_index("dp")
    me_ctx = lax.axis_index("ctx")
    me_mp = lax.axis_index("mp")
    mine_count = experts // dp
    group = mine_count // 2
    micros = range(micro)
    per = seq_count * local
    half = per // 2
    rows = micro * per
    qw = w_query.shape[1]
    kw = w_key.shape[1]
    ctx_now = me_ctx.astype(jnp.int32).reshape(1)
    dp_now = me_dp.astype(jnp.int32).reshape(1)
    place = jnp.stack([me_dp * mine_count, me_ctx]).astype(jnp.int32)

    def in_order(mine, other):
        first = me_mp == 0
        return jnp.concatenate([jnp.where(first, mine, other), jnp.where(first, other, mine)])

    def halves(full):
        cut = full.reshape(2, half, full.shape[1])
        mine = lax.dynamic_index_in_dim(cut, me_mp, 0, keepdims=False)
        return mine, lax.dynamic_index_in_dim(cut, 1 - me_mp, 0, keepdims=False)

    def far_pieces(mine, steps=range(1, dp)):
        return [lax.ppermute(mine, "dp", apart(dp, s)) for s in steps]

    def paired(mine, far, other, near):
        return [piece for pair in zip([mine] + far, [other] + near) for piece in pair]

    def gather_line(value):
        return jnp.stack(
            [value] + [lax.ppermute(value, "ctx", apart(n, s)) for s in range(1, n)]
        )

    def gather_plane(value):
        return [value] + [lax.ppermute(value, "dp", apart(dp, s)) for s in range(1, dp)]

    def whole_rows(pieces):
        lines = by_xor(pieces, me_dp)
        full = jnp.stack(lines)
        cols = by_xor([full[:, i] for i in range(n)], me_ctx)
        return jnp.stack(cols, axis=1).reshape(dp * n * shard, full.shape[3])

    live = {}

    def seal(**values):
        live.update(values)
        live.update(lax.optimization_barrier(live))

    small = jnp.concatenate([w_router, norm_gain[:, None], ffn_gain[:, None]], axis=1)
    small = jnp.pad(small, ((0, 0), (0, 128 - small.shape[1])))
    kv_shard = jnp.concatenate([w_key, w_value, small], axis=1)
    qo_shard = jnp.concatenate([head_order(w_query), head_order(w_output)], axis=1)
    side = lambda w: w.reshape(dp, 2, group, shard, units)
    w3 = jnp.concatenate(
        [side(w)[:, :, e] for w in (w_gate, w_up, w_down) for e in range(group)], axis=3
    )
    if hops:
        kv_line = gather_line(kv_shard)
        qo_line = gather_line(qo_shard)
    w3_parts = exchange(by_xor([w3[i] for i in range(dp)], me_dp), "dp")
    own3 = by_xor(w3_parts, me_dp)
    own3 = [jnp.stack([o[g] for o in own3]) for g in range(2)]
    def weight_send(g, *steps):
        if hops:
            for s in steps:
                at, hop = (2, 1) if s == 3 else (0, s)
                live["weights"][g][s] = lax.ppermute(live["weights"][g][at], "ctx", apart(n, hop))

    def seal_but(under_way, **values):
        kept = [(d, {k: d.pop(k) for k in keys if k in d}) for d, keys in under_way()]
        seal(**values)
        for (d, keys), (_, taken) in zip(under_way(), kept):
            d.update(taken)

    if hops:
        own3 = [{0: o} for o in own3]
        seal(kv_line=kv_line, qo_line=qo_line, weights=own3, x=tokens, dy=cotangent, routes=routes)
        kv_pieces = gather_plane(live.pop("kv_line"))
        weight_send(0, 1)
        seal(kv_pieces=kv_pieces)
        kv_full = whole_rows(live.pop("kv_pieces"))
        qo_pieces = gather_plane(live.pop("qo_line"))
    else:
        kv_full = lax.all_gather(kv_shard, ("dp", "ctx"), axis=0, tiled=True)
        qo_full = lax.all_gather(qo_shard, ("dp", "ctx"), axis=0, tiled=True)
        own3 = [lax.all_gather(o, "ctx", axis=1, tiled=False) for o in own3]
        own3 = [{0: o.reshape(width, o.shape[-1])} for o in own3]
        seal(weights=own3, x=tokens, dy=cotangent, routes=routes)
    small = kv_full[:, 2 * kw :]
    router = small[:, :experts]
    router_wide = jnp.pad(router, ((0, 0), (0, 128 - experts)))
    gain_one = small[:, experts].astype(F32)[None, :]
    gain_two = small[:, experts + 1].astype(F32)[None, :]

    position = me_ctx * local + jnp.arange(local, dtype=jnp.int32)
    freqs = THETA ** (-(jnp.arange(HD // 2, dtype=F32) * 2.0) / HD)
    angles = position.astype(F32)[:, None] * freqs[None, :]
    cosine = jnp.tile(jnp.cos(angles), (1, 4))
    sine = jnp.sin(angles)
    sine = jnp.concatenate([-sine, sine, -sine, sine], axis=1)
    live["x"] = live["x"].reshape(rows, width)
    live["dy"] = live["dy"].reshape(rows, width)
    normed, kv = kv_call(live["x"], gain_one, kv_full, 2 * kw, cosine, sine)
    kv = kv.reshape(1, micro * seq_count, local, 2 * kw)

    ids = live.pop("routes").reshape(rows, top)
    marks = jnp.sum(
        (ids[:, :, None] == jnp.arange(128, dtype=jnp.int32)[None, None, :]).astype(F32), axis=1
    ).astype(BF)
    dyx = jnp.concatenate([live["dy"], marks], axis=1)
    dyx = dyx.reshape(micro, 2, half, width + 128)
    dy_cut = [
        lax.dynamic_index_in_dim(dyx, at, 1, keepdims=False) for at in (me_mp, 1 - me_mp)
    ]

    if hops:
        kv_got = up_hop(kv, n, 0)
        seal(
            kv=kv,
            kv_prev=[kv_got],
            qo_pieces=qo_pieces,
            normed=normed,
            dy_cut=dy_cut,
            marks=marks[:, :experts],
            kv_full=kv_full,
            cosine=cosine,
            sine=sine,
            router=router,
            router_wide=router_wide,
            gain_one=gain_one,
            gain_two=gain_two,
        )
        qo_full = whole_rows(live.pop("qo_pieces"))
    else:
        every = lax.all_gather(kv[0], "ctx", axis=0, tiled=False)
        seal(
            kv=kv,
            kv_prev=[from_last(every, n - me_ctx, n - 1)],
            normed=normed,
            dy_cut=dy_cut,
            marks=marks[:, :experts],
            kv_full=kv_full,
            cosine=cosine,
            sine=sine,
            router=router,
            router_wide=router_wide,
            gain_one=gain_one,
            gain_two=gain_two,
        )
    live.update(qo_full=qo_full, dy_far=[], dy_near=[])
    q = q_call(live["normed"], qo_full, qw, live["cosine"], live["sine"])
    live["q"] = q.reshape(micro * seq_count, local, qw)

    def dy_send(steps):
        for s in steps:
            live["dy_far"].append(lax.ppermute(live["dy_cut"][0], "dp", apart(dp, s)))

    def attend(first, s, done):
        return attn_part(
            ctx_now,
            live["q"],
            live["kv"] if first else None,
            [live["kv_prev"][s - 1]],
            s,
            None if first else live.pop("carry"),
            done,
        )

    def mix(attn):
        return dot(attn.reshape(rows, qw), live["qo_full"][:, qw:], 1, 1).astype(BF)

    if hops:
        dy_send((1, 2))
        got = up_hop(live["kv_prev"][-1], n, 1)
        carry = attend(True, 1, False)
        live["kv_prev"].append(got)
        seal(carry=carry)
        dy_send((3,))
        got = up_hop(live["kv_prev"][-1], n, 2)
        carry = attend(False, 2, False)
        live["kv_prev"].append(got)
        seal(carry=carry)
        weight_send(0, 2)
        attn, lse = attend(False, 3, True)
    else:
        attn, lse = attend(True, 1, True)
        dy_send(range(1, dp))
    live["dy_near"] = [swap(f) for f in live["dy_far"]]
    late = lambda: [(live["weights"][0], [2])]
    seal_but(late, attn=attn, lse=lse, mixed=mix(attn))

    mixed_got = swap(live["mixed"])
    hidden = live["x"].astype(F32) + (live.pop("mixed").astype(F32) + mixed_got.astype(F32))
    inv_two = lax.rsqrt(jnp.mean(hidden * hidden, axis=1, keepdims=True) + EPS)
    ffn_low = (hidden * inv_two * live["gain_two"]).astype(BF)
    x_cut = [halves(ffn_low[m * per : (m + 1) * per]) for m in micros]

    seal_but(late, hidden=hidden, inv_two=inv_two, ffn_low=ffn_low, x_cut=x_cut)
    first = far_pieces(live["x_cut"][0][0], (1, 2))
    live["x_far"] = [first] + [[]] * (micro - 1)
    seal()
    live["x_far"][0] = live["x_far"][0] + far_pieces(live["x_cut"][0][0], (3,))
    weight_send(0, 3)
    seal()
    live["x_near"] = [[swap(f) for f in live["x_far"][0]]] + [[]] * (micro - 1)
    seal()
    live.update(sums=[], dws=[[], []], parts=[])

    def run(g, m, before):
        weights = [live["weights"][g][s] for s in sorted(live["weights"][g])]
        x_cut, dy_cut = live["x_cut"][m], live["dy_cut"]
        xs = paired(x_cut[0], live["x_far"][m], x_cut[1], live["x_near"][m])
        dys = paired(dy_cut[0], live["dy_far"], dy_cut[1], live["dy_near"])
        part = experts_call(
            xs,
            dys,
            m,
            place,
            live["router_wide"],
            weights,
            g * group,
            group,
            before,
            live["dws"][g],
        )
        live["dws"][g] = part[4:]
        return list(part[:4])

    live["x_far"][1] = far_pieces(live["x_cut"][1][0])
    weight_send(1, 1, 2)
    live["sums"].append(run(0, 0, None))
    seal()
    live["x_near"][1] = [swap(f) for f in live["x_far"][1]]
    seal()
    weight_send(1, 3)
    live["sums"].append(run(0, 1, None))
    seal()

    live.update(rows=[{}, {}])

    def grad_send(g, *steps):
        if hops:
            for s in steps:
                live["rows"][g][s] = lax.ppermute(live["dws"][g][s], "ctx", apart(n, s))

    def grad_own(g):
        if hops:
            own = add(live["dws"][g][0], *live["rows"][g].values())
        else:
            whole = live["dws"][g][0].reshape(dp, n, shard, -1)
            own = lax.psum_scatter(whole, "ctx", scatter_dimension=1, tiled=False)
        return exchange(by_xor([own[i] for i in range(dp)], me_dp), "dp")

    def terms_of(mine, got):
        return [add(mine[s], got[s]) for s in range(dp)]

    live.update(dx_terms=[None] * micro, dx_back=[None] * micro)
    live.update(out_terms=[None] * micro, out_back={})

    def dx_terms(m):
        part = live["parts"][m]
        live["dx_terms"][m] = terms_of(part[2], swap(part[3]))

    def dx_send(m):
        live["dx_back"][m] = exchange(live["dx_terms"][m], "dp")

    def out_terms(m):
        part = live["parts"][m]
        live["out_terms"][m] = terms_of(part[0], swap(part[1]))

    def out_send(m):
        live["out_back"][m] = exchange(live["out_terms"][m], "dp")

    grad_send(0, 1, 2)
    live["parts"].append(run(1, 0, live["sums"][0]))
    seal()
    dx_terms(0)
    seal()
    dx_send(0)
    grad_send(0, 3)
    live["parts"].append(run(1, 1, live.pop("sums")[1]))
    seal()

    cut = lambda whole, m: whole[m * per : (m + 1) * per]
    live.update({name: [None] * micro for name in ("dh", "dz", "d_attn", "dq", "dkv")})
    live.update(dkv_sum=[{} for _ in micros])
    live.update(router_sums=[None] * micro, gain_sums=[None] * micro)

    def before_attention(m):
        total = add(*live["dx_back"][m])
        moe = in_order(total, swap(total)).astype(F32)
        low = cut(live["ffn_low"], m)
        inv = cut(live["inv_two"], m)
        dgate = moe[:, width : width + experts]
        gate = masked_softmax(
            dot(low, live["router"], 1, 0), cut(live["marks"], m).astype(F32) > 0.5
        )
        dlogit = gate * (dgate - jnp.sum(gate * dgate, axis=1, keepdims=True))
        dlogit = dlogit.astype(BF)
        live["router_sums"][m] = dot(low, dlogit, 0, 0)
        d_ffn = moe[:, :width] + dot(dlogit, live["router"], 1, 1)
        unit = cut(live["hidden"], m) * inv
        live["gain_sums"][m] = jnp.sum(d_ffn * unit, axis=0)
        g_two = d_ffn * live["gain_two"]
        dh = cut(live["dy"], m).astype(F32) + inv * (
            g_two - unit * jnp.mean(g_two * unit, axis=1, keepdims=True)
        )
        dz = dh.astype(BF)
        live["dh"][m] = dh
        live["dz"][m] = dz
        live["d_attn"][m] = dot(dz, live["qo_full"][:, qw:], 1, 0).astype(BF)

    def attention_back(m):
        dq, *dkv = attn_bwd(
            ctx_now,
            live["q"],
            live["d_attn"][m].reshape(seq_count, local, qw),
            live["attn"],
            live["lse"],
            live["cosine"],
            live["sine"],
            live["kv"],
            live["kv_prev"],
            m * seq_count,
        )
        live["dq"][m] = dq.reshape(per, qw)
        live["dkv"][m] = dkv

    def dkv_send(m, *steps):
        if hops:
            for d in steps:
                live["dkv_sum"][m][d] = lax.ppermute(
                    live["dkv"][m][d], "ctx", [(c, c - d) for c in range(d, n)]
                )

    def back(m):
        if hops:
            terms = [live["dkv"][m][0], *live["dkv_sum"][m].values()]
        else:
            every = from_last(jnp.concatenate(live["dkv"][m]), n - 1 - me_ctx, n)
            terms = [lax.psum_scatter(every, "ctx", scatter_dimension=0, tiled=True)]
        terms = [t.reshape(per, 2 * kw) for t in terms]
        return back_call(
            live["dq"][m],
            terms,
            live["x"],
            m,
            live["cosine"],
            live["sine"],
            live["qo_full"],
            live["kv_full"],
        )

    def out_total(m):
        total = add(*live["out_back"][m])
        moe = in_order(total, swap(total)).astype(F32)
        return (cut(live["hidden"], m) + moe).astype(BF)

    def early_send(*steps):
        if hops:
            for s in steps:
                live["early"][s] = lax.ppermute(live["early"][s], "dp", apart(dp, s))

    before_attention(0)
    dx_terms(1)
    grad_send(1, 1, 2)
    out_terms(0)
    seal_but(lambda: [(live["rows"][1], [1, 2])])
    dx_send(1)
    attention_back(0)
    seal()
    dkv_send(0, 1, 3)
    out_send(0)
    before_attention(1)
    out_terms(1)
    seal_but(lambda: [(live["out_back"], [0])])
    dkv_send(0, 2)
    out_send(1)
    attention_back(1)
    seal()
    dkv_send(1, 1, 2, 3)
    pieces_now = dp_now if hops else jnp.zeros((1,), jnp.int32)
    early = grads_call(
        pieces_now,
        [
            [(live["normed"], live["dq"][m], m * per) for m in micros],
            [(jnp.concatenate(live["dz"]), live["attn"].reshape(rows, qw), 0)],
        ],
        None,
        dp,
    )
    owned = [grad_own(0)]
    seal_but(lambda: [(live["dkv_sum"][1], [1, 2, 3])], early=list(early), owned=owned)
    early_send(1, 2, 3)
    dkv_first, part_first, gain_first = back(0)
    got_first = swap(part_first)
    out_first = out_total(0)
    out_last = out_total(1)
    seal(
        got=[got_first],
        output=[out_first, out_last],
        dkv_final=[dkv_first],
        part=[part_first],
        gain_one_sums=[gain_first],
    )
    grad_send(1, 3)
    dkv_last, part_last, gain_last = back(1)
    live["dkv_final"].append(dkv_last)
    live["part"].append(part_last)
    small = jnp.concatenate(
        [
            live["router_sums"][0] + live["router_sums"][1],
            (live["gain_one_sums"][0] + gain_last)[0][:, None],
            (live["gain_sums"][0] + live["gain_sums"][1])[:, None],
        ],
        axis=1,
    )
    small = jnp.pad(small, ((0, 0), (0, 128 - small.shape[1]))).astype(BF)
    late = grads_call(
        pieces_now,
        [[(live["normed"], live["dkv_final"][m], m * per) for m in micros]],
        small,
        dp,
    )
    got_last = swap(part_last)
    seal_but(
        lambda: [(live["rows"][1], [3])], late=late, got=live["got"] + [got_last]
    )
    early, late = live["early"], live["late"]
    if hops:
        late = exchange(late, "dp")
        early = line_call(ctx_now, early, n)
    d_normed = jnp.concatenate(
        [p.astype(F32) + g.astype(F32) for p, g in zip(live["part"], live["got"])]
    )
    x32 = live["x"].astype(F32)
    inv_one = lax.rsqrt(jnp.mean(x32 * x32, axis=1, keepdims=True) + EPS)
    n_one = x32 * inv_one
    g_one = d_normed * live["gain_one"]
    input_grad = (
        jnp.concatenate(live["dh"])
        + inv_one * (g_one - n_one * jnp.mean(g_one * n_one, axis=1, keepdims=True))
    ).astype(BF)
    seal_but(
        lambda: [(live["rows"][1], [3])], late=late, early=early, input_grad=input_grad
    )
    early, late = live["early"], live["late"]
    if hops:
        late = exchange(line_call(ctx_now, late, n), "ctx")
        early = exchange(early, "ctx")
    else:
        early, late = (
            [
                lax.psum_scatter(
                    jnp.concatenate(p), ("dp", "ctx"), scatter_dimension=0, tiled=True
                )
            ]
            for p in (early, late)
        )
    owned = [live["owned"][0], grad_own(1)]
    output = jnp.concatenate(live["output"])
    grad_q, grad_k, grad_v, grad_o, small_grad = finish_call(early, late, qw, kw)
    gain_part = small_grad[:, experts]
    dw_gate, dw_up, dw_down = expert_rows_call(dp_now, owned[0] + owned[1], experts, units)
    shape = tokens.shape
    return (
        output.reshape(shape),
        live["input_grad"].reshape(shape),
        gain_part + swap(gain_part),
        grad_q,
        grad_k,
        grad_v,
        grad_o,
        small_grad[:, experts + 1],
        small_grad[:, :experts],
        dw_gate,
        dw_up,
        dw_down,
    )


def solution(mesh):
    rows = P(None, "dp", "ctx", None)
    vector = P(("dp", "ctx"))
    matrix = P(("dp", "ctx"), "mp")
    router = P(("dp", "ctx"), None)
    expert = P(None, ("dp", "ctx"), "mp")
    return jax.shard_map(
        per_device,
        mesh=mesh,
        in_specs=(
            rows,
            rows,
            rows,
            vector,
            matrix,
            matrix,
            matrix,
            matrix,
            vector,
            router,
            expert,
            expert,
            expert,
        ),
        out_specs=(
            rows,
            rows,
            vector,
            matrix,
            matrix,
            matrix,
            matrix,
            vector,
            router,
            expert,
            expert,
            expert,
        ),
        check_vma=False,
    )
```

```python
import functools
import math

import jax
import jax.numpy as jnp
from jax import lax
from jax.experimental import pallas as pl
from jax.experimental.pallas import tpu as pltpu
from jax.sharding import PartitionSpec as P

HD = 64
EPS = 1e-06
THETA = 10000.0
NEG = -1e30
VMEM_LIMIT = 60 * 1024 * 1024
BF = jnp.bfloat16
F32 = jnp.float32


def dot(a, b, ca, cb, precision=None):
    return lax.dot_general(
        a, b, (((ca,), (cb,)), ((), ())), preferred_element_type=F32, precision=precision
    )


def params(*semantics):
    return pltpu.CompilerParams(dimension_semantics=semantics, vmem_limit_bytes=VMEM_LIMIT)


def turn(values, cosine, sine):
    width = values.shape[1]
    lane = lax.broadcasted_iota(jnp.int32, values.shape, 1)
    ahead = pltpu.roll(values, width - HD // 2, 1)
    behind = pltpu.roll(values, HD // 2, 1)
    swapped = jnp.where(lane % HD < HD // 2, ahead, behind)
    reps = width // cosine.shape[1]
    return values * jnp.tile(cosine, (1, reps)) + swapped * jnp.tile(sine, (1, reps))


def kv_kernel(x_ref, gain_ref, w_ref, cos_ref, sin_ref, normed_ref, kv_ref):
    x = x_ref[...].astype(F32)
    inv = lax.rsqrt(jnp.mean(x * x, axis=1, keepdims=True) + EPS)
    normed = (x * inv * gain_ref[...]).astype(BF)
    normed_ref[...] = normed
    kw = kv_ref.shape[1] // 2
    raw = dot(normed, w_ref[...], 1, 0)
    kv_ref[:, :kw] = turn(raw[:, :kw], cos_ref[...], sin_ref[...]).astype(BF)
    kv_ref[:, kw:] = raw[:, kw:].astype(BF)


def q_kernel(normed_ref, w_ref, cos_ref, sin_ref, q_ref):
    raw = dot(normed_ref[...], w_ref[...], 1, 0)
    q_ref[...] = turn(raw, cos_ref[...], sin_ref[...]).astype(BF)


def row_specs(rows, local, d, lanes):
    tile = min(256, local)
    per = local // tile
    return (
        rows // tile,
        pl.BlockSpec((tile, d), lambda i: (i, 0)),
        pl.BlockSpec((d, lanes), lambda i: (0, 0)),
        pl.BlockSpec((tile, 128), lambda i: (i % per, 0)),
        pl.BlockSpec((tile, lanes), lambda i: (i, 0)),
        pl.CostEstimate(
            flops=2 * rows * d * lanes, bytes_accessed=6 * rows * d, transcendentals=rows
        ),
    )


def kv_call(x, gain, w, lanes, cosine, sine):
    rows, d = x.shape
    steps, row, weight, table, out, cost = row_specs(rows, cosine.shape[0], d, lanes)
    return pl.pallas_call(
        kv_kernel,
        grid=(steps,),
        in_specs=[row, pl.BlockSpec((1, d), lambda i: (0, 0)), weight, table, table],
        out_specs=[row, out],
        out_shape=[
            jax.ShapeDtypeStruct((rows, d), BF),
            jax.ShapeDtypeStruct((rows, lanes), BF),
        ],
        compiler_params=params("arbitrary"),
        cost_estimate=cost,
        name="kv",
    )(x, gain, w, cosine, sine)


def q_call(normed, w, lanes, cosine, sine):
    rows, d = normed.shape
    steps, row, weight, table, out, cost = row_specs(rows, cosine.shape[0], d, lanes)
    return pl.pallas_call(
        q_kernel,
        grid=(steps,),
        in_specs=[row, weight, table, table],
        out_specs=out,
        out_shape=jax.ShapeDtypeStruct((rows, lanes), BF),
        compiler_params=params("arbitrary"),
        cost_estimate=cost,
        name="q",
    )(normed, w, cosine, sine)


def half_mask(block, which):
    lane = lax.broadcasted_iota(jnp.int32, block.shape, 1)
    keep = (lane < HD) if which == 0 else (lane >= HD)
    return jnp.where(keep, block, jnp.zeros_like(block))


def stacked(ref):
    return jnp.concatenate([ref[0, :, :128], ref[0, :, 128:]], axis=0)


def causal(shape, length):
    key = lax.broadcasted_iota(jnp.int32, shape, 0)
    query = lax.broadcasted_iota(jnp.int32, shape, 1) % length
    return key <= query


def each_earlier(c, counts, visit, otherwise=None, first=1):
    for piece, count in enumerate(counts):
        if count == 1:

            @pl.when(c >= first)
            def _():
                visit(piece, 0)

            if otherwise is not None:

                @pl.when(c < first)
                def _():
                    otherwise(piece, 0)

        else:
            reach = jnp.clip(c - first + 1, 0, count)

            @pl.loop(0, reach)
            def _(entry):
                visit(piece, entry)

            if otherwise is not None:

                @pl.loop(reach, count)
                def _(entry):
                    otherwise(piece, entry)

        first += count


def attn_part_kernel(counts, start, first, last, ctx_ref, q_ref, *refs):
    refs = list(refs)
    pieces = len(counts) + first
    keys = [refs.pop(0) for _ in range(pieces)]
    vals = [refs.pop(0) for _ in range(pieces)]
    old = None if first else [refs.pop(0) for _ in range(2)]
    if last:
        o_ref, lse_ref, stats_ref, acc_ref = refs
    else:
        stats_ref, acc_ref = (ref.at[0, 0] for ref in refs)
    length = q_ref.shape[1]
    both = (stacked(q_ref).astype(F32) * HD**-0.5).astype(BF)
    c = ctx_ref[0]

    if first:
        k = keys[0][0, 0]
        v = vals[0][0, 0]
        for i in range(2):
            s = dot(half_mask(k, i), both, 1, 1)
            s = jnp.where(causal(s.shape, length), s, NEG)
            peak = jnp.max(s, axis=0, keepdims=True)
            p = jnp.exp(s - peak)
            stats_ref[i : i + 1] = peak
            stats_ref[i + 2 : i + 3] = jnp.sum(p, axis=0, keepdims=True)
            acc_ref[i] = dot(v, p.astype(BF), 0, 0)
    else:
        stats_ref[...] = old[0][0, 0]
        acc_ref[...] = old[1][0, 0]

    def visit(piece, entry):
        k = keys[piece + first][entry, 0]
        v = vals[piece + first][entry, 0]
        for i in range(2):
            s = dot(half_mask(k, i), both, 1, 1)
            peak = stats_ref[i : i + 1]
            now = jnp.maximum(peak, jnp.max(s, axis=0, keepdims=True))
            p = jnp.exp(s - now)
            factor = jnp.exp(peak - now)
            stats_ref[i : i + 1] = now
            stats_ref[i + 2 : i + 3] = stats_ref[i + 2 : i + 3] * factor + jnp.sum(
                p, axis=0, keepdims=True
            )
            acc_ref[i] = acc_ref[i] * factor + dot(v, p.astype(BF), 0, 0)

    each_earlier(c, counts, visit, None, start)
    if last:
        row = lax.broadcasted_iota(jnp.int32, acc_ref.shape[1:], 0)
        stats = stats_ref[...]
        out = jnp.where(row < HD, acc_ref[0] / stats[2:3], acc_ref[1] / stats[3:4]).T
        o_ref[0, :, :128] = out[:length].astype(BF)
        o_ref[0, :, 128:] = out[length:].astype(BF)
        lse_ref[0, 0] = stats[:2] + jnp.log(stats[2:])


def kv_specs(pieces, length, lanes, at=0):
    kb = lanes // 256
    keys = [
        pl.BlockSpec((a.shape[0], 1, length, 128), lambda s, p: (0, s + at, 0, p)) for a in pieces
    ]
    vals = [
        pl.BlockSpec((a.shape[0], 1, length, 128), lambda s, p: (0, s + at, 0, kb + p))
        for a in pieces
    ]
    return keys + vals


def attn_part(ctx, q, own, prev, start, carry, last):
    seqs, length, qw = q.shape
    pairs = qw // 256
    cols = 2 * length
    first = own is not None
    pieces = ([own] if first else []) + prev
    counts = tuple(a.shape[0] for a in prev)
    spans = first + sum(counts)
    state = [
        pl.BlockSpec((1, 1, 4, cols), lambda s, p: (s, p, 0, 0)),
        pl.BlockSpec((1, 1, 2, 128, cols), lambda s, p: (s, p, 0, 0, 0)),
    ]
    if last:
        out_specs = [
            pl.BlockSpec((1, length, 256), lambda s, p: (s, 0, p)),
            pl.BlockSpec((1, 1, 2, cols), lambda s, p: (s, p, 0, 0)),
        ]
        out_shape = [
            jax.ShapeDtypeStruct((seqs, length, qw), BF),
            jax.ShapeDtypeStruct((seqs, pairs, 2, cols), F32),
        ]
        scratch = [pltpu.VMEM((4, cols), F32), pltpu.VMEM((2, 128, cols), F32)]
    else:
        out_specs = state
        out_shape = [
            jax.ShapeDtypeStruct((seqs, pairs, 4, cols), F32),
            jax.ShapeDtypeStruct((seqs, pairs, 2, 128, cols), F32),
        ]
        scratch = []
    return pl.pallas_call(
        functools.partial(attn_part_kernel, counts, start, first, last),
        grid=(seqs, pairs),
        in_specs=[
            pl.BlockSpec(memory_space=pltpu.SMEM),
            pl.BlockSpec((1, length, 256), lambda s, p: (s, 0, p)),
        ]
        + kv_specs(pieces, length, pieces[0].shape[3])
        + ([] if first else state),
        out_specs=out_specs,
        out_shape=out_shape,
        scratch_shapes=scratch,
        compiler_params=params("arbitrary", "arbitrary"),
        cost_estimate=pl.CostEstimate(
            flops=16 * seqs * length * length * spans * qw,
            bytes_accessed=4 * seqs * length * spans * qw,
            transcendentals=seqs * length * length * spans * qw // 64,
        ),
        name="attn_fwd",
    )(ctx, q, *pieces, *pieces, *(carry or []))


def attn_bwd_kernel(counts, ctx_ref, q_ref, do_ref, o_ref, lse_ref, cos_ref, sin_ref, *refs):
    pieces = len(counts)
    keys = refs[: pieces + 1]
    vals = refs[pieces + 1 : 2 * pieces + 2]
    dq_ref = refs[2 * pieces + 2]
    outs = refs[2 * pieces + 3 : 3 * pieces + 4]
    acc_ref = refs[3 * pieces + 4]
    length = q_ref.shape[1]
    lanes = outs[0].shape[3]
    pair = pl.program_id(1)
    both = (stacked(q_ref).astype(F32) * HD**-0.5).astype(BF)
    dboth = stacked(do_ref)
    prod = dboth.astype(F32) * stacked(o_ref).astype(F32)
    pick_row = lax.broadcasted_iota(jnp.int32, (8, 128), 0)
    pick_lane = lax.broadcasted_iota(jnp.int32, (8, 128), 1) // HD
    picks = (pick_row == pick_lane).astype(F32)
    delta = dot(picks, prod, 1, 1, lax.Precision.HIGHEST)
    c = ctx_ref[0]
    k_at = pl.ds(pl.multiple_of(pair * 128, 128), 128)
    v_at = pl.ds(pl.multiple_of(lanes // 2 + pair * 128, 128), 128)

    def block(piece, entry, diagonal):
        k = keys[piece][entry, 0]
        v = vals[piece][entry, 0]
        parts = []
        dq = None
        for i in range(2):
            ki = half_mask(k, i)
            s = dot(ki, both, 1, 1)
            p = jnp.exp(s - lse_ref[0, 0, i : i + 1, :])
            if diagonal:
                p = jnp.where(causal(s.shape, length), p, 0.0)
            dp = dot(half_mask(v, i), dboth, 1, 1)
            ds = (p * (dp - delta[i : i + 1, :])).astype(BF)
            parts.append((dot(ds, both, 1, 0), dot(p.astype(BF), dboth, 1, 0)))
            part = dot(ki, ds, 0, 0)
            dq = part if dq is None else dq + part
        low = lax.broadcasted_iota(jnp.int32, (length, 128), 1) < HD
        outs[piece][entry, 0, :, k_at] = jnp.where(low, parts[0][0], parts[1][0]).astype(BF)
        outs[piece][entry, 0, :, v_at] = jnp.where(low, parts[0][1], parts[1][1]).astype(BF)
        return dq

    acc_ref[...] = block(0, 0, True)

    def visit(piece, entry):
        acc_ref[...] += block(piece + 1, entry, False)

    def clear(piece, entry):
        outs[piece + 1][entry, 0, :, k_at] = jnp.zeros((length, 128), BF)
        outs[piece + 1][entry, 0, :, v_at] = jnp.zeros((length, 128), BF)

    each_earlier(c, counts, visit, clear)
    out = acc_ref[...].T * HD**-0.5
    cosine = cos_ref[...]
    sine = -sin_ref[...]
    dq_ref[0, :, :128] = turn(out[:length], cosine, sine).astype(BF)
    dq_ref[0, :, 128:] = turn(out[length:], cosine, sine).astype(BF)


def attn_bwd(ctx, q, do, o, lse, cosine, sine, own, prev, at):
    seqs, length, qw = do.shape
    pairs = qw // 256
    pieces = [own] + prev
    counts = tuple(a.shape[0] for a in prev)
    spans = 1 + sum(counts)
    blk = pl.BlockSpec((1, length, 256), lambda s, p: (s, 0, p))
    blk_at = pl.BlockSpec((1, length, 256), lambda s, p: (s + at, 0, p))
    tab = pl.BlockSpec((length, 128), lambda s, p: (0, 0))
    return pl.pallas_call(
        functools.partial(attn_bwd_kernel, counts),
        grid=(seqs, pairs),
        in_specs=[
            pl.BlockSpec(memory_space=pltpu.SMEM),
            blk_at,
            blk,
            blk_at,
            pl.BlockSpec((1, 1, 2, 2 * length), lambda s, p: (s + at, p, 0, 0)),
            tab,
            tab,
        ]
        + kv_specs(pieces, length, own.shape[3], at),
        out_specs=[blk]
        + [
            pl.BlockSpec((a.shape[0], 1) + a.shape[2:], lambda s, p: (0, s, 0, 0)) for a in pieces
        ],
        out_shape=[jax.ShapeDtypeStruct((seqs, length, qw), BF)]
        + [jax.ShapeDtypeStruct((a.shape[0], seqs) + a.shape[2:], BF) for a in pieces],
        scratch_shapes=[pltpu.VMEM((128, 2 * length), F32)],
        compiler_params=params("arbitrary", "arbitrary"),
        cost_estimate=pl.CostEstimate(
            flops=40 * seqs * length * length * spans * qw,
            bytes_accessed=8 * seqs * length * spans * qw,
            transcendentals=seqs * length * length * spans * qw // 64,
        ),
        name="attn_bwd",
    )(ctx, q, do, o, lse, cosine, sine, *pieces, *pieces)


def masked_softmax(logits, named):
    peak = jnp.max(jnp.where(named, logits, NEG), axis=1, keepdims=True)
    grown = jnp.where(named, jnp.exp(jnp.where(named, logits - peak, 0.0)), 0.0)
    return grown / jnp.sum(grown, axis=1, keepdims=True)


def experts_kernel(steps, first, count, micro, more, added, joined, place_ref, router_ref, *refs):
    refs = list(refs)
    n = 1 if joined else refs[-7].shape[1]
    xs = [refs.pop(0) for _ in range(2 * steps)]
    dys = [refs.pop(0) for _ in range(2 * steps)]
    ws = [refs.pop(0) for _ in range(n)]
    before = [refs.pop(0) for _ in range(4)] if more else None
    dws_before = [refs.pop(0) for _ in range(n)] if added else []
    outs = [refs.pop(0) for _ in range(4)]
    dws = [refs.pop(0) for _ in range(n)]
    acc_ref, w_ref, xbuf, dybuf, dwbuf, sems, wsems, dwsems = refs
    step = pl.program_id(0)
    base = place_ref[0]
    c = place_ref[1]
    rows, width = xbuf.shape[1:]
    units = w_ref.shape[-1] // (3 * count)
    both = 2 * count * units
    half = rows // 2

    def copies(t, slot):
        return [
            pltpu.make_async_copy(
                src[2 * t + part].at[micro] if which else src[2 * t + part],
                buf.at[slot, pl.ds(part * half, half)],
                sems.at[slot, 2 * which + part],
            )
            for which, (src, buf) in enumerate(((xs, xbuf), (dys, dybuf)))
            for part in range(2)
        ]

    def fetch(at, slot):
        for t in range(steps):

            @pl.when(at == t)
            def _():
                for copy in copies(t, slot):
                    copy.start()

    def weight_copy(d):
        to = w_ref if joined else w_ref.at[:, c ^ d]
        return pltpu.make_async_copy(ws[d], to, wsems.at[d])

    def added_copy(d):
        return pltpu.make_async_copy(dws_before[d], dwbuf.at[d], dwsems.at[d])

    slot = step % 2

    @pl.when(step == 0)
    def _():
        fetch(step, slot)
        for d in range(n):
            weight_copy(d).start()
        for d in range(n):
            weight_copy(d).wait()
        if added:
            for d in range(n):
                added_copy(d).start()

    @pl.when(step + 1 < steps)
    def _():
        fetch(step + 1, 1 - slot)

    for copy in copies(0, slot):
        copy.wait()

    x = xbuf[slot]
    dy = dybuf[slot, :, :width]
    lane = lax.broadcasted_iota(jnp.int32, (rows, 128), 1)
    named = dybuf[slot, :, width:].astype(F32) > 0.5
    gates = masked_softmax(dot(x, router_ref[...], 1, 0), named)
    gates = pltpu.roll(gates, 128 - base, 1)
    w_in = w_ref[..., :both].reshape(width, both)
    w_back = w_ref[..., both:].reshape(width, both // 2)
    gu = dot(x, w_in, 1, 0)
    g = gu[:, : both // 2]
    u = gu[:, both // 2 :]
    z = dot(dy, w_back, 1, 0)
    gate = jnp.concatenate(
        [
            jnp.broadcast_to(gates[:, first + e : first + e + 1], (rows, units))
            for e in range(count)
        ],
        axis=1,
    )
    sig = 1.0 / (1.0 + jnp.exp(-g))
    silu = g * sig
    act = silu * u
    product = act.astype(BF).astype(F32) * z
    dgates = jnp.zeros((rows, 128), F32)
    for e in range(count):
        total = jnp.sum(product[:, e * units : (e + 1) * units], axis=1, keepdims=True)
        dgates = jnp.where(lane == base + first + e, total, dgates)
    gact = (gate * act).astype(BF)
    da = gate * z
    dgu = jnp.concatenate(
        [
            (da * u * (sig * (1.0 + g * (1.0 - sig)))).astype(BF),
            (da * silu).astype(BF),
        ],
        axis=1,
    )
    out = dot(gact, w_back, 1, 1)
    dx = dot(dgu, w_in, 1, 1)
    for part in range(2):
        at = slice(part * half, (part + 1) * half)
        o, d, t = out[at], dx[at], dgates[at]
        if more:
            o = o + before[part][0].astype(F32)
            d = d + before[2 + part][0, :, :width].astype(F32)
            t = t + before[2 + part][0, :, width:].astype(F32)
        outs[part][0] = o.astype(BF)
        outs[2 + part][0, :, :width] = d.astype(BF)
        outs[2 + part][0, :, width:] = t.astype(BF)

    @pl.when(step == 0)
    def _():
        acc_ref[...] = jnp.zeros_like(acc_ref)

    acc_ref[:, :both] += dot(x.T, dgu, 1, 0)
    acc_ref[:, both:] += dot(dy.T, gact, 1, 0)

    @pl.when(step == pl.num_programs(0) - 1)
    def _():
        for d in range(n):
            if added:
                added_copy(d).wait()
            if joined:
                total = acc_ref[...]
                dws[0][...] = (total + dwbuf[0].astype(F32) if added else total).astype(BF)
                continue
            planes, _, shard, _ = w_ref.shape
            for plane in range(planes):
                row = pl.multiple_of((plane * n + (c ^ d)) * shard, shard)
                total = acc_ref[pl.ds(row, shard)]
                if added:
                    total = total + dwbuf[d, plane].astype(F32)
                dws[d][plane] = total.astype(BF)


def experts_call(
    xs, dys, micro, place, router, weights, first, count, before, dws_before
):
    steps = len(xs) // 2
    half, width = xs[0].shape
    tile = 2 * half
    n = len(weights)
    joined = n == 1
    block = weights[0].shape
    whole_shape = block if joined else block[:1] + (n,) + block[1:]
    lanes = block[-1]
    out_block = pl.BlockSpec((1, half, width), lambda i: (i, 0, 0))
    dx_block = pl.BlockSpec((1, half, width + 128), lambda i: (i, 0, 0))
    whole = pl.BlockSpec(memory_space=pltpu.VMEM)
    anywhere = pl.BlockSpec(memory_space=pl.ANY)
    blocks = [out_block, out_block, dx_block, dx_block]
    rows = steps * tile
    return pl.pallas_call(
        functools.partial(
            experts_kernel, steps, first, count, micro, bool(before), bool(dws_before), joined
        ),
        grid=(steps,),
        in_specs=[
            pl.BlockSpec(memory_space=pltpu.SMEM),
            pl.BlockSpec((width, 128), lambda i: (0, 0)),
        ]
        + [anywhere] * (4 * steps + n)
        + (blocks if before else [])
        + [anywhere] * len(dws_before),
        out_specs=blocks + [whole] * n,
        out_shape=[jax.ShapeDtypeStruct((steps, half, width), BF)] * 2
        + [jax.ShapeDtypeStruct((steps, half, width + 128), BF)] * 2
        + [jax.ShapeDtypeStruct(block, BF)] * n,
        scratch_shapes=[
            pltpu.VMEM((width, lanes), F32),
            pltpu.VMEM(whole_shape, BF),
            pltpu.VMEM((2, tile, width), BF),
            pltpu.VMEM((2, tile, width + 128), BF),
            pltpu.VMEM(((n if dws_before else 1),) + (block if dws_before else (16, 128)), BF),
            pltpu.SemaphoreType.DMA((2, 4)),
            pltpu.SemaphoreType.DMA((n,)),
            pltpu.SemaphoreType.DMA((n,)),
        ],
        compiler_params=params("arbitrary"),
        cost_estimate=pl.CostEstimate(
            flops=6 * rows * width * lanes,
            bytes_accessed=8 * rows * width + 4 * width * lanes,
            transcendentals=rows * lanes // 3,
        ),
        name="experts",
    )(place, router, *xs, *dys, *weights, *(before or []), *dws_before)


def back_kernel(dq_ref, x_ref, cos_ref, sin_ref, wq_ref, wkv_ref, *refs):
    *terms, dkv_ref, part_ref, gain_ref = refs
    total = functools.reduce(jnp.add, [t[...].astype(F32) for t in terms])
    kw = total.shape[1] // 2
    dk = turn(total[:, :kw], cos_ref[...], -sin_ref[...]).astype(BF)
    dkv = jnp.concatenate([dk, total[:, kw:].astype(BF)], axis=1)
    dkv_ref[...] = dkv
    part = dot(dq_ref[...], wq_ref[...], 1, 1) + dot(dkv, wkv_ref[...], 1, 1)
    part_ref[...] = part.astype(BF)
    x = x_ref[...].astype(F32)
    unit = x * lax.rsqrt(jnp.mean(x * x, axis=1, keepdims=True) + EPS)
    sums = jnp.broadcast_to(jnp.sum(part * unit, axis=0, keepdims=True), gain_ref.shape)

    @pl.when(pl.program_id(0) == 0)
    def _():
        gain_ref[...] = sums

    @pl.when(pl.program_id(0) > 0)
    def _():
        gain_ref[...] += sums


def back_call(dq, terms, x, micro, cosine, sine, w_qo, w_kv):
    rows, qw = dq.shape
    lanes = terms[0].shape[1]
    d = w_qo.shape[0]
    tile = min(256, cosine.shape[0])
    per = cosine.shape[0] // tile
    row = lambda width: pl.BlockSpec((tile, width), lambda i: (i, 0))
    table = pl.BlockSpec((tile, 128), lambda i: (i % per, 0))
    return pl.pallas_call(
        back_kernel,
        grid=(rows // tile,),
        in_specs=[
            row(qw),
            pl.BlockSpec((tile, d), lambda i: (i + micro * (rows // tile), 0)),
            table,
            table,
            pl.BlockSpec((d, qw), lambda i: (0, 0)),
            pl.BlockSpec((d, lanes), lambda i: (0, 0)),
        ]
        + [row(lanes)] * len(terms),
        out_specs=[row(lanes), row(d), pl.BlockSpec((8, d), lambda i: (0, 0))],
        out_shape=[
            jax.ShapeDtypeStruct((rows, lanes), BF),
            jax.ShapeDtypeStruct((rows, d), BF),
            jax.ShapeDtypeStruct((8, d), F32),
        ],
        compiler_params=params("arbitrary"),
        cost_estimate=pl.CostEstimate(
            flops=2 * rows * d * (qw + lanes), bytes_accessed=8 * rows * d, transcendentals=0
        ),
        name="back",
    )(dq, x, cosine, sine, w_qo, w_kv, *terms)


def grads_kernel(pairs, starts, extra, place_ref, *refs):
    refs = list(refs)
    sides = [[(refs.pop(0), refs.pop(0)) for _ in range(count)] for count in pairs]
    more = refs.pop(0) if extra else None
    count = len(refs)
    block = refs[0].shape[0]
    for s in range(count):
        at = pl.ds(pl.multiple_of((place_ref[0] ^ s) * block, block), block)
        column = 0
        for side, firsts in zip(sides, starts):
            total = functools.reduce(
                jnp.add,
                [
                    dot(left[first : first + right.shape[0], at], right[...], 0, 0)
                    for (left, right), first in zip(side, firsts)
                ],
            )
            refs[s][:, column : column + total.shape[1]] = total.astype(BF)
            column += total.shape[1]
        if extra:
            refs[s][:, column:] = more[at, :]


def grads_call(me, sides, extra, count):
    d = sides[0][0][0].shape[1]
    lanes = sum(side[0][1].shape[1] for side in sides) + (0 if extra is None else extra.shape[1])
    whole = pl.BlockSpec(memory_space=pltpu.VMEM)
    operands = [a for side in sides for term in side for a in term[:2]]
    starts = [[term[2] for term in side] for side in sides]
    operands += [] if extra is None else [extra]
    return pl.pallas_call(
        functools.partial(grads_kernel, [len(side) for side in sides], starts, extra is not None),
        in_specs=[pl.BlockSpec(memory_space=pltpu.SMEM)] + [whole] * len(operands),
        out_specs=[whole] * count,
        out_shape=[jax.ShapeDtypeStruct((d // count, lanes), BF)] * count,
        compiler_params=pltpu.CompilerParams(vmem_limit_bytes=VMEM_LIMIT),
        cost_estimate=pl.CostEstimate(
            flops=2 * d * lanes * 1024, bytes_accessed=4 * d * lanes, transcendentals=0
        ),
        name="grads",
    )(me, *operands)


def line_kernel(count, place_ref, *refs):
    terms, outs, scratch = refs[:-count - 1], refs[-count - 1 : -1], refs[-1]
    scratch[...] = functools.reduce(jnp.add, [t[...].astype(F32) for t in terms])
    shard = outs[0].shape[0]
    for s in range(count):
        row = pl.multiple_of((place_ref[0] ^ s) * shard, shard)
        outs[s][...] = scratch[pl.ds(row, shard)].astype(BF)


def line_call(me, terms, count):
    rows, lanes = terms[0].shape
    whole = pl.BlockSpec(memory_space=pltpu.VMEM)
    return pl.pallas_call(
        functools.partial(line_kernel, count),
        in_specs=[pl.BlockSpec(memory_space=pltpu.SMEM)] + [whole] * len(terms),
        out_specs=[whole] * count,
        out_shape=[jax.ShapeDtypeStruct((rows // count, lanes), BF)] * count,
        scratch_shapes=[pltpu.VMEM((rows, lanes), F32)],
        compiler_params=pltpu.CompilerParams(vmem_limit_bytes=VMEM_LIMIT),
        name="line",
    )(me, *terms)


def reorder_heads(values):
    parts = []
    for at in range(0, values.shape[1], 256):
        a = values[:, at : at + 128]
        b = values[:, at + 128 : at + 256]
        low = lax.broadcasted_iota(jnp.int32, a.shape, 1) < HD
        parts += [
            jnp.where(low, a, pltpu.roll(b, HD, 1)),
            jnp.where(low, pltpu.roll(a, HD, 1), b),
        ]
    return jnp.concatenate(parts, axis=1)


def finish_kernel(count, *refs):
    early = functools.reduce(jnp.add, [r[...].astype(F32) for r in refs[:count]])
    late = functools.reduce(jnp.add, [r[...].astype(F32) for r in refs[count : 2 * count]])
    q_ref, k_ref, v_ref, o_ref, small_ref = refs[2 * count :]
    qw = q_ref.shape[1]
    kw = k_ref.shape[1]
    q_ref[...] = reorder_heads(early[:, :qw])
    o_ref[...] = reorder_heads(early[:, qw:])
    k_ref[...] = late[:, :kw]
    v_ref[...] = late[:, kw : 2 * kw]
    small_ref[...] = late[:, 2 * kw :]


def finish_call(early, late, qw, kw):
    shard = early[0].shape[0]
    whole = pl.BlockSpec(memory_space=pltpu.VMEM)
    return pl.pallas_call(
        functools.partial(finish_kernel, len(early)),
        in_specs=[whole] * (2 * len(early)),
        out_specs=[whole] * 5,
        out_shape=[
            jax.ShapeDtypeStruct((shard, w), F32) for w in (qw, kw, kw, qw, 128)
        ],
        name="finish",
    )(*early, *late)


def expert_rows_kernel(count, place_ref, *refs):
    pieces, outs = refs[:-3], refs[-3:]
    groups = 2
    units = outs[0].shape[2]
    group = outs[0].shape[0] // (count * groups)
    for g in range(groups):
        for s in range(count):
            piece = pieces[g * count + s]
            at = ((place_ref[0] ^ s) * groups + g) * group
            for i in range(3):
                for e in range(group):
                    lanes = (i * group + e) * units
                    outs[i][at + e] = piece[:, lanes : lanes + units].astype(F32)


def expert_rows_call(me, pieces, experts, units):
    shard = pieces[0].shape[0]
    whole = pl.BlockSpec(memory_space=pltpu.VMEM)
    return pl.pallas_call(
        functools.partial(expert_rows_kernel, len(pieces) // 2),
        in_specs=[pl.BlockSpec(memory_space=pltpu.SMEM)] + [whole] * len(pieces),
        out_specs=[whole] * 3,
        out_shape=[jax.ShapeDtypeStruct((experts, shard, units), F32)] * 3,
        compiler_params=pltpu.CompilerParams(vmem_limit_bytes=VMEM_LIMIT),
        name="expert_rows",
    )(me, *pieces)


def apart(count, step):
    return [(i, i ^ step) for i in range(count)]


def swap(value):
    return lax.ppermute(value, "mp", [(0, 1), (1, 0)])


def up_hop(value, n, s):
    return lax.ppermute(value, "ctx", [(c, c + 1) for c in range(s, n - 1)])


def add(*terms):
    return functools.reduce(jnp.add, [t.astype(F32) for t in terms]).astype(BF)


def by_xor(parts, me):
    bit = 1
    while bit < len(parts):
        flip = (me & bit) != 0
        parts = [jnp.where(flip, parts[i ^ bit], parts[i]) for i in range(len(parts))]
        bit *= 2
    return parts


def exchange(parts, axis):
    count = len(parts)
    return [parts[0]] + [
        lax.ppermute(parts[s], axis, apart(count, s)) for s in range(1, count)
    ]


def from_last(values, start, count):
    values = values[::-1]
    return lax.dynamic_slice_in_dim(jnp.concatenate([values, values]), start, count, 0)


def head_order(weight):
    rows, width = weight.shape
    return (
        weight.reshape(rows, width // (4 * HD), 2, 2, HD).swapaxes(2, 3).reshape(rows, width)
    )


def per_device(
    tokens,
    cotangent,
    routes,
    norm_gain,
    w_query,
    w_key,
    w_value,
    w_output,
    ffn_gain,
    w_router,
    w_gate,
    w_up,
    w_down,
):
    micro, seq_count, local, width = tokens.shape
    top = routes.shape[3]
    experts, shard, units = w_gate.shape
    dp = lax.axis_size("dp")
    n = lax.axis_size("ctx")
    hops = n == 4
    me_dp = lax.axis_index("dp")
    me_ctx = lax.axis_index("ctx")
    me_mp = lax.axis_index("mp")
    mine_count = experts // dp
    group = mine_count // 2
    micros = range(micro)
    per = seq_count * local
    half = per // 2
    rows = micro * per
    qw = w_query.shape[1]
    kw = w_key.shape[1]
    ctx_now = me_ctx.astype(jnp.int32).reshape(1)
    dp_now = me_dp.astype(jnp.int32).reshape(1)
    place = jnp.stack([me_dp * mine_count, me_ctx]).astype(jnp.int32)

    def in_order(mine, other):
        first = me_mp == 0
        return jnp.concatenate([jnp.where(first, mine, other), jnp.where(first, other, mine)])

    def halves(full):
        cut = full.reshape(2, half, full.shape[1])
        mine = lax.dynamic_index_in_dim(cut, me_mp, 0, keepdims=False)
        return mine, lax.dynamic_index_in_dim(cut, 1 - me_mp, 0, keepdims=False)

    def far_pieces(mine, steps=range(1, dp)):
        return [lax.ppermute(mine, "dp", apart(dp, s)) for s in steps]

    def paired(mine, far, other, near):
        return [piece for pair in zip([mine] + far, [other] + near) for piece in pair]

    def gather_line(value):
        return jnp.stack(
            [value] + [lax.ppermute(value, "ctx", apart(n, s)) for s in range(1, n)]
        )

    def gather_plane(value):
        return [value] + [lax.ppermute(value, "dp", apart(dp, s)) for s in range(1, dp)]

    def whole_rows(pieces):
        lines = by_xor(pieces, me_dp)
        full = jnp.stack(lines)
        cols = by_xor([full[:, i] for i in range(n)], me_ctx)
        return jnp.stack(cols, axis=1).reshape(dp * n * shard, full.shape[3])

    live = {}

    def seal(**values):
        live.update(values)
        live.update(lax.optimization_barrier(live))

    small = jnp.concatenate([w_router, norm_gain[:, None], ffn_gain[:, None]], axis=1)
    small = jnp.pad(small, ((0, 0), (0, 128 - small.shape[1])))
    kv_shard = jnp.concatenate([w_key, w_value, small], axis=1)
    qo_shard = jnp.concatenate([head_order(w_query), head_order(w_output)], axis=1)
    if hops:
        kv_line = gather_line(kv_shard)
        qo_line = gather_line(qo_shard)

    def own_experts(gate_up_down):
        cut = [w.reshape(dp, 2, group, shard, units) for w in gate_up_down]
        side = jnp.concatenate([w[:, :, e] for w in cut for e in range(group)], axis=3)
        parts = exchange(by_xor([side[i] for i in range(dp)], me_dp), "dp")
        parts = by_xor(parts, me_dp)
        return [jnp.stack([p[g] for p in parts]) for g in range(2)]

    def weight_send(g, *steps):
        if hops:
            for s in steps:
                at, hop = (2, 1) if s == 3 else (0, s)
                live["weights"][g][s] = lax.ppermute(live["weights"][g][at], "ctx", apart(n, hop))

    def seal_but(under_way, **values):
        kept = [(d, {k: d.pop(k) for k in keys if k in d}) for d, keys in under_way()]
        seal(**values)
        for (d, keys), (_, taken) in zip(under_way(), kept):
            d.update(taken)

    if hops:
        seal_but(
            lambda: [(live, ["qo_line"])],
            kv_line=kv_line,
            qo_line=qo_line,
            raw=[w_gate, w_up, w_down],
            x=tokens,
            dy=cotangent,
            routes=routes,
        )
        kv_pieces = gather_plane(live.pop("kv_line"))
        seal(kv_pieces=kv_pieces)
        kv_full = whole_rows(live.pop("kv_pieces"))
        qo_pieces = gather_plane(live.pop("qo_line"))
    else:
        kv_full = lax.all_gather(kv_shard, ("dp", "ctx"), axis=0, tiled=True)
        qo_full = lax.all_gather(qo_shard, ("dp", "ctx"), axis=0, tiled=True)
        own3 = own_experts([w_gate, w_up, w_down])
        own3 = [lax.all_gather(o, "ctx", axis=1, tiled=False) for o in own3]
        own3 = [{0: o.reshape(width, o.shape[-1])} for o in own3]
        seal(weights=own3, x=tokens, dy=cotangent, routes=routes)
    small = kv_full[:, 2 * kw :]
    router = small[:, :experts]
    router_wide = jnp.pad(router, ((0, 0), (0, 128 - experts)))
    gain_one = small[:, experts].astype(F32)[None, :]
    gain_two = small[:, experts + 1].astype(F32)[None, :]

    position = me_ctx * local + jnp.arange(local, dtype=jnp.int32)
    freqs = THETA ** (-(jnp.arange(HD // 2, dtype=F32) * 2.0) / HD)
    angles = position.astype(F32)[:, None] * freqs[None, :]
    cosine = jnp.tile(jnp.cos(angles), (1, 4))
    sine = jnp.sin(angles)
    sine = jnp.concatenate([-sine, sine, -sine, sine], axis=1)
    live["x"] = live["x"].reshape(rows, width)
    live["dy"] = live["dy"].reshape(rows, width)
    normed, kv = kv_call(live["x"], gain_one, kv_full, 2 * kw, cosine, sine)
    kv = kv.reshape(1, micro * seq_count, local, 2 * kw)

    ids = live.pop("routes").reshape(rows, top)
    marks = jnp.sum(
        (ids[:, :, None] == jnp.arange(128, dtype=jnp.int32)[None, None, :]).astype(F32), axis=1
    ).astype(BF)
    dyx = jnp.concatenate([live["dy"], marks], axis=1)
    dyx = dyx.reshape(micro, 2, half, width + 128)
    dy_cut = [
        lax.dynamic_index_in_dim(dyx, at, 1, keepdims=False) for at in (me_mp, 1 - me_mp)
    ]

    if hops:
        kv_got = up_hop(kv, n, 0)
        seal(
            kv=kv,
            kv_prev=[kv_got],
            qo_pieces=qo_pieces,
            normed=normed,
            dy_cut=dy_cut,
            marks=marks[:, :experts],
            kv_full=kv_full,
            cosine=cosine,
            sine=sine,
            router=router,
            router_wide=router_wide,
            gain_one=gain_one,
            gain_two=gain_two,
        )
        qo_full = whole_rows(live.pop("qo_pieces"))
    else:
        every = lax.all_gather(kv[0], "ctx", axis=0, tiled=False)
        seal(
            kv=kv,
            kv_prev=[from_last(every, n - me_ctx, n - 1)],
            normed=normed,
            dy_cut=dy_cut,
            marks=marks[:, :experts],
            kv_full=kv_full,
            cosine=cosine,
            sine=sine,
            router=router,
            router_wide=router_wide,
            gain_one=gain_one,
            gain_two=gain_two,
        )
    live.update(qo_full=qo_full, dy_far={}, dy_near={})
    q = q_call(live["normed"], qo_full, qw, live["cosine"], live["sine"])
    live["q"] = q.reshape(micro * seq_count, local, qw)

    def dy_send(steps):
        for s in steps:
            live["dy_far"][s] = lax.ppermute(live["dy_cut"][0], "dp", apart(dp, s))

    def attend(first, s, done):
        return attn_part(
            ctx_now,
            live["q"],
            live["kv"] if first else None,
            [live["kv_prev"][s - 1]],
            s,
            None if first else live.pop("carry"),
            done,
        )

    def mix(attn):
        return dot(attn.reshape(rows, qw), live["qo_full"][:, qw:], 1, 1).astype(BF)

    if hops:
        dy_send((1, 2))
        got = up_hop(live["kv_prev"][-1], n, 1)
        carry = attend(True, 1, False)
        live["kv_prev"].append(got)
        seal(carry=carry)
        weights = [{0: own} for own in own_experts(live.pop("raw"))]
        got = up_hop(live["kv_prev"][-1], n, 2)
        carry = attend(False, 2, False)
        live["kv_prev"].append(got)
        seal(carry=carry, weights=weights)
        weight_send(0, 1, 2)
        dy_send((3,))
        attn, lse = attend(False, 3, True)
    else:
        attn, lse = attend(True, 1, True)
        dy_send(range(1, dp))
    live["dy_near"] = {s: swap(live["dy_far"][s]) for s in (1, 2)}
    late = lambda: [(live["weights"][0], [1, 2]), (live["dy_far"], [3])]
    seal_but(late, attn=attn, lse=lse, mixed=mix(attn))

    mixed_got = swap(live["mixed"])
    hidden = live["x"].astype(F32) + (live.pop("mixed").astype(F32) + mixed_got.astype(F32))
    inv_two = lax.rsqrt(jnp.mean(hidden * hidden, axis=1, keepdims=True) + EPS)
    ffn_low = (hidden * inv_two * live["gain_two"]).astype(BF)
    x_cut = [halves(ffn_low[m * per : (m + 1) * per]) for m in micros]

    late = lambda: [(live["weights"][0], [1, 2]), (live["dy_far"], [3])]
    seal_but(late, hidden=hidden, inv_two=inv_two, ffn_low=ffn_low, x_cut=x_cut)
    first = far_pieces(live["x_cut"][0][0], (1, 2))
    live["x_far"] = [first] + [[]] * (micro - 1)
    seal()
    live["x_far"][0] = live["x_far"][0] + far_pieces(live["x_cut"][0][0], (3,))
    weight_send(0, 3)
    live["dy_near"][3] = swap(live["dy_far"][3])
    seal()
    live["x_near"] = [[swap(f) for f in live["x_far"][0]]] + [[]] * (micro - 1)
    seal()
    live.update(sums=[], dws=[[], []], parts=[])

    def run(g, m, before):
        weights = [live["weights"][g][s] for s in sorted(live["weights"][g])]
        x_cut, dy_cut = live["x_cut"][m], live["dy_cut"]
        xs = paired(x_cut[0], live["x_far"][m], x_cut[1], live["x_near"][m])
        dys = paired(
            dy_cut[0],
            [live["dy_far"][s] for s in range(1, dp)],
            dy_cut[1],
            [live["dy_near"][s] for s in range(1, dp)],
        )
        part = experts_call(
            xs,
            dys,
            m,
            place,
            live["router_wide"],
            weights,
            g * group,
            group,
            before,
            live["dws"][g],
        )
        live["dws"][g] = part[4:]
        return list(part[:4])

    live["x_far"][1] = far_pieces(live["x_cut"][1][0])
    weight_send(1, 1, 2)
    live["sums"].append(run(0, 0, None))
    seal()
    live["x_near"][1] = [swap(f) for f in live["x_far"][1]]
    seal()
    weight_send(1, 3)
    live["sums"].append(run(0, 1, None))
    seal()

    live.update(rows=[{}, {}])

    def grad_send(g, *steps):
        if hops:
            for s in steps:
                live["rows"][g][s] = lax.ppermute(live["dws"][g][s], "ctx", apart(n, s))

    def grad_own(g):
        if hops:
            own = add(live["dws"][g][0], *live["rows"][g].values())
        else:
            whole = live["dws"][g][0].reshape(dp, n, shard, -1)
            own = lax.psum_scatter(whole, "ctx", scatter_dimension=1, tiled=False)
        return exchange(by_xor([own[i] for i in range(dp)], me_dp), "dp")

    def terms_of(mine, got):
        return [add(mine[s], got[s]) for s in range(dp)]

    live.update(dx_terms=[None] * micro, dx_back=[None] * micro)
    live.update(out_terms=[None] * micro, out_back={})

    def dx_terms(m):
        part = live["parts"][m]
        live["dx_terms"][m] = terms_of(part[2], swap(part[3]))

    def dx_send(m):
        live["dx_back"][m] = exchange(live["dx_terms"][m], "dp")

    def out_terms(m):
        part = live["parts"][m]
        live["out_terms"][m] = terms_of(part[0], swap(part[1]))

    def out_send(m):
        live["out_back"][m] = exchange(live["out_terms"][m], "dp")

    grad_send(0, 1, 2)
    live["parts"].append(run(1, 0, live["sums"][0]))
    seal()
    dx_terms(0)
    seal()
    dx_send(0)
    grad_send(0, 3)
    live["parts"].append(run(1, 1, live.pop("sums")[1]))
    seal()

    cut = lambda whole, m: whole[m * per : (m + 1) * per]
    live.update({name: [None] * micro for name in ("dh", "dz", "d_attn", "dq", "dkv")})
    live.update(dkv_sum=[{} for _ in micros])
    live.update(router_sums=[None] * micro, gain_sums=[None] * micro)

    def before_attention(m):
        total = add(*live["dx_back"][m])
        moe = in_order(total, swap(total)).astype(F32)
        low = cut(live["ffn_low"], m)
        inv = cut(live["inv_two"], m)
        dgate = moe[:, width : width + experts]
        gate = masked_softmax(
            dot(low, live["router"], 1, 0), cut(live["marks"], m).astype(F32) > 0.5
        )
        dlogit = gate * (dgate - jnp.sum(gate * dgate, axis=1, keepdims=True))
        dlogit = dlogit.astype(BF)
        live["router_sums"][m] = dot(low, dlogit, 0, 0)
        d_ffn = moe[:, :width] + dot(dlogit, live["router"], 1, 1)
        unit = cut(live["hidden"], m) * inv
        live["gain_sums"][m] = jnp.sum(d_ffn * unit, axis=0)
        g_two = d_ffn * live["gain_two"]
        dh = cut(live["dy"], m).astype(F32) + inv * (
            g_two - unit * jnp.mean(g_two * unit, axis=1, keepdims=True)
        )
        dz = dh.astype(BF)
        live["dh"][m] = dh
        live["dz"][m] = dz
        live["d_attn"][m] = dot(dz, live["qo_full"][:, qw:], 1, 0).astype(BF)

    def attention_back(m):
        dq, *dkv = attn_bwd(
            ctx_now,
            live["q"],
            live["d_attn"][m].reshape(seq_count, local, qw),
            live["attn"],
            live["lse"],
            live["cosine"],
            live["sine"],
            live["kv"],
            live["kv_prev"],
            m * seq_count,
        )
        live["dq"][m] = dq.reshape(per, qw)
        live["dkv"][m] = dkv

    def dkv_send(m, *steps):
        if hops:
            for d in steps:
                live["dkv_sum"][m][d] = lax.ppermute(
                    live["dkv"][m][d], "ctx", [(c, c - d) for c in range(d, n)]
                )

    def back(m):
        if hops:
            terms = [live["dkv"][m][0], *live["dkv_sum"][m].values()]
        else:
            every = from_last(jnp.concatenate(live["dkv"][m]), n - 1 - me_ctx, n)
            terms = [lax.psum_scatter(every, "ctx", scatter_dimension=0, tiled=True)]
        terms = [t.reshape(per, 2 * kw) for t in terms]
        return back_call(
            live["dq"][m],
            terms,
            live["x"],
            m,
            live["cosine"],
            live["sine"],
            live["qo_full"],
            live["kv_full"],
        )

    def out_total(m):
        total = add(*live["out_back"][m])
        moe = in_order(total, swap(total)).astype(F32)
        return (cut(live["hidden"], m) + moe).astype(BF)

    def early_send(*steps):
        if hops:
            for s in steps:
                live["early"][s] = lax.ppermute(live["early"][s], "dp", apart(dp, s))

    before_attention(0)
    dx_terms(1)
    grad_send(1, 1, 2)
    out_terms(0)
    seal_but(lambda: [(live["rows"][1], [1, 2])])
    dx_send(1)
    attention_back(0)
    seal()
    dkv_send(0, 1, 3)
    out_send(0)
    before_attention(1)
    out_terms(1)
    seal_but(lambda: [(live["out_back"], [0])])
    dkv_send(0, 2)
    out_send(1)
    attention_back(1)
    seal()
    dkv_send(1, 1, 2, 3)
    pieces_now = dp_now if hops else jnp.zeros((1,), jnp.int32)
    early = grads_call(
        pieces_now,
        [
            [(live["normed"], live["dq"][m], m * per) for m in micros],
            [(jnp.concatenate(live["dz"]), live["attn"].reshape(rows, qw), 0)],
        ],
        None,
        dp,
    )
    owned = [grad_own(0)]
    seal_but(lambda: [(live["dkv_sum"][1], [1, 2, 3])], early=list(early), owned=owned)
    early_send(1, 2, 3)
    dkv_first, part_first, gain_first = back(0)
    got_first = swap(part_first)
    out_first = out_total(0)
    out_last = out_total(1)
    seal(
        got=[got_first],
        output=[out_first, out_last],
        dkv_final=[dkv_first],
        part=[part_first],
        gain_one_sums=[gain_first],
    )
    grad_send(1, 3)
    dkv_last, part_last, gain_last = back(1)
    live["dkv_final"].append(dkv_last)
    live["part"].append(part_last)
    small = jnp.concatenate(
        [
            live["router_sums"][0] + live["router_sums"][1],
            (live["gain_one_sums"][0] + gain_last)[0][:, None],
            (live["gain_sums"][0] + live["gain_sums"][1])[:, None],
        ],
        axis=1,
    )
    small = jnp.pad(small, ((0, 0), (0, 128 - small.shape[1]))).astype(BF)
    late = grads_call(
        pieces_now,
        [[(live["normed"], live["dkv_final"][m], m * per) for m in micros]],
        small,
        dp,
    )
    got_last = swap(part_last)
    seal_but(
        lambda: [(live["rows"][1], [3])], late=late, got=live["got"] + [got_last]
    )
    early, late = live["early"], live["late"]
    if hops:
        late = exchange(late, "dp")
        early = line_call(ctx_now, early, n)
    d_normed = jnp.concatenate(
        [p.astype(F32) + g.astype(F32) for p, g in zip(live["part"], live["got"])]
    )
    x32 = live["x"].astype(F32)
    inv_one = lax.rsqrt(jnp.mean(x32 * x32, axis=1, keepdims=True) + EPS)
    n_one = x32 * inv_one
    g_one = d_normed * live["gain_one"]
    input_grad = (
        jnp.concatenate(live["dh"])
        + inv_one * (g_one - n_one * jnp.mean(g_one * n_one, axis=1, keepdims=True))
    ).astype(BF)
    seal_but(
        lambda: [(live["rows"][1], [3])], late=late, early=early, input_grad=input_grad
    )
    early, late = live["early"], live["late"]
    if hops:
        late = exchange(line_call(ctx_now, late, n), "ctx")
        early = exchange(early, "ctx")
    else:
        early, late = (
            [
                lax.psum_scatter(
                    jnp.concatenate(p), ("dp", "ctx"), scatter_dimension=0, tiled=True
                )
            ]
            for p in (early, late)
        )
    owned = [live["owned"][0], grad_own(1)]
    output = jnp.concatenate(live["output"])
    grad_q, grad_k, grad_v, grad_o, small_grad = finish_call(early, late, qw, kw)
    gain_part = small_grad[:, experts]
    dw_gate, dw_up, dw_down = expert_rows_call(dp_now, owned[0] + owned[1], experts, units)
    shape = tokens.shape
    return (
        output.reshape(shape),
        live["input_grad"].reshape(shape),
        gain_part + swap(gain_part),
        grad_q,
        grad_k,
        grad_v,
        grad_o,
        small_grad[:, experts + 1],
        small_grad[:, :experts],
        dw_gate,
        dw_up,
        dw_down,
    )


def solution(mesh):
    rows = P(None, "dp", "ctx", None)
    vector = P(("dp", "ctx"))
    matrix = P(("dp", "ctx"), "mp")
    router = P(("dp", "ctx"), None)
    expert = P(None, ("dp", "ctx"), "mp")
    return jax.shard_map(
        per_device,
        mesh=mesh,
        in_specs=(
            rows,
            rows,
            rows,
            vector,
            matrix,
            matrix,
            matrix,
            matrix,
            vector,
            router,
            expert,
            expert,
            expert,
        ),
        out_specs=(
            rows,
            rows,
            vector,
            matrix,
            matrix,
            matrix,
            matrix,
            vector,
            router,
            expert,
            expert,
            expert,
        ),
        check_vma=False,
    )
```

```python
import functools
import math

import jax
import jax.numpy as jnp
from jax import lax
from jax.experimental import pallas as pl
from jax.experimental.pallas import tpu as pltpu
from jax.sharding import PartitionSpec as P

HD = 64
EPS = 1e-06
THETA = 10000.0
NEG = -1e30
VMEM_LIMIT = 60 * 1024 * 1024
BF = jnp.bfloat16
F32 = jnp.float32


def dot(a, b, ca, cb, precision=None):
    return lax.dot_general(
        a, b, (((ca,), (cb,)), ((), ())), preferred_element_type=F32, precision=precision
    )


def params(*semantics):
    return pltpu.CompilerParams(dimension_semantics=semantics, vmem_limit_bytes=VMEM_LIMIT)


def turn(values, cosine, sine):
    width = values.shape[1]
    lane = lax.broadcasted_iota(jnp.int32, values.shape, 1)
    ahead = pltpu.roll(values, width - HD // 2, 1)
    behind = pltpu.roll(values, HD // 2, 1)
    swapped = jnp.where(lane % HD < HD // 2, ahead, behind)
    reps = width // cosine.shape[1]
    return values * jnp.tile(cosine, (1, reps)) + swapped * jnp.tile(sine, (1, reps))


def kv_kernel(x_ref, gain_ref, w_ref, cos_ref, sin_ref, normed_ref, kv_ref):
    x = x_ref[...].astype(F32)
    inv = lax.rsqrt(jnp.mean(x * x, axis=1, keepdims=True) + EPS)
    normed = (x * inv * gain_ref[...]).astype(BF)
    normed_ref[...] = normed
    kw = kv_ref.shape[1] // 2
    raw = dot(normed, w_ref[...], 1, 0)
    kv_ref[:, :kw] = turn(raw[:, :kw], cos_ref[...], sin_ref[...]).astype(BF)
    kv_ref[:, kw:] = raw[:, kw:].astype(BF)


def q_kernel(normed_ref, w_ref, cos_ref, sin_ref, q_ref):
    raw = dot(normed_ref[...], w_ref[...], 1, 0)
    q_ref[...] = turn(raw, cos_ref[...], sin_ref[...]).astype(BF)


def row_specs(rows, local, d, lanes):
    tile = min(256, local)
    per = local // tile
    return (
        rows // tile,
        pl.BlockSpec((tile, d), lambda i: (i, 0)),
        pl.BlockSpec((d, lanes), lambda i: (0, 0)),
        pl.BlockSpec((tile, 128), lambda i: (i % per, 0)),
        pl.BlockSpec((tile, lanes), lambda i: (i, 0)),
        pl.CostEstimate(
            flops=2 * rows * d * lanes, bytes_accessed=6 * rows * d, transcendentals=rows
        ),
    )


def kv_call(x, gain, w, lanes, cosine, sine):
    rows, d = x.shape
    steps, row, weight, table, out, cost = row_specs(rows, cosine.shape[0], d, lanes)
    return pl.pallas_call(
        kv_kernel,
        grid=(steps,),
        in_specs=[row, pl.BlockSpec((1, d), lambda i: (0, 0)), weight, table, table],
        out_specs=[row, out],
        out_shape=[
            jax.ShapeDtypeStruct((rows, d), BF),
            jax.ShapeDtypeStruct((rows, lanes), BF),
        ],
        compiler_params=params("arbitrary"),
        cost_estimate=cost,
        name="kv",
    )(x, gain, w, cosine, sine)


def q_call(normed, w, lanes, cosine, sine):
    rows, d = normed.shape
    steps, row, weight, table, out, cost = row_specs(rows, cosine.shape[0], d, lanes)
    return pl.pallas_call(
        q_kernel,
        grid=(steps,),
        in_specs=[row, weight, table, table],
        out_specs=out,
        out_shape=jax.ShapeDtypeStruct((rows, lanes), BF),
        compiler_params=params("arbitrary"),
        cost_estimate=cost,
        name="q",
    )(normed, w, cosine, sine)


def half_mask(block, which):
    lane = lax.broadcasted_iota(jnp.int32, block.shape, 1)
    keep = (lane < HD) if which == 0 else (lane >= HD)
    return jnp.where(keep, block, jnp.zeros_like(block))


def stacked(ref):
    return jnp.concatenate([ref[0, :, :128], ref[0, :, 128:]], axis=0)


def causal(shape, length):
    key = lax.broadcasted_iota(jnp.int32, shape, 0)
    query = lax.broadcasted_iota(jnp.int32, shape, 1) % length
    return key <= query


def each_earlier(c, counts, visit, otherwise=None, first=1):
    for piece, count in enumerate(counts):
        if count == 1:

            @pl.when(c >= first)
            def _():
                visit(piece, 0)

            if otherwise is not None:

                @pl.when(c < first)
                def _():
                    otherwise(piece, 0)

        else:
            reach = jnp.clip(c - first + 1, 0, count)

            @pl.loop(0, reach)
            def _(entry):
                visit(piece, entry)

            if otherwise is not None:

                @pl.loop(reach, count)
                def _(entry):
                    otherwise(piece, entry)

        first += count


def attn_part_kernel(counts, start, first, last, ctx_ref, q_ref, *refs):
    refs = list(refs)
    pieces = len(counts) + first
    keys = [refs.pop(0) for _ in range(pieces)]
    vals = [refs.pop(0) for _ in range(pieces)]
    old = None if first else [refs.pop(0) for _ in range(2)]
    if last:
        o_ref, lse_ref, stats_ref, acc_ref = refs
    else:
        stats_ref, acc_ref = (ref.at[0, 0] for ref in refs)
    length = q_ref.shape[1]
    both = (stacked(q_ref).astype(F32) * HD**-0.5).astype(BF)
    c = ctx_ref[0]

    if first:
        k = keys[0][0, 0]
        v = vals[0][0, 0]
        for i in range(2):
            s = dot(half_mask(k, i), both, 1, 1)
            s = jnp.where(causal(s.shape, length), s, NEG)
            peak = jnp.max(s, axis=0, keepdims=True)
            p = jnp.exp(s - peak)
            stats_ref[i : i + 1] = peak
            stats_ref[i + 2 : i + 3] = jnp.sum(p, axis=0, keepdims=True)
            acc_ref[i] = dot(v, p.astype(BF), 0, 0)
    else:
        stats_ref[...] = old[0][0, 0]
        acc_ref[...] = old[1][0, 0]

    def visit(piece, entry):
        k = keys[piece + first][entry, 0]
        v = vals[piece + first][entry, 0]
        for i in range(2):
            s = dot(half_mask(k, i), both, 1, 1)
            peak = stats_ref[i : i + 1]
            now = jnp.maximum(peak, jnp.max(s, axis=0, keepdims=True))
            p = jnp.exp(s - now)
            factor = jnp.exp(peak - now)
            stats_ref[i : i + 1] = now
            stats_ref[i + 2 : i + 3] = stats_ref[i + 2 : i + 3] * factor + jnp.sum(
                p, axis=0, keepdims=True
            )
            acc_ref[i] = acc_ref[i] * factor + dot(v, p.astype(BF), 0, 0)

    each_earlier(c, counts, visit, None, start)
    if last:
        row = lax.broadcasted_iota(jnp.int32, acc_ref.shape[1:], 0)
        stats = stats_ref[...]
        out = jnp.where(row < HD, acc_ref[0] / stats[2:3], acc_ref[1] / stats[3:4]).T
        o_ref[0, :, :128] = out[:length].astype(BF)
        o_ref[0, :, 128:] = out[length:].astype(BF)
        lse_ref[0, 0] = stats[:2] + jnp.log(stats[2:])


def kv_specs(pieces, length, lanes, at=0):
    kb = lanes // 256
    keys = [
        pl.BlockSpec((a.shape[0], 1, length, 128), lambda s, p: (0, s + at, 0, p)) for a in pieces
    ]
    vals = [
        pl.BlockSpec((a.shape[0], 1, length, 128), lambda s, p: (0, s + at, 0, kb + p))
        for a in pieces
    ]
    return keys + vals


def attn_part(ctx, q, own, prev, start, carry, last):
    seqs, length, qw = q.shape
    pairs = qw // 256
    cols = 2 * length
    first = own is not None
    pieces = ([own] if first else []) + prev
    counts = tuple(a.shape[0] for a in prev)
    spans = first + sum(counts)
    state = [
        pl.BlockSpec((1, 1, 4, cols), lambda s, p: (s, p, 0, 0)),
        pl.BlockSpec((1, 1, 2, 128, cols), lambda s, p: (s, p, 0, 0, 0)),
    ]
    if last:
        out_specs = [
            pl.BlockSpec((1, length, 256), lambda s, p: (s, 0, p)),
            pl.BlockSpec((1, 1, 2, cols), lambda s, p: (s, p, 0, 0)),
        ]
        out_shape = [
            jax.ShapeDtypeStruct((seqs, length, qw), BF),
            jax.ShapeDtypeStruct((seqs, pairs, 2, cols), F32),
        ]
        scratch = [pltpu.VMEM((4, cols), F32), pltpu.VMEM((2, 128, cols), F32)]
    else:
        out_specs = state
        out_shape = [
            jax.ShapeDtypeStruct((seqs, pairs, 4, cols), F32),
            jax.ShapeDtypeStruct((seqs, pairs, 2, 128, cols), F32),
        ]
        scratch = []
    return pl.pallas_call(
        functools.partial(attn_part_kernel, counts, start, first, last),
        grid=(seqs, pairs),
        in_specs=[
            pl.BlockSpec(memory_space=pltpu.SMEM),
            pl.BlockSpec((1, length, 256), lambda s, p: (s, 0, p)),
        ]
        + kv_specs(pieces, length, pieces[0].shape[3])
        + ([] if first else state),
        out_specs=out_specs,
        out_shape=out_shape,
        scratch_shapes=scratch,
        compiler_params=params("arbitrary", "arbitrary"),
        cost_estimate=pl.CostEstimate(
            flops=16 * seqs * length * length * spans * qw,
            bytes_accessed=4 * seqs * length * spans * qw,
            transcendentals=seqs * length * length * spans * qw // 64,
        ),
        name="attn_fwd",
    )(ctx, q, *pieces, *pieces, *(carry or []))


def attn_bwd_kernel(counts, ctx_ref, q_ref, do_ref, o_ref, lse_ref, cos_ref, sin_ref, *refs):
    pieces = len(counts)
    keys = refs[: pieces + 1]
    vals = refs[pieces + 1 : 2 * pieces + 2]
    dq_ref = refs[2 * pieces + 2]
    outs = refs[2 * pieces + 3 : 3 * pieces + 4]
    acc_ref = refs[3 * pieces + 4]
    length = q_ref.shape[1]
    lanes = outs[0].shape[3]
    pair = pl.program_id(1)
    both = (stacked(q_ref).astype(F32) * HD**-0.5).astype(BF)
    dboth = stacked(do_ref)
    prod = dboth.astype(F32) * stacked(o_ref).astype(F32)
    pick_row = lax.broadcasted_iota(jnp.int32, (8, 128), 0)
    pick_lane = lax.broadcasted_iota(jnp.int32, (8, 128), 1) // HD
    picks = (pick_row == pick_lane).astype(F32)
    delta = dot(picks, prod, 1, 1, lax.Precision.HIGHEST)
    c = ctx_ref[0]
    k_at = pl.ds(pl.multiple_of(pair * 128, 128), 128)
    v_at = pl.ds(pl.multiple_of(lanes // 2 + pair * 128, 128), 128)

    def block(piece, entry, diagonal):
        k = keys[piece][entry, 0]
        v = vals[piece][entry, 0]
        parts = []
        dq = None
        for i in range(2):
            ki = half_mask(k, i)
            s = dot(ki, both, 1, 1)
            p = jnp.exp(s - lse_ref[0, 0, i : i + 1, :])
            if diagonal:
                p = jnp.where(causal(s.shape, length), p, 0.0)
            dp = dot(half_mask(v, i), dboth, 1, 1)
            ds = (p * (dp - delta[i : i + 1, :])).astype(BF)
            parts.append((dot(ds, both, 1, 0), dot(p.astype(BF), dboth, 1, 0)))
            part = dot(ki, ds, 0, 0)
            dq = part if dq is None else dq + part
        low = lax.broadcasted_iota(jnp.int32, (length, 128), 1) < HD
        outs[piece][entry, 0, :, k_at] = jnp.where(low, parts[0][0], parts[1][0]).astype(BF)
        outs[piece][entry, 0, :, v_at] = jnp.where(low, parts[0][1], parts[1][1]).astype(BF)
        return dq

    acc_ref[...] = block(0, 0, True)

    def visit(piece, entry):
        acc_ref[...] += block(piece + 1, entry, False)

    def clear(piece, entry):
        outs[piece + 1][entry, 0, :, k_at] = jnp.zeros((length, 128), BF)
        outs[piece + 1][entry, 0, :, v_at] = jnp.zeros((length, 128), BF)

    each_earlier(c, counts, visit, clear)
    out = acc_ref[...].T * HD**-0.5
    cosine = cos_ref[...]
    sine = -sin_ref[...]
    dq_ref[0, :, :128] = turn(out[:length], cosine, sine).astype(BF)
    dq_ref[0, :, 128:] = turn(out[length:], cosine, sine).astype(BF)


def attn_bwd(ctx, q, do, o, lse, cosine, sine, own, prev, at):
    seqs, length, qw = do.shape
    pairs = qw // 256
    pieces = [own] + prev
    counts = tuple(a.shape[0] for a in prev)
    spans = 1 + sum(counts)
    blk = pl.BlockSpec((1, length, 256), lambda s, p: (s, 0, p))
    blk_at = pl.BlockSpec((1, length, 256), lambda s, p: (s + at, 0, p))
    tab = pl.BlockSpec((length, 128), lambda s, p: (0, 0))
    return pl.pallas_call(
        functools.partial(attn_bwd_kernel, counts),
        grid=(seqs, pairs),
        in_specs=[
            pl.BlockSpec(memory_space=pltpu.SMEM),
            blk_at,
            blk,
            blk_at,
            pl.BlockSpec((1, 1, 2, 2 * length), lambda s, p: (s + at, p, 0, 0)),
            tab,
            tab,
        ]
        + kv_specs(pieces, length, own.shape[3], at),
        out_specs=[blk]
        + [
            pl.BlockSpec((a.shape[0], 1) + a.shape[2:], lambda s, p: (0, s, 0, 0)) for a in pieces
        ],
        out_shape=[jax.ShapeDtypeStruct((seqs, length, qw), BF)]
        + [jax.ShapeDtypeStruct((a.shape[0], seqs) + a.shape[2:], BF) for a in pieces],
        scratch_shapes=[pltpu.VMEM((128, 2 * length), F32)],
        compiler_params=params("arbitrary", "arbitrary"),
        cost_estimate=pl.CostEstimate(
            flops=40 * seqs * length * length * spans * qw,
            bytes_accessed=8 * seqs * length * spans * qw,
            transcendentals=seqs * length * length * spans * qw // 64,
        ),
        name="attn_bwd",
    )(ctx, q, do, o, lse, cosine, sine, *pieces, *pieces)


def masked_softmax(logits, named):
    peak = jnp.max(jnp.where(named, logits, NEG), axis=1, keepdims=True)
    grown = jnp.where(named, jnp.exp(jnp.where(named, logits - peak, 0.0)), 0.0)
    return grown / jnp.sum(grown, axis=1, keepdims=True)


def experts_kernel(steps, first, count, micro, more, added, joined, place_ref, router_ref, *refs):
    refs = list(refs)
    n = 1 if joined else refs[-7].shape[1]
    xs = [refs.pop(0) for _ in range(2 * steps)]
    dys = [refs.pop(0) for _ in range(2 * steps)]
    ws = [refs.pop(0) for _ in range(n)]
    before = [refs.pop(0) for _ in range(4)] if more else None
    dws_before = [refs.pop(0) for _ in range(n)] if added else []
    outs = [refs.pop(0) for _ in range(4)]
    dws = [refs.pop(0) for _ in range(n)]
    acc_ref, w_ref, xbuf, dybuf, dwbuf, sems, wsems, dwsems = refs
    step = pl.program_id(0)
    base = place_ref[0]
    c = place_ref[1]
    rows, width = xbuf.shape[1:]
    units = w_ref.shape[-1] // (3 * count)
    both = 2 * count * units
    half = rows // 2

    def copies(t, slot):
        return [
            pltpu.make_async_copy(
                src[2 * t + part].at[micro] if which else src[2 * t + part],
                buf.at[slot, pl.ds(part * half, half)],
                sems.at[slot, 2 * which + part],
            )
            for which, (src, buf) in enumerate(((xs, xbuf), (dys, dybuf)))
            for part in range(2)
        ]

    def fetch(at, slot):
        for t in range(steps):

            @pl.when(at == t)
            def _():
                for copy in copies(t, slot):
                    copy.start()

    def weight_copy(d):
        to = w_ref if joined else w_ref.at[:, c ^ d]
        return pltpu.make_async_copy(ws[d], to, wsems.at[d])

    def added_copy(d):
        return pltpu.make_async_copy(dws_before[d], dwbuf.at[d], dwsems.at[d])

    slot = step % 2

    @pl.when(step == 0)
    def _():
        fetch(step, slot)
        for d in range(n):
            weight_copy(d).start()
        acc_ref[...] = jnp.zeros_like(acc_ref)
    @pl.when(step + 1 < steps)
    def _():
        fetch(step + 1, 1 - slot)

    for copy in copies(0, slot):
        copy.wait()

    x = xbuf[slot]
    dy = dybuf[slot, :, :width]
    lane = lax.broadcasted_iota(jnp.int32, (rows, 128), 1)
    named = dybuf[slot, :, width:].astype(F32) > 0.5
    gates = masked_softmax(dot(x, router_ref[...], 1, 0), named)
    gates = pltpu.roll(gates, 128 - base, 1)

    @pl.when(step == 0)
    def _():
        for d in range(n):
            weight_copy(d).wait()
        if added:
            for d in range(n):
                added_copy(d).start()

    w_in = w_ref[..., :both].reshape(width, both)
    w_back = w_ref[..., both:].reshape(width, both // 2)
    gu = dot(x, w_in, 1, 0)
    g = gu[:, : both // 2]
    u = gu[:, both // 2 :]
    z = dot(dy, w_back, 1, 0)
    gate = jnp.concatenate(
        [
            jnp.broadcast_to(gates[:, first + e : first + e + 1], (rows, units))
            for e in range(count)
        ],
        axis=1,
    )
    sig = 1.0 / (1.0 + jnp.exp(-g))
    silu = g * sig
    act = silu * u
    product = act.astype(BF).astype(F32) * z
    dgates = jnp.zeros((rows, 128), F32)
    for e in range(count):
        total = jnp.sum(product[:, e * units : (e + 1) * units], axis=1, keepdims=True)
        dgates = jnp.where(lane == base + first + e, total, dgates)
    gact = (gate * act).astype(BF)
    da = gate * z
    dgu = jnp.concatenate(
        [
            (da * u * (sig * (1.0 + g * (1.0 - sig)))).astype(BF),
            (da * silu).astype(BF),
        ],
        axis=1,
    )
    out = dot(gact, w_back, 1, 1)
    dx = dot(dgu, w_in, 1, 1)
    for part in range(2):
        at = slice(part * half, (part + 1) * half)
        o, d, t = out[at], dx[at], dgates[at]
        if more:
            o = o + before[part][0].astype(F32)
            d = d + before[2 + part][0, :, :width].astype(F32)
            t = t + before[2 + part][0, :, width:].astype(F32)
        outs[part][0] = o.astype(BF)
        outs[2 + part][0, :, :width] = d.astype(BF)
        outs[2 + part][0, :, width:] = t.astype(BF)

    acc_ref[:, :both] += dot(x.T, dgu, 1, 0)
    acc_ref[:, both:] += dot(dy.T, gact, 1, 0)

    @pl.when(step == pl.num_programs(0) - 1)
    def _():
        for d in range(n):
            if added:
                added_copy(d).wait()
            if joined:
                total = acc_ref[...]
                dws[0][...] = (total + dwbuf[0].astype(F32) if added else total).astype(BF)
                continue
            planes, _, shard, _ = w_ref.shape
            for plane in range(planes):
                row = pl.multiple_of((plane * n + (c ^ d)) * shard, shard)
                total = acc_ref[pl.ds(row, shard)]
                if added:
                    total = total + dwbuf[d, plane].astype(F32)
                dws[d][plane] = total.astype(BF)


def experts_call(
    xs, dys, micro, place, router, weights, first, count, before, dws_before
):
    steps = len(xs) // 2
    half, width = xs[0].shape
    tile = 2 * half
    n = len(weights)
    joined = n == 1
    block = weights[0].shape
    whole_shape = block if joined else block[:1] + (n,) + block[1:]
    lanes = block[-1]
    out_block = pl.BlockSpec((1, half, width), lambda i: (i, 0, 0))
    dx_block = pl.BlockSpec((1, half, width + 128), lambda i: (i, 0, 0))
    whole = pl.BlockSpec(memory_space=pltpu.VMEM)
    anywhere = pl.BlockSpec(memory_space=pl.ANY)
    blocks = [out_block, out_block, dx_block, dx_block]
    rows = steps * tile
    return pl.pallas_call(
        functools.partial(
            experts_kernel, steps, first, count, micro, bool(before), bool(dws_before), joined
        ),
        grid=(steps,),
        in_specs=[
            pl.BlockSpec(memory_space=pltpu.SMEM),
            pl.BlockSpec((width, 128), lambda i: (0, 0)),
        ]
        + [anywhere] * (4 * steps + n)
        + (blocks if before else [])
        + [anywhere] * len(dws_before),
        out_specs=blocks + [whole] * n,
        out_shape=[jax.ShapeDtypeStruct((steps, half, width), BF)] * 2
        + [jax.ShapeDtypeStruct((steps, half, width + 128), BF)] * 2
        + [jax.ShapeDtypeStruct(block, BF)] * n,
        scratch_shapes=[
            pltpu.VMEM((width, lanes), F32),
            pltpu.VMEM(whole_shape, BF),
            pltpu.VMEM((2, tile, width), BF),
            pltpu.VMEM((2, tile, width + 128), BF),
            pltpu.VMEM(((n if dws_before else 1),) + (block if dws_before else (16, 128)), BF),
            pltpu.SemaphoreType.DMA((2, 4)),
            pltpu.SemaphoreType.DMA((n,)),
            pltpu.SemaphoreType.DMA((n,)),
        ],
        compiler_params=params("arbitrary"),
        cost_estimate=pl.CostEstimate(
            flops=6 * rows * width * lanes,
            bytes_accessed=8 * rows * width + 4 * width * lanes,
            transcendentals=rows * lanes // 3,
        ),
        name="experts",
    )(place, router, *xs, *dys, *weights, *(before or []), *dws_before)


def back_kernel(dq_ref, x_ref, cos_ref, sin_ref, wq_ref, wkv_ref, *refs):
    *terms, dkv_ref, part_ref, gain_ref = refs
    total = functools.reduce(jnp.add, [t[...].astype(F32) for t in terms])
    kw = total.shape[1] // 2
    dk = turn(total[:, :kw], cos_ref[...], -sin_ref[...]).astype(BF)
    dkv = jnp.concatenate([dk, total[:, kw:].astype(BF)], axis=1)
    dkv_ref[...] = dkv
    part = dot(dq_ref[...], wq_ref[...], 1, 1) + dot(dkv, wkv_ref[...], 1, 1)
    part_ref[...] = part.astype(BF)
    x = x_ref[...].astype(F32)
    unit = x * lax.rsqrt(jnp.mean(x * x, axis=1, keepdims=True) + EPS)
    sums = jnp.broadcast_to(jnp.sum(part * unit, axis=0, keepdims=True), gain_ref.shape)

    @pl.when(pl.program_id(0) == 0)
    def _():
        gain_ref[...] = sums

    @pl.when(pl.program_id(0) > 0)
    def _():
        gain_ref[...] += sums


def back_call(dq, terms, x, micro, cosine, sine, w_qo, w_kv):
    rows, qw = dq.shape
    lanes = terms[0].shape[1]
    d = w_qo.shape[0]
    tile = min(256, cosine.shape[0])
    per = cosine.shape[0] // tile
    row = lambda width: pl.BlockSpec((tile, width), lambda i: (i, 0))
    table = pl.BlockSpec((tile, 128), lambda i: (i % per, 0))
    return pl.pallas_call(
        back_kernel,
        grid=(rows // tile,),
        in_specs=[
            row(qw),
            pl.BlockSpec((tile, d), lambda i: (i + micro * (rows // tile), 0)),
            table,
            table,
            pl.BlockSpec((d, qw), lambda i: (0, 0)),
            pl.BlockSpec((d, lanes), lambda i: (0, 0)),
        ]
        + [row(lanes)] * len(terms),
        out_specs=[row(lanes), row(d), pl.BlockSpec((8, d), lambda i: (0, 0))],
        out_shape=[
            jax.ShapeDtypeStruct((rows, lanes), BF),
            jax.ShapeDtypeStruct((rows, d), BF),
            jax.ShapeDtypeStruct((8, d), F32),
        ],
        compiler_params=params("arbitrary"),
        cost_estimate=pl.CostEstimate(
            flops=2 * rows * d * (qw + lanes), bytes_accessed=8 * rows * d, transcendentals=0
        ),
        name="back",
    )(dq, x, cosine, sine, w_qo, w_kv, *terms)


def grads_kernel(pairs, starts, extra, place_ref, *refs):
    refs = list(refs)
    sides = [[(refs.pop(0), refs.pop(0)) for _ in range(count)] for count in pairs]
    more = refs.pop(0) if extra else None
    count = len(refs)
    block = refs[0].shape[0]
    for s in range(count):
        at = pl.ds(pl.multiple_of((place_ref[0] ^ s) * block, block), block)
        column = 0
        for side, firsts in zip(sides, starts):
            total = functools.reduce(
                jnp.add,
                [
                    dot(left[first : first + right.shape[0], at], right[...], 0, 0)
                    for (left, right), first in zip(side, firsts)
                ],
            )
            refs[s][:, column : column + total.shape[1]] = total.astype(BF)
            column += total.shape[1]
        if extra:
            refs[s][:, column:] = more[at, :]


def grads_call(me, sides, extra, count):
    d = sides[0][0][0].shape[1]
    lanes = sum(side[0][1].shape[1] for side in sides) + (0 if extra is None else extra.shape[1])
    whole = pl.BlockSpec(memory_space=pltpu.VMEM)
    operands = [a for side in sides for term in side for a in term[:2]]
    starts = [[term[2] for term in side] for side in sides]
    operands += [] if extra is None else [extra]
    return pl.pallas_call(
        functools.partial(grads_kernel, [len(side) for side in sides], starts, extra is not None),
        in_specs=[pl.BlockSpec(memory_space=pltpu.SMEM)] + [whole] * len(operands),
        out_specs=[whole] * count,
        out_shape=[jax.ShapeDtypeStruct((d // count, lanes), BF)] * count,
        compiler_params=pltpu.CompilerParams(vmem_limit_bytes=VMEM_LIMIT),
        cost_estimate=pl.CostEstimate(
            flops=2 * d * lanes * 1024, bytes_accessed=4 * d * lanes, transcendentals=0
        ),
        name="grads",
    )(me, *operands)


def line_kernel(count, place_ref, *refs):
    terms, outs, scratch = refs[:-count - 1], refs[-count - 1 : -1], refs[-1]
    scratch[...] = functools.reduce(jnp.add, [t[...].astype(F32) for t in terms])
    shard = outs[0].shape[0]
    for s in range(count):
        row = pl.multiple_of((place_ref[0] ^ s) * shard, shard)
        outs[s][...] = scratch[pl.ds(row, shard)].astype(BF)


def line_call(me, terms, count):
    rows, lanes = terms[0].shape
    whole = pl.BlockSpec(memory_space=pltpu.VMEM)
    return pl.pallas_call(
        functools.partial(line_kernel, count),
        in_specs=[pl.BlockSpec(memory_space=pltpu.SMEM)] + [whole] * len(terms),
        out_specs=[whole] * count,
        out_shape=[jax.ShapeDtypeStruct((rows // count, lanes), BF)] * count,
        scratch_shapes=[pltpu.VMEM((rows, lanes), F32)],
        compiler_params=pltpu.CompilerParams(vmem_limit_bytes=VMEM_LIMIT),
        name="line",
    )(me, *terms)


def reorder_heads(values):
    parts = []
    for at in range(0, values.shape[1], 256):
        a = values[:, at : at + 128]
        b = values[:, at + 128 : at + 256]
        low = lax.broadcasted_iota(jnp.int32, a.shape, 1) < HD
        parts += [
            jnp.where(low, a, pltpu.roll(b, HD, 1)),
            jnp.where(low, pltpu.roll(a, HD, 1), b),
        ]
    return jnp.concatenate(parts, axis=1)


def finish_kernel(count, *refs):
    early = functools.reduce(jnp.add, [r[...].astype(F32) for r in refs[:count]])
    late = functools.reduce(jnp.add, [r[...].astype(F32) for r in refs[count : 2 * count]])
    q_ref, k_ref, v_ref, o_ref, small_ref = refs[2 * count :]
    qw = q_ref.shape[1]
    kw = k_ref.shape[1]
    q_ref[...] = reorder_heads(early[:, :qw])
    o_ref[...] = reorder_heads(early[:, qw:])
    k_ref[...] = late[:, :kw]
    v_ref[...] = late[:, kw : 2 * kw]
    small_ref[...] = late[:, 2 * kw :]


def finish_call(early, late, qw, kw):
    shard = early[0].shape[0]
    whole = pl.BlockSpec(memory_space=pltpu.VMEM)
    return pl.pallas_call(
        functools.partial(finish_kernel, len(early)),
        in_specs=[whole] * (2 * len(early)),
        out_specs=[whole] * 5,
        out_shape=[
            jax.ShapeDtypeStruct((shard, w), F32) for w in (qw, kw, kw, qw, 128)
        ],
        name="finish",
    )(*early, *late)


def expert_rows_kernel(count, place_ref, *refs):
    pieces, outs = refs[:-3], refs[-3:]
    groups = 2
    units = outs[0].shape[2]
    group = outs[0].shape[0] // (count * groups)
    for g in range(groups):
        for s in range(count):
            piece = pieces[g * count + s]
            at = ((place_ref[0] ^ s) * groups + g) * group
            for i in range(3):
                for e in range(group):
                    lanes = (i * group + e) * units
                    outs[i][at + e] = piece[:, lanes : lanes + units].astype(F32)


def expert_rows_call(me, pieces, experts, units):
    shard = pieces[0].shape[0]
    whole = pl.BlockSpec(memory_space=pltpu.VMEM)
    return pl.pallas_call(
        functools.partial(expert_rows_kernel, len(pieces) // 2),
        in_specs=[pl.BlockSpec(memory_space=pltpu.SMEM)] + [whole] * len(pieces),
        out_specs=[whole] * 3,
        out_shape=[jax.ShapeDtypeStruct((experts, shard, units), F32)] * 3,
        compiler_params=pltpu.CompilerParams(vmem_limit_bytes=VMEM_LIMIT),
        name="expert_rows",
    )(me, *pieces)


def apart(count, step):
    return [(i, i ^ step) for i in range(count)]


def swap(value):
    return lax.ppermute(value, "mp", [(0, 1), (1, 0)])


def up_hop(value, n, s):
    return lax.ppermute(value, "ctx", [(c, c + 1) for c in range(s, n - 1)])


def add(*terms):
    return functools.reduce(jnp.add, [t.astype(F32) for t in terms]).astype(BF)


def by_xor(parts, me):
    bit = 1
    while bit < len(parts):
        flip = (me & bit) != 0
        parts = [jnp.where(flip, parts[i ^ bit], parts[i]) for i in range(len(parts))]
        bit *= 2
    return parts


def exchange(parts, axis):
    count = len(parts)
    return [parts[0]] + [
        lax.ppermute(parts[s], axis, apart(count, s)) for s in range(1, count)
    ]


def from_last(values, start, count):
    values = values[::-1]
    return lax.dynamic_slice_in_dim(jnp.concatenate([values, values]), start, count, 0)


def head_order(weight):
    rows, width = weight.shape
    return (
        weight.reshape(rows, width // (4 * HD), 2, 2, HD).swapaxes(2, 3).reshape(rows, width)
    )


def per_device(
    tokens,
    cotangent,
    routes,
    norm_gain,
    w_query,
    w_key,
    w_value,
    w_output,
    ffn_gain,
    w_router,
    w_gate,
    w_up,
    w_down,
):
    micro, seq_count, local, width = tokens.shape
    top = routes.shape[3]
    experts, shard, units = w_gate.shape
    dp = lax.axis_size("dp")
    n = lax.axis_size("ctx")
    hops = n == 4
    me_dp = lax.axis_index("dp")
    me_ctx = lax.axis_index("ctx")
    me_mp = lax.axis_index("mp")
    mine_count = experts // dp
    group = mine_count // 2
    micros = range(micro)
    per = seq_count * local
    half = per // 2
    rows = micro * per
    qw = w_query.shape[1]
    kw = w_key.shape[1]
    ctx_now = me_ctx.astype(jnp.int32).reshape(1)
    dp_now = me_dp.astype(jnp.int32).reshape(1)
    place = jnp.stack([me_dp * mine_count, me_ctx]).astype(jnp.int32)

    def in_order(mine, other):
        first = me_mp == 0
        return jnp.concatenate([jnp.where(first, mine, other), jnp.where(first, other, mine)])

    def halves(full):
        cut = full.reshape(2, half, full.shape[1])
        mine = lax.dynamic_index_in_dim(cut, me_mp, 0, keepdims=False)
        return mine, lax.dynamic_index_in_dim(cut, 1 - me_mp, 0, keepdims=False)

    def far_pieces(mine, steps=range(1, dp)):
        return [lax.ppermute(mine, "dp", apart(dp, s)) for s in steps]

    def paired(mine, far, other, near):
        return [piece for pair in zip([mine] + far, [other] + near) for piece in pair]

    def gather_line(value):
        return jnp.stack(
            [value] + [lax.ppermute(value, "ctx", apart(n, s)) for s in range(1, n)]
        )

    def gather_plane(value):
        return [value] + [lax.ppermute(value, "dp", apart(dp, s)) for s in range(1, dp)]

    def whole_rows(pieces):
        lines = by_xor(pieces, me_dp)
        full = jnp.stack(lines)
        cols = by_xor([full[:, i] for i in range(n)], me_ctx)
        return jnp.stack(cols, axis=1).reshape(dp * n * shard, full.shape[3])

    live = {}

    def seal(**values):
        live.update(values)
        live.update(lax.optimization_barrier(live))

    small = jnp.concatenate([w_router, norm_gain[:, None], ffn_gain[:, None]], axis=1)
    small = jnp.pad(small, ((0, 0), (0, 128 - small.shape[1])))
    kv_shard = jnp.concatenate([w_key, w_value, small], axis=1)
    qo_shard = jnp.concatenate([head_order(w_query), head_order(w_output)], axis=1)
    if hops:
        kv_line = gather_line(kv_shard)
        qo_line = gather_line(qo_shard)

    def own_experts(gate_up_down):
        cut = [w.reshape(dp, 2, group, shard, units) for w in gate_up_down]
        side = jnp.concatenate([w[:, :, e] for w in cut for e in range(group)], axis=3)
        parts = exchange(by_xor([side[i] for i in range(dp)], me_dp), "dp")
        parts = by_xor(parts, me_dp)
        return [jnp.stack([p[g] for p in parts]) for g in range(2)]

    def weight_send(g, *steps):
        if hops:
            for s in steps:
                at, hop = (2, 1) if s == 3 else (0, s)
                live["weights"][g][s] = lax.ppermute(live["weights"][g][at], "ctx", apart(n, hop))

    def seal_but(under_way, **values):
        kept = [(d, {k: d.pop(k) for k in keys if k in d}) for d, keys in under_way()]
        seal(**values)
        for (d, keys), (_, taken) in zip(under_way(), kept):
            d.update(taken)

    if hops:
        seal_but(
            lambda: [(live, ["qo_line"])],
            kv_line=kv_line,
            qo_line=qo_line,
            raw=[w_gate, w_up, w_down],
            x=tokens,
            dy=cotangent,
            routes=routes,
        )
        kv_pieces = gather_plane(live.pop("kv_line"))
        seal(kv_pieces=kv_pieces)
        kv_full = whole_rows(live.pop("kv_pieces"))
        qo_pieces = gather_plane(live.pop("qo_line"))
    else:
        kv_full = lax.all_gather(kv_shard, ("dp", "ctx"), axis=0, tiled=True)
        qo_full = lax.all_gather(qo_shard, ("dp", "ctx"), axis=0, tiled=True)
        own3 = own_experts([w_gate, w_up, w_down])
        own3 = [lax.all_gather(o, "ctx", axis=1, tiled=False) for o in own3]
        own3 = [{0: o.reshape(width, o.shape[-1])} for o in own3]
        seal(weights=own3, x=tokens, dy=cotangent, routes=routes)
    small = kv_full[:, 2 * kw :]
    router = small[:, :experts]
    router_wide = jnp.pad(router, ((0, 0), (0, 128 - experts)))
    gain_one = small[:, experts].astype(F32)[None, :]
    gain_two = small[:, experts + 1].astype(F32)[None, :]

    position = me_ctx * local + jnp.arange(local, dtype=jnp.int32)
    freqs = THETA ** (-(jnp.arange(HD // 2, dtype=F32) * 2.0) / HD)
    angles = position.astype(F32)[:, None] * freqs[None, :]
    cosine = jnp.tile(jnp.cos(angles), (1, 4))
    sine = jnp.sin(angles)
    sine = jnp.concatenate([-sine, sine, -sine, sine], axis=1)
    live["x"] = live["x"].reshape(rows, width)
    live["dy"] = live["dy"].reshape(rows, width)
    normed, kv = kv_call(live["x"], gain_one, kv_full, 2 * kw, cosine, sine)
    kv = kv.reshape(1, micro * seq_count, local, 2 * kw)

    ids = live.pop("routes").reshape(rows, top)
    marks = jnp.sum(
        (ids[:, :, None] == jnp.arange(128, dtype=jnp.int32)[None, None, :]).astype(F32), axis=1
    ).astype(BF)
    dyx = jnp.concatenate([live["dy"], marks], axis=1)
    dyx = dyx.reshape(micro, 2, half, width + 128)
    dy_cut = [
        lax.dynamic_index_in_dim(dyx, at, 1, keepdims=False) for at in (me_mp, 1 - me_mp)
    ]

    if hops:
        kv_got = up_hop(kv, n, 0)
        seal(
            kv=kv,
            kv_prev=[kv_got],
            qo_pieces=qo_pieces,
            normed=normed,
            dy_cut=dy_cut,
            marks=marks[:, :experts],
            kv_full=kv_full,
            cosine=cosine,
            sine=sine,
            router=router,
            router_wide=router_wide,
            gain_one=gain_one,
            gain_two=gain_two,
        )
        qo_full = whole_rows(live.pop("qo_pieces"))
    else:
        every = lax.all_gather(kv[0], "ctx", axis=0, tiled=False)
        seal(
            kv=kv,
            kv_prev=[from_last(every, n - me_ctx, n - 1)],
            normed=normed,
            dy_cut=dy_cut,
            marks=marks[:, :experts],
            kv_full=kv_full,
            cosine=cosine,
            sine=sine,
            router=router,
            router_wide=router_wide,
            gain_one=gain_one,
            gain_two=gain_two,
        )
    live.update(qo_full=qo_full, dy_far={}, dy_near={})
    q = q_call(live["normed"], qo_full, qw, live["cosine"], live["sine"])
    live["q"] = q.reshape(micro * seq_count, local, qw)

    def dy_send(steps):
        for s in steps:
            live["dy_far"][s] = lax.ppermute(live["dy_cut"][0], "dp", apart(dp, s))

    def attend(first, s, done):
        return attn_part(
            ctx_now,
            live["q"],
            live["kv"] if first else None,
            [live["kv_prev"][s - 1]],
            s,
            None if first else live.pop("carry"),
            done,
        )

    def mix(attn):
        return dot(attn.reshape(rows, qw), live["qo_full"][:, qw:], 1, 1).astype(BF)

    if hops:
        dy_send((1, 2))
        got = up_hop(live["kv_prev"][-1], n, 1)
        carry = attend(True, 1, False)
        live["kv_prev"].append(got)
        seal(carry=carry)
        weights = [{0: own} for own in own_experts(live.pop("raw"))]
        got = up_hop(live["kv_prev"][-1], n, 2)
        carry = attend(False, 2, False)
        live["kv_prev"].append(got)
        seal(carry=carry, weights=weights)
        weight_send(0, 1, 2)
        dy_send((3,))
        attn, lse = attend(False, 3, True)
    else:
        attn, lse = attend(True, 1, True)
        dy_send(range(1, dp))
    live["dy_near"] = {s: swap(live["dy_far"][s]) for s in (1, 2)}
    late = lambda: [(live["weights"][0], [1, 2]), (live["dy_far"], [3])]
    seal_but(late, attn=attn, lse=lse, mixed=mix(attn))

    mixed_got = swap(live["mixed"])
    hidden = live["x"].astype(F32) + (live.pop("mixed").astype(F32) + mixed_got.astype(F32))
    inv_two = lax.rsqrt(jnp.mean(hidden * hidden, axis=1, keepdims=True) + EPS)
    ffn_low = (hidden * inv_two * live["gain_two"]).astype(BF)
    x_cut = [halves(ffn_low[m * per : (m + 1) * per]) for m in micros]

    late = lambda: [(live["weights"][0], [1, 2]), (live["dy_far"], [3])]
    seal_but(late, hidden=hidden, inv_two=inv_two, ffn_low=ffn_low, x_cut=x_cut)
    first = far_pieces(live["x_cut"][0][0], (1, 2))
    live["x_far"] = [first] + [[]] * (micro - 1)
    seal()
    live["x_far"][0] = live["x_far"][0] + far_pieces(live["x_cut"][0][0], (3,))
    weight_send(0, 3)
    live["dy_near"][3] = swap(live["dy_far"][3])
    seal()
    live["x_near"] = [[swap(f) for f in live["x_far"][0]]] + [[]] * (micro - 1)
    seal()
    live.update(sums=[], dws=[[], []], parts=[])

    def run(g, m, before):
        weights = [live["weights"][g][s] for s in sorted(live["weights"][g])]
        x_cut, dy_cut = live["x_cut"][m], live["dy_cut"]
        xs = paired(x_cut[0], live["x_far"][m], x_cut[1], live["x_near"][m])
        dys = paired(
            dy_cut[0],
            [live["dy_far"][s] for s in range(1, dp)],
            dy_cut[1],
            [live["dy_near"][s] for s in range(1, dp)],
        )
        part = experts_call(
            xs,
            dys,
            m,
            place,
            live["router_wide"],
            weights,
            g * group,
            group,
            before,
            live["dws"][g],
        )
        live["dws"][g] = part[4:]
        return list(part[:4])

    live["x_far"][1] = far_pieces(live["x_cut"][1][0])
    weight_send(1, 1, 2)
    live["sums"].append(run(0, 0, None))
    seal()
    live["x_near"][1] = [swap(f) for f in live["x_far"][1]]
    seal()
    weight_send(1, 3)
    live["sums"].append(run(0, 1, None))
    seal()

    live.update(rows=[{}, {}])

    def grad_send(g, *steps):
        if hops:
            for s in steps:
                live["rows"][g][s] = lax.ppermute(live["dws"][g][s], "ctx", apart(n, s))

    def grad_own(g):
        if hops:
            own = add(live["dws"][g][0], *live["rows"][g].values())
        else:
            whole = live["dws"][g][0].reshape(dp, n, shard, -1)
            own = lax.psum_scatter(whole, "ctx", scatter_dimension=1, tiled=False)
        return exchange(by_xor([own[i] for i in range(dp)], me_dp), "dp")

    def terms_of(mine, got):
        return [add(mine[s], got[s]) for s in range(dp)]

    live.update(dx_terms=[None] * micro, dx_back=[None] * micro)
    live.update(out_terms=[None] * micro, out_back={})

    def dx_terms(m):
        part = live["parts"][m]
        live["dx_terms"][m] = terms_of(part[2], swap(part[3]))

    def dx_send(m):
        live["dx_back"][m] = exchange(live["dx_terms"][m], "dp")

    def out_terms(m):
        part = live["parts"][m]
        live["out_terms"][m] = terms_of(part[0], swap(part[1]))

    def out_send(m):
        live["out_back"][m] = exchange(live["out_terms"][m], "dp")

    grad_send(0, 1, 2)
    live["parts"].append(run(1, 0, live["sums"][0]))
    seal()
    dx_terms(0)
    seal()
    dx_send(0)
    grad_send(0, 3)
    live["parts"].append(run(1, 1, live.pop("sums")[1]))
    seal()

    cut = lambda whole, m: whole[m * per : (m + 1) * per]
    live.update({name: [None] * micro for name in ("dh", "dz", "d_attn", "dq", "dkv")})
    live.update(dkv_sum=[{} for _ in micros])
    live.update(router_sums=[None] * micro, gain_sums=[None] * micro)

    def before_attention(m):
        total = add(*live["dx_back"][m])
        moe = in_order(total, swap(total)).astype(F32)
        low = cut(live["ffn_low"], m)
        inv = cut(live["inv_two"], m)
        dgate = moe[:, width : width + experts]
        gate = masked_softmax(
            dot(low, live["router"], 1, 0), cut(live["marks"], m).astype(F32) > 0.5
        )
        dlogit = gate * (dgate - jnp.sum(gate * dgate, axis=1, keepdims=True))
        dlogit = dlogit.astype(BF)
        live["router_sums"][m] = dot(low, dlogit, 0, 0)
        d_ffn = moe[:, :width] + dot(dlogit, live["router"], 1, 1)
        unit = cut(live["hidden"], m) * inv
        live["gain_sums"][m] = jnp.sum(d_ffn * unit, axis=0)
        g_two = d_ffn * live["gain_two"]
        dh = cut(live["dy"], m).astype(F32) + inv * (
            g_two - unit * jnp.mean(g_two * unit, axis=1, keepdims=True)
        )
        dz = dh.astype(BF)
        live["dh"][m] = dh
        live["dz"][m] = dz
        live["d_attn"][m] = dot(dz, live["qo_full"][:, qw:], 1, 0).astype(BF)

    def attention_back(m):
        dq, *dkv = attn_bwd(
            ctx_now,
            live["q"],
            live["d_attn"][m].reshape(seq_count, local, qw),
            live["attn"],
            live["lse"],
            live["cosine"],
            live["sine"],
            live["kv"],
            live["kv_prev"],
            m * seq_count,
        )
        live["dq"][m] = dq.reshape(per, qw)
        live["dkv"][m] = dkv

    def dkv_send(m, *steps):
        if hops:
            for d in steps:
                live["dkv_sum"][m][d] = lax.ppermute(
                    live["dkv"][m][d], "ctx", [(c, c - d) for c in range(d, n)]
                )

    def back(m):
        if hops:
            terms = [live["dkv"][m][0], *live["dkv_sum"][m].values()]
        else:
            every = from_last(jnp.concatenate(live["dkv"][m]), n - 1 - me_ctx, n)
            terms = [lax.psum_scatter(every, "ctx", scatter_dimension=0, tiled=True)]
        terms = [t.reshape(per, 2 * kw) for t in terms]
        return back_call(
            live["dq"][m],
            terms,
            live["x"],
            m,
            live["cosine"],
            live["sine"],
            live["qo_full"],
            live["kv_full"],
        )

    def out_total(m):
        total = add(*live["out_back"][m])
        moe = in_order(total, swap(total)).astype(F32)
        return (cut(live["hidden"], m) + moe).astype(BF)

    def early_send(*steps):
        if hops:
            for s in steps:
                live["early"][s] = lax.ppermute(live["early"][s], "dp", apart(dp, s))

    before_attention(0)
    dx_terms(1)
    grad_send(1, 1, 2)
    out_terms(0)
    seal_but(lambda: [(live["rows"][1], [1, 2])])
    dx_send(1)
    attention_back(0)
    seal()
    dkv_send(0, 1, 3)
    out_send(0)
    before_attention(1)
    out_terms(1)
    seal_but(lambda: [(live["out_back"], [0])])
    dkv_send(0, 2)
    out_send(1)
    attention_back(1)
    seal()
    dkv_send(1, 1, 2, 3)
    pieces_now = dp_now if hops else jnp.zeros((1,), jnp.int32)
    early = grads_call(
        pieces_now,
        [
            [(live["normed"], live["dq"][m], m * per) for m in micros],
            [(jnp.concatenate(live["dz"]), live["attn"].reshape(rows, qw), 0)],
        ],
        None,
        dp,
    )
    owned = [grad_own(0)]
    seal_but(lambda: [(live["dkv_sum"][1], [1, 2, 3])], early=list(early), owned=owned)
    early_send(1, 2, 3)
    dkv_first, part_first, gain_first = back(0)
    got_first = swap(part_first)
    out_first = out_total(0)
    out_last = out_total(1)
    seal(
        got=[got_first],
        output=[out_first, out_last],
        dkv_final=[dkv_first],
        part=[part_first],
        gain_one_sums=[gain_first],
    )
    grad_send(1, 3)
    dkv_last, part_last, gain_last = back(1)
    live["dkv_final"].append(dkv_last)
    live["part"].append(part_last)
    small = jnp.concatenate(
        [
            live["router_sums"][0] + live["router_sums"][1],
            (live["gain_one_sums"][0] + gain_last)[0][:, None],
            (live["gain_sums"][0] + live["gain_sums"][1])[:, None],
        ],
        axis=1,
    )
    small = jnp.pad(small, ((0, 0), (0, 128 - small.shape[1]))).astype(BF)
    late = grads_call(
        pieces_now,
        [[(live["normed"], live["dkv_final"][m], m * per) for m in micros]],
        small,
        dp,
    )
    got_last = swap(part_last)
    seal_but(
        lambda: [(live["rows"][1], [3])], late=late, got=live["got"] + [got_last]
    )
    early, late = live["early"], live["late"]
    if hops:
        late = exchange(late, "dp")
        early = line_call(ctx_now, early, n)
    d_normed = jnp.concatenate(
        [p.astype(F32) + g.astype(F32) for p, g in zip(live["part"], live["got"])]
    )
    x32 = live["x"].astype(F32)
    inv_one = lax.rsqrt(jnp.mean(x32 * x32, axis=1, keepdims=True) + EPS)
    n_one = x32 * inv_one
    g_one = d_normed * live["gain_one"]
    input_grad = (
        jnp.concatenate(live["dh"])
        + inv_one * (g_one - n_one * jnp.mean(g_one * n_one, axis=1, keepdims=True))
    ).astype(BF)
    seal_but(
        lambda: [(live["rows"][1], [3])], late=late, early=early, input_grad=input_grad
    )
    early, late = live["early"], live["late"]
    if hops:
        late = exchange(line_call(ctx_now, late, n), "ctx")
        early = exchange(early, "ctx")
    else:
        early, late = (
            [
                lax.psum_scatter(
                    jnp.concatenate(p), ("dp", "ctx"), scatter_dimension=0, tiled=True
                )
            ]
            for p in (early, late)
        )
    owned = [live["owned"][0], grad_own(1)]
    output = jnp.concatenate(live["output"])
    grad_q, grad_k, grad_v, grad_o, small_grad = finish_call(early, late, qw, kw)
    gain_part = small_grad[:, experts]
    dw_gate, dw_up, dw_down = expert_rows_call(dp_now, owned[0] + owned[1], experts, units)
    shape = tokens.shape
    return (
        output.reshape(shape),
        live["input_grad"].reshape(shape),
        gain_part + swap(gain_part),
        grad_q,
        grad_k,
        grad_v,
        grad_o,
        small_grad[:, experts + 1],
        small_grad[:, :experts],
        dw_gate,
        dw_up,
        dw_down,
    )


def solution(mesh):
    rows = P(None, "dp", "ctx", None)
    vector = P(("dp", "ctx"))
    matrix = P(("dp", "ctx"), "mp")
    router = P(("dp", "ctx"), None)
    expert = P(None, ("dp", "ctx"), "mp")
    return jax.shard_map(
        per_device,
        mesh=mesh,
        in_specs=(
            rows,
            rows,
            rows,
            vector,
            matrix,
            matrix,
            matrix,
            matrix,
            vector,
            router,
            expert,
            expert,
            expert,
        ),
        out_specs=(
            rows,
            rows,
            vector,
            matrix,
            matrix,
            matrix,
            matrix,
            vector,
            router,
            expert,
            expert,
            expert,
        ),
        check_vma=False,
    )
```
